512 devices in a mesh: section: 16 (over z, core), dp: 4 (over x), tp: 8 (over y).
Axes of the slice: x: 4, y: 8, z: 8, core: 2. Of those that a mesh axis runs over, the one named last changes fastest.
Arguments:
- hidden_in: bfloat16 [4, 128, 4096], P(None, 'dp', 'tp'), may hold values from -6 to 6
- rotation: bfloat16 [4096, 4096], P(('section', 'dp'), 'tp'), may hold values from -0.09375 to 0.09375
- proj: bfloat16 [16, 4096, 4096], P('section', None, 'tp'), may hold values from -0.09375 to 0.09375
- norm_gain: float32 [16, 4096], P('section'), may hold values from 0.5 to 8
- quant_exp: int32 [16, 32], P('section', 'tp'), may hold values from 0 to 7
Outputs:
- rotation_grad: float32 [4096, 4096], P(('section', 'dp'), 'tp')
- loss: float32 [], replicated
The draws below stay inside these ranges and needn't reach their ends.
All inputs are finite; a program needn't handle non-finite values.
Results may differ from the reference program's by a relative error of at most 0.04.
Values may be sent and summed in bfloat16 or wider, within the bound.
No kernel may reach another device: no remote copies, remote signals or barrier semaphores. Data moves between devices by JAX's collectives and lax.ppermute only.
A program may use at most 64 MiB of HBM per device.

```python
import math
import jax
import jax.numpy as jnp
from jax import lax

D = 4096
GROUP = 128
MB = 4
SECTIONS = 16
TOKENS = 128


def draw_norm_gain(key, part):
    key = jax.random.fold_in(key, 11)
    section_pos = jnp.arange(SECTIONS, dtype=jnp.float32)[:, None]
    section_ramp = 1.0 + 3.0 * section_pos / max(SECTIONS - 1, 1)
    base_gain = jnp.exp(jax.random.uniform(key, (SECTIONS, D), jnp.float32, math.log(0.5), math.log(2.0)))
    return (base_gain * section_ramp).astype(jnp.float32)


def plant(values, key, low, high):
    extent = values.shape
    spot = [jax.random.randint(jax.random.fold_in(key, axis), (), 0, extent[axis]) for axis in range(len(extent))]
    values = values.at[tuple(spot)].set(low)
    longest = extent.index(max(extent))
    spot[longest] = (spot[longest] + 1) % extent[longest]
    return values.at[tuple(spot)].set(high)


def block_levels(stream_key, shape, split, smallest, high):
    def one(axis_at, shards_of):
        draws = jax.random.uniform(jax.random.fold_in(jax.random.fold_in(stream_key, 6), axis_at), (shards_of,), jnp.float32, smallest / len(split), high / len(split))
        return jnp.repeat(jnp.exp(draws), shape[axis_at] // shards_of).reshape((-1,) + (1,) * (len(shape) - axis_at - 1))

    factor_of = one(*split[0])
    for cut in split[1:]:
        factor_of = factor_of * one(*cut)
    return factor_of


def noise(stream_key, dims, width, most, cuts=(), kind=jnp.bfloat16):
    array = width * jax.random.normal(stream_key, dims, jnp.float32)
    if cuts:
        array = array * block_levels(stream_key, dims, cuts, -0.22, 0.18)
    return jnp.clip(array, -most, most).astype(kind)


def setup_inputs(seed: int = 0) -> dict:
    arg_keys = jax.random.split(jax.random.key(seed), 6)
    return {
        "hidden_in": noise(arg_keys[0], (MB, TOKENS, D), 1.0, 6.0, ((1, 4), (2, 8))),
        "rotation": noise(arg_keys[1], (D, D), D ** -0.5, 0.09375, ((0, 64), (1, 8))),
        "proj": noise(arg_keys[2], (SECTIONS, D, D), D ** -0.5, 0.09375, ((0, 16), (2, 8))),
        "norm_gain": draw_norm_gain(jax.random.fold_in(arg_keys[5], 71), 0),
        "quant_exp": plant(jax.random.randint(arg_keys[4], (SECTIONS, D // GROUP), 0, 8), jax.random.fold_in(arg_keys[4], 1), 0, 7).astype(jnp.int32),
    }


norm_eps = 1e-05
full_turn = 2.0 * math.pi

def quantize(values, scale):
    ratio = values / scale
    stair = ratio - jnp.sin(full_turn * ratio) / full_turn
    return scale * jnp.clip(stair, -8.0, 7.0)

def staircase_slope(values, scale):
    ratio = values / scale
    stair = ratio - jnp.sin(full_turn * ratio) / full_turn
    inside = (stair > -8.0) & (stair < 7.0)
    return jnp.where(inside, 1.0 - jnp.cos(full_turn * ratio), 0.0)

def reference(hidden_in, rotation, proj, norm_gain, quant_exp):
    scales = jnp.exp2(quant_exp.astype(jnp.float32) * 0.25) * 0.125
    col_scales = jnp.repeat(scales, GROUP, axis=1)
    stream = hidden_in.reshape(-1, D)
    grad_sum = jnp.zeros((D, D), jnp.float32)
    loss_sum = jnp.zeros((), jnp.float32)
    for section_num in range(SECTIONS):
        wide_rows = stream.astype(jnp.float32)
        mean_square = lax.optimization_barrier(jnp.mean(wide_rows * wide_rows, axis=-1, keepdims=True))
        normed = (wide_rows * lax.rsqrt(mean_square + norm_eps) * norm_gain[section_num]).astype(jnp.bfloat16)
        rotated = jnp.dot(normed, rotation, preferred_element_type=jnp.float32)
        level = quantize(rotated, col_scales[section_num])
        quantized = level.astype(jnp.bfloat16)
        update = jnp.dot(quantized, proj[section_num], preferred_element_type=jnp.float32)
        stream = (wide_rows + update).astype(jnp.bfloat16)
        error_part = level - rotated
        grad_rot = (error_part * (staircase_slope(rotated, col_scales[section_num]) - 1.0)).astype(jnp.bfloat16)
        grad_sum = grad_sum + jnp.dot(normed.T, grad_rot, preferred_element_type=jnp.float32)
        loss_sum = loss_sum + jnp.sum(error_part * error_part)
    factor = 1.0 / math.sqrt(SECTIONS * MB * TOKENS)
    return (grad_sum * factor, loss_sum / (MB * TOKENS * D))
```

```python
import math

import jax
import jax.numpy as jnp
from jax import lax
from jax.experimental import pallas as pl
from jax.experimental.pallas import tpu as pltpu
from jax.sharding import PartitionSpec as P

D = 4096
GROUP = 128
STAGE = 4

norm_eps = 1e-05
full_turn = 2.0 * math.pi


def quantize(values, scale):
    ratio = values / scale
    stair = ratio - jnp.sin(full_turn * ratio) / full_turn
    return scale * jnp.clip(stair, -8.0, 7.0)


def staircase_slope(values, scale):
    ratio = values / scale
    stair = ratio - jnp.sin(full_turn * ratio) / full_turn
    inside = (stair > -8.0) & (stair < 7.0)
    return jnp.where(inside, 1.0 - jnp.cos(full_turn * ratio), 0.0)


def gather(value, axis):
    copies = jnp.broadcast_to(value[None], (lax.axis_size(axis),) + value.shape)
    return lax.all_to_all(copies, axis, 0, 0, tiled=True)


def total_of(value, axis):
    return jnp.sum(gather(value, axis), axis=0)


def crossed(value, mask):
    return lax.ppermute(value, "section", [(i, i ^ mask) for i in range(lax.axis_size("section"))])


def order_kernel(place_ref, own, by1, by2, by3, out, sems):
    sources = (own, by1, by2, by3)
    place = place_ref[0]
    for layer in range(STAGE):
        for mask in range(STAGE):
            @pl.when((place ^ layer) == mask)
            def _():
                pltpu.make_async_copy(sources[mask], out.at[layer], sems.at[layer]).start()
    for layer in range(STAGE):
        pltpu.make_async_copy(own, out.at[layer], sems.at[layer]).wait()


def in_order(place, own, by1, by2, by3):
    anywhere = pl.BlockSpec(memory_space=pl.ANY)
    return pl.pallas_call(
        order_kernel,
        out_shape=jax.ShapeDtypeStruct((STAGE,) + own.shape, own.dtype),
        in_specs=[pl.BlockSpec(memory_space=pltpu.SMEM)] + [anywhere] * 4,
        out_specs=anywhere,
        scratch_shapes=[pltpu.SemaphoreType.DMA((STAGE,))],
        name="in_order",
    )(place, own, by1, by2, by3)


def local(hidden_in, rotation, proj, norm_gain, quant_exp):
    sections = lax.axis_size("section")
    replicas = lax.axis_size("dp")
    section_pos = lax.axis_index("section")
    micro_count, tok_rows, part_cols = hidden_in.shape
    stages = sections // STAGE
    stage_pos = section_pos // STAGE
    place = section_pos % STAGE

    own = proj[0]
    by1 = crossed(own, 1)
    by2 = crossed(own, 2)
    by3 = crossed(by2, 1)
    rot_cols = lax.all_gather(rotation, ("section", "dp"), axis=0, tiled=True)
    scale_row = jnp.repeat(jnp.exp2(quant_exp.astype(jnp.float32) * 0.25) * 0.125, GROUP, axis=1)
    params = jnp.concatenate([norm_gain, scale_row], axis=1)
    groups = [[STAGE * g + i for i in range(STAGE)] for g in range(stages)]
    params = lax.all_gather(params, "section", axis=0, tiled=True, axis_index_groups=groups)
    gains, scales = params[:, :D], params[:, D:]
    weights = in_order(place[None].astype(jnp.int32), own, by1, by2, by3)

    stream = lax.dynamic_index_in_dim(hidden_in, place, 0, keepdims=False)
    kept_normed = None
    kept_rotated = None
    for stage in range(stages):
        normed_list, rotated_list = [], []
        for layer in range(STAGE):
            rows = gather(stream, "tp").transpose(1, 0, 2).reshape(tok_rows, D).astype(jnp.float32)
            mean_square = jnp.mean(rows * rows, axis=-1, keepdims=True)
            normed = (rows * lax.rsqrt(mean_square + norm_eps) * gains[layer]).astype(jnp.bfloat16)
            rotated = jnp.dot(normed, rot_cols, preferred_element_type=jnp.float32)
            normed_list.append(normed)
            rotated_list.append(rotated)
            if stage == stages - 1 and layer == STAGE - 1:
                break
            quantized = quantize(rotated, scales[layer]).astype(jnp.bfloat16)
            quant_full = gather(quantized, "tp").transpose(1, 0, 2).reshape(tok_rows, D)
            update = jnp.dot(quant_full, weights[layer], preferred_element_type=jnp.float32)
            stream = (stream.astype(jnp.float32) + update).astype(jnp.bfloat16)
        normed_now = jnp.concatenate(normed_list, axis=0)
        rotated_now = jnp.concatenate(rotated_list, axis=0)
        if stage == 0:
            kept_normed, kept_rotated = normed_now, rotated_now
        else:
            valid = stage_pos == stage
            kept_normed = jnp.where(valid, normed_now, kept_normed)
            kept_rotated = jnp.where(valid, rotated_now, kept_rotated)
        if stage < stages - 1:
            stream = lax.ppermute(
                stream, "section", [(i, i + STAGE) for i in range(sections - STAGE)]
            )

    all_rows = STAGE * tok_rows
    row_scales = jnp.repeat(scales, tok_rows, axis=0)
    level = quantize(kept_rotated, row_scales)
    error_part = level - kept_rotated
    grad_rot = (error_part * (staircase_slope(kept_rotated, row_scales) - 1.0)).astype(jnp.bfloat16)
    loss = jnp.full((8, 128), jnp.sum(error_part * error_part), jnp.float32)
    for axis in ("tp", "dp", "section"):
        loss = total_of(loss, axis)

    grad_all = gather(grad_rot, "dp").reshape(replicas * all_rows, part_cols)
    row_block = D // (sections * replicas)
    blocks = kept_normed.reshape(all_rows, sections, replicas, row_block)
    blocks = blocks.transpose(2, 0, 1, 3).reshape(replicas, all_rows, sections * row_block)
    normed_all = lax.all_to_all(blocks, "dp", 0, 0, tiled=True).reshape(replicas * all_rows, sections * row_block)
    terms = lax.dot_general(
        normed_all, grad_all, (((0,), (0,)), ((), ())), preferred_element_type=jnp.float32
    )
    halves = terms.reshape(sections // 2, 2, row_block, part_cols)
    core = section_pos % 2
    mine = lax.dynamic_index_in_dim(halves, core, 1, keepdims=False)
    other = lax.dynamic_index_in_dim(halves, 1 - core, 1, keepdims=False).astype(jnp.bfloat16)
    pair_sum = (mine + crossed(other, 1).astype(jnp.float32)).astype(jnp.bfloat16)
    same_core = [[2 * z + c for z in range(sections // 2)] for c in range(2)]
    parts = lax.all_to_all(pair_sum, "section", 0, 0, axis_index_groups=same_core, tiled=True)
    grad_share = jnp.sum(parts.astype(jnp.float32), axis=0)
    factor = 1.0 / math.sqrt(sections * all_rows * replicas)
    norm_count = all_rows * replicas * D
    return (grad_share * factor, loss[0, 0] / norm_count)


def solution(mesh):
    placed = (
        P(None, "dp", "tp"),
        P(("section", "dp"), "tp"),
        P("section", None, "tp"),
        P("section", None),
        P("section", "tp"),
    )
    return jax.shard_map(
        local,
        mesh=mesh,
        in_specs=placed,
        out_specs=(P(("section", "dp"), "tp"), P()),
        check_vma=False,
    )
```

```python
import math

import jax
import jax.numpy as jnp
from jax import lax
from jax.sharding import PartitionSpec as P

D = 4096
GROUP = 128
STAGE = 4

norm_eps = 1e-05
full_turn = 2.0 * math.pi

SIN_TERMS = (3.141592653536291, -5.167712764624543, 2.5501633189471025,
             -0.5992521978250058, 0.08205040181365181, -0.007028386419353805)
COS_TERMS = (0.9999999997799043, -4.934802137078827, 4.058709159556301,
             -1.3352120030506605, 0.23493731381815505, -0.024396324355626643)


def horner(terms, square):
    total = jnp.full_like(square, terms[-1])
    for term in terms[-2::-1]:
        total = total * square + term
    return total


def half_turn(ratio):
    part = ratio - jnp.round(ratio)
    square = part * part
    return part * horner(SIN_TERMS, square), horner(COS_TERMS, square)


def quantize(values, scale):
    ratio = values / scale
    sine, cosine = half_turn(ratio)
    return scale * jnp.clip(ratio - sine * cosine / math.pi, -8.0, 7.0)


def level_and_slope(values, scale):
    ratio = values / scale
    sine, cosine = half_turn(ratio)
    stair = ratio - sine * cosine / math.pi
    inside = (stair > -8.0) & (stair < 7.0)
    level = scale * jnp.clip(stair, -8.0, 7.0)
    return level, jnp.where(inside, 2.0 * sine * sine, 0.0)


def copies_of(value, count):
    return jnp.broadcast_to(value[None], (count,) + value.shape)


def gather(value, axis):
    return lax.all_to_all(copies_of(value, lax.axis_size(axis)), axis, 0, 0, tiled=True)


def crossed(value, mask):
    return lax.ppermute(value, "section", [(i, i ^ mask) for i in range(lax.axis_size("section"))])


def local(hidden_in, rotation, proj, norm_gain, quant_exp):
    sections = lax.axis_size("section")
    replicas = lax.axis_size("dp")
    section_pos = lax.axis_index("section")
    micro_count, tok_rows, part_cols = hidden_in.shape
    stages = sections // STAGE
    planes = sections // 2
    stage_pos = section_pos // STAGE
    place = section_pos % STAGE
    core = section_pos % 2
    lower = place < 2
    same_core = [[2 * z + c for z in range(planes)] for c in range(2)]
    row_block = rotation.shape[0]

    own = proj[0]
    by1 = crossed(own, 1)
    along_z = lax.all_to_all(
        copies_of(rotation, planes), "section", 0, 0, axis_index_groups=same_core, tiled=True
    )
    along_z, own_later = lax.optimization_barrier((along_z, own))
    by2 = crossed(own_later, 2)
    along_x = gather(along_z, "dp")
    other_rows = crossed(along_x, 1)
    even_rows = jnp.where(core == 0, along_x, other_rows)
    odd_rows = jnp.where(core == 0, other_rows, along_x)
    rot_cols = jnp.stack([even_rows, odd_rows]).transpose(2, 0, 1, 3, 4).reshape(D, part_cols)

    scale_row = jnp.repeat(jnp.exp2(quant_exp.astype(jnp.float32) * 0.25) * 0.125, GROUP, axis=1)
    params = jnp.concatenate([norm_gain, scale_row], axis=1)
    groups = [[STAGE * g + i for i in range(STAGE)] for g in range(stages)]
    params = lax.all_gather(params, "section", axis=0, tiled=True, axis_index_groups=groups)
    gains, scales = params[:, :D], params[:, D:]

    weights = jnp.zeros((STAGE,) + own.shape, own.dtype)
    weights = lax.dynamic_update_index_in_dim(weights, own, place, 0)
    weights = lax.dynamic_update_index_in_dim(weights, by1, place ^ 1, 0)

    def rotate(stream, layer):
        rows = gather(stream, "tp").transpose(1, 0, 2).reshape(stream.shape[0], D).astype(jnp.float32)
        mean_square = jnp.mean(rows * rows, axis=-1, keepdims=True)
        normed = (rows * lax.rsqrt(mean_square + norm_eps) * gains[layer]).astype(jnp.bfloat16)
        return normed, jnp.dot(normed, rot_cols, preferred_element_type=jnp.float32)

    def project(stream, rotated, layer):
        quantized = quantize(rotated, scales[layer]).astype(jnp.bfloat16)
        quant_full = gather(quantized, "tp").transpose(1, 0, 2).reshape(stream.shape[0], D)
        update = jnp.dot(quant_full, weights[layer], preferred_element_type=jnp.float32)
        return (stream.astype(jnp.float32) + update).astype(jnp.bfloat16)

    stream = jnp.concatenate(
        [lax.dynamic_index_in_dim(hidden_in, core + k, 0, keepdims=False) for k in (0, 2)], axis=0
    )
    early = []
    for layer in (0, 1):
        normed, rotated = rotate(stream, layer)
        early.append((normed, rotated))
        stream = project(stream, rotated, layer)
    first, second = stream[:tok_rows], stream[tok_rows:]
    stream = jnp.where(lower, first, crossed(second, 2))
    stream, by2 = lax.optimization_barrier((stream, by2))
    by3 = crossed(by2, 1)
    weights = lax.dynamic_update_index_in_dim(weights, by2, place ^ 2, 0)
    weights = lax.dynamic_update_index_in_dim(weights, by3, place ^ 3, 0)
    early_normed = jnp.concatenate([n for n, _ in early], axis=0).reshape(2, 2, tok_rows, D)
    early_rotated = jnp.concatenate([r for _, r in early], axis=0).reshape(2, 2, tok_rows, part_cols)
    moved_normed = crossed(early_normed[:, 1], 2)
    moved_rotated = crossed(early_rotated[:, 1], 2)
    early_normed = jnp.where(lower, early_normed[:, 0], moved_normed)
    early_rotated = jnp.where(lower, early_rotated[:, 0], moved_rotated)
    kept_normed = kept_rotated = None

    for stage in range(stages):
        normed_list, rotated_list = [], []
        for layer in range(STAGE):
            if stage == 0 and layer < 2:
                normed_list.append(early_normed[layer])
                rotated_list.append(early_rotated[layer])
                continue
            normed, rotated = rotate(stream, layer)
            normed_list.append(normed)
            rotated_list.append(rotated)
            if stage < stages - 1 or layer < STAGE - 1:
                stream = project(stream, rotated, layer)
        normed_now = jnp.concatenate(normed_list, axis=0)
        rotated_now = jnp.concatenate(rotated_list, axis=0)
        if stage == 0:
            kept_normed, kept_rotated = normed_now, rotated_now
        else:
            valid = stage_pos == stage
            kept_normed = jnp.where(valid, normed_now, kept_normed)
            kept_rotated = jnp.where(valid, rotated_now, kept_rotated)
        if stage < stages - 1:
            stream = lax.ppermute(
                stream, "section", [(i, i + STAGE) for i in range(sections - STAGE)]
            )

    all_rows = STAGE * tok_rows
    turned = lax.optimization_barrier(kept_normed.T)
    turned = turned.reshape(sections, replicas, row_block, all_rows).transpose(1, 0, 2, 3)
    turned = lax.all_to_all(turned, "dp", 0, 0, tiled=True)
    turned = turned.transpose(1, 2, 0, 3).reshape(sections * row_block, replicas * all_rows)
    row_scales = jnp.repeat(scales, tok_rows, axis=0)
    level, slope = level_and_slope(kept_rotated, row_scales)
    error_part = level - kept_rotated
    grad_rot = (error_part * (slope - 1.0)).astype(jnp.bfloat16)
    grad_all = gather(grad_rot, "dp").reshape(replicas * all_rows, part_cols)
    terms = jnp.dot(turned, grad_all, preferred_element_type=jnp.float32)

    loss = jnp.full((8, 128), jnp.sum(error_part * error_part), jnp.float32)
    loss = jnp.sum(gather(loss, "tp"), axis=0)
    loss = loss + crossed(loss, 1)
    loss = jnp.sum(gather(loss, "dp"), axis=0)
    high = lax.reduce_precision(loss[0, 0], 8, 7)
    middle = lax.reduce_precision(loss[0, 0] - high, 8, 7)
    low = loss[0, 0] - high - middle
    lane = lax.broadcasted_iota(jnp.int32, (16, part_cols), 1)
    tail_rows = jnp.where(lane == 0, high, jnp.where(lane == 1, middle, jnp.where(lane == 2, low, 0.0)))
    tail_rows = tail_rows.astype(jnp.bfloat16)

    halves = terms.reshape(planes, 2, row_block, part_cols)
    mine = lax.dynamic_index_in_dim(halves, core, 1, keepdims=False)
    other = lax.dynamic_index_in_dim(halves, 1 - core, 1, keepdims=False).astype(jnp.bfloat16)
    pair_sum = (mine + crossed(other, 1).astype(jnp.float32)).astype(jnp.bfloat16)
    sent = jnp.concatenate([pair_sum, copies_of(tail_rows, planes)], axis=1)
    parts = lax.all_to_all(sent, "section", 0, 0, axis_index_groups=same_core, tiled=True)
    sums = jnp.sum(parts.astype(jnp.float32), axis=0)
    factor = 1.0 / math.sqrt(sections * all_rows * replicas)
    norm_count = all_rows * replicas * D
    return (sums[:row_block] * factor, jnp.sum(sums[row_block, :3]) / norm_count)


def solution(mesh):
    placed = (
        P(None, "dp", "tp"),
        P(("section", "dp"), "tp"),
        P("section", None, "tp"),
        P("section", None),
        P("section", "tp"),
    )
    return jax.shard_map(
        local,
        mesh=mesh,
        in_specs=placed,
        out_specs=(P(("section", "dp"), "tp"), P()),
        check_vma=False,
    )
```

```python
import math

import jax
import jax.numpy as jnp
from jax import lax
from jax.experimental import pallas as pl
from jax.experimental.pallas import tpu as pltpu
from jax.sharding import PartitionSpec as P

D = 4096
GROUP = 128
STAGE = 4

norm_eps = 1e-05
full_turn = 2.0 * math.pi

SIN_TERMS = (3.141592653536291, -5.167712764624543, 2.5501633189471025,
             -0.5992521978250058, 0.08205040181365181, -0.007028386419353805)
COS_TERMS = (0.9999999997799043, -4.934802137078827, 4.058709159556301,
             -1.3352120030506605, 0.23493731381815505, -0.024396324355626643)


def horner(terms, square):
    total = jnp.full_like(square, terms[-1])
    for term in terms[-2::-1]:
        total = total * square + term
    return total


def half_turn(ratio):
    part = ratio - jnp.round(ratio)
    square = part * part
    return part * horner(SIN_TERMS, square), horner(COS_TERMS, square)


def quantize(values, scale):
    ratio = values / scale
    sine, cosine = half_turn(ratio)
    return scale * jnp.clip(ratio - sine * cosine / math.pi, -8.0, 7.0)


def level_and_slope(values, scale):
    ratio = values / scale
    sine, cosine = half_turn(ratio)
    stair = ratio - sine * cosine / math.pi
    inside = (stair > -8.0) & (stair < 7.0)
    level = scale * jnp.clip(stair, -8.0, 7.0)
    return level, jnp.where(inside, 2.0 * sine * sine, 0.0)


def copies_of(value, count):
    return jnp.broadcast_to(value[None], (count,) + value.shape)


def exchange(copies, axis):
    return lax.all_to_all(copies, axis, 0, 0, tiled=True)


def gather(value, axis):
    return exchange(copies_of(value, lax.axis_size(axis)), axis)


def crossed(value, mask):
    return lax.ppermute(value, "section", [(i, i ^ mask) for i in range(lax.axis_size("section"))])


VMEM = pl.BlockSpec(memory_space=pltpu.VMEM)
PARAMS = pltpu.CompilerParams(vmem_limit_bytes=8 * 1024 * 1024)


def load_kernel(place_ref, own, by1, by2, by3, *rest):
    outs, sems = rest[:STAGE], rest[STAGE]
    sources = (own, by1, by2, by3)
    place = place_ref[0]
    for layer in range(STAGE):
        for mask in range(STAGE):
            @pl.when((place ^ layer) == mask)
            def _():
                pltpu.make_async_copy(sources[mask], outs[layer], sems.at[layer]).start()
    for layer in range(STAGE):
        pltpu.make_async_copy(own, outs[layer], sems.at[layer]).wait()


def load_weights(place, own, by1, by2, by3):
    far = pl.BlockSpec(memory_space=pl.ANY)
    return pl.pallas_call(
        load_kernel,
        out_shape=[jax.ShapeDtypeStruct(own.shape, own.dtype)] * STAGE,
        in_specs=[pl.BlockSpec(memory_space=pltpu.SMEM)] + [far] * 4,
        out_specs=[VMEM] * STAGE,
        scratch_shapes=[pltpu.SemaphoreType.DMA((STAGE,))],
        compiler_params=PARAMS,
        name="load_weights",
    )(place, own, by1, by2, by3)


def rotate_kernel(rows_ref, gain_ref, rot_ref, scale_ref, normed_ref, rotated_ref, *copies):
    count, _, part = rows_ref.shape
    total = None
    for k in range(count):
        rows = rows_ref[k].astype(jnp.float32)
        square = jnp.sum(rows * rows, axis=-1, keepdims=True)
        total = square if total is None else total + square
    factor = lax.rsqrt(total / (count * part) + norm_eps)
    for k in range(count):
        cols = slice(k * part, (k + 1) * part)
        rows = rows_ref[k].astype(jnp.float32)
        normed_ref[:, cols] = (rows * factor * gain_ref[:, cols]).astype(jnp.bfloat16)
    rotated = jnp.dot(normed_ref[...], rot_ref[...], preferred_element_type=jnp.float32)
    rotated_ref[...] = rotated
    if copies:
        quantized = quantize(rotated, scale_ref[...]).astype(jnp.bfloat16)
        for k in range(count):
            copies[0][k] = quantized


def rotate(rows, gain, rot_cols, scale, last):
    count, tok_rows, part = rows.shape
    shapes = [
        jax.ShapeDtypeStruct((tok_rows, count * part), jnp.bfloat16),
        jax.ShapeDtypeStruct((tok_rows, part), jnp.float32),
        jax.ShapeDtypeStruct(rows.shape, jnp.bfloat16),
    ][: 2 if last else 3]
    return pl.pallas_call(
        rotate_kernel,
        out_shape=shapes,
        in_specs=[VMEM] * 4,
        out_specs=[VMEM] * len(shapes),
        compiler_params=PARAMS,
        name="rotate",
    )(rows, gain, rot_cols, scale)


def project_kernel(quant_ref, weight_ref, stream_ref, out_ref):
    count, tok_rows, part = quant_ref.shape
    total = stream_ref[0].astype(jnp.float32)
    for k in range(count):
        total = total + jnp.dot(
            quant_ref[k], weight_ref[k * part : (k + 1) * part, :], preferred_element_type=jnp.float32
        )
    stream = total.astype(jnp.bfloat16)
    for k in range(count):
        out_ref[k] = stream


def project(quant_rows, weight, copies):
    return pl.pallas_call(
        project_kernel,
        out_shape=jax.ShapeDtypeStruct(copies.shape, jnp.bfloat16),
        in_specs=[VMEM] * 3,
        out_specs=VMEM,
        compiler_params=PARAMS,
        name="project",
    )(quant_rows, weight, copies)


def local(hidden_in, rotation, proj, norm_gain, quant_exp):
    sections = lax.axis_size("section")
    replicas = lax.axis_size("dp")
    tensor = lax.axis_size("tp")
    section_pos = lax.axis_index("section")
    micro_count, tok_rows, part_cols = hidden_in.shape
    stages = sections // STAGE
    planes = sections // 2
    stage_pos = section_pos // STAGE
    place = section_pos % STAGE
    core = section_pos % 2
    same_core = [[2 * z + c for z in range(planes)] for c in range(2)]
    row_block = rotation.shape[0]

    own = proj[0]
    by2 = crossed(own, 2)
    by1 = crossed(own, 1)

    along_z = lax.all_to_all(
        copies_of(rotation, planes), "section", 0, 0, axis_index_groups=same_core, tiled=True
    )
    scale_row = jnp.repeat(jnp.exp2(quant_exp.astype(jnp.float32) * 0.25) * 0.125, GROUP, axis=1)
    params = jnp.concatenate([norm_gain, scale_row], axis=1)
    groups = [[STAGE * g + i for i in range(STAGE)] for g in range(stages)]
    params = lax.all_gather(params, "section", axis=0, tiled=True, axis_index_groups=groups)
    along_z, params = lax.optimization_barrier((along_z, params))
    gains, scales = params[:, :D], params[:, D:]
    along_x = gather(along_z, "dp")
    other_rows = crossed(along_x, 1)
    even_rows = jnp.where(core == 0, along_x, other_rows)
    odd_rows = jnp.where(core == 0, other_rows, along_x)
    rot_cols = jnp.stack([even_rows, odd_rows]).transpose(2, 0, 1, 3, 4).reshape(D, part_cols)

    copies = copies_of(lax.dynamic_index_in_dim(hidden_in, place, 0, keepdims=False), tensor)
    kept_normed = kept_rotated = None
    for stage in range(stages):
        normed_list, rotated_list = [], []
        for layer in range(STAGE):
            last = stage == stages - 1 and layer == STAGE - 1
            rows = exchange(copies, "tp")
            normed, rotated, *quant = rotate(
                rows, gains[layer : layer + 1], rot_cols, scales[layer : layer + 1], last
            )
            normed_list.append(normed)
            rotated_list.append(rotated)
            if stage == 0 and layer == 0:
                by2, _ = lax.optimization_barrier((by2, quant[0]))
                by3 = crossed(by2, 1)
                weights = load_weights(place[None].astype(jnp.int32), own, by1, by2, by3)
            if not last:
                copies = project(exchange(quant[0], "tp"), weights[layer], copies)
        normed_now = jnp.concatenate(normed_list, axis=0)
        rotated_now = jnp.concatenate(rotated_list, axis=0)
        if stage == 0:
            kept_normed, kept_rotated = normed_now, rotated_now
        else:
            valid = stage_pos == stage
            kept_normed = jnp.where(valid, normed_now, kept_normed)
            kept_rotated = jnp.where(valid, rotated_now, kept_rotated)
        if stage < stages - 1:
            stream = lax.ppermute(
                copies[0], "section", [(i, i + STAGE) for i in range(sections - STAGE)]
            )
            copies = copies_of(stream, tensor)

    all_rows = STAGE * tok_rows
    turned = lax.optimization_barrier(kept_normed.T)
    turned = turned.reshape(sections, replicas, row_block, all_rows).transpose(1, 0, 2, 3)
    turned = exchange(turned, "dp")
    turned = turned.transpose(1, 2, 0, 3).reshape(sections * row_block, replicas * all_rows)
    row_scales = jnp.repeat(scales, tok_rows, axis=0)
    level, slope = level_and_slope(kept_rotated, row_scales)
    error_part = level - kept_rotated
    grad_rot = (error_part * (slope - 1.0)).astype(jnp.bfloat16)
    loss = jnp.full((8, 128), jnp.sum(error_part * error_part), jnp.float32)
    losses = exchange(copies_of(loss, replicas * tensor), ("dp", "tp"))
    grad_all = gather(grad_rot, "dp").reshape(replicas * all_rows, part_cols)
    grad_all, losses = lax.optimization_barrier((grad_all, losses))
    terms = jnp.dot(turned, grad_all, preferred_element_type=jnp.float32)
    loss = jnp.sum(losses[:, 0], axis=0, keepdims=True)

    halves = terms.reshape(planes, 2, row_block, part_cols)
    mine = lax.dynamic_index_in_dim(halves, core, 1, keepdims=False)
    other = lax.dynamic_index_in_dim(halves, 1 - core, 1, keepdims=False).astype(jnp.bfloat16)
    pair_sum = (mine + crossed(other, 1).astype(jnp.float32)).astype(jnp.bfloat16)
    loss = (loss + crossed(loss, 1))[0, 0]
    high = lax.reduce_precision(loss, 8, 7)
    middle = lax.reduce_precision(loss - high, 8, 7)
    low = loss - high - middle
    lane = lax.broadcasted_iota(jnp.int32, (16, part_cols), 1)
    tail_rows = jnp.where(lane == 0, high, jnp.where(lane == 1, middle, jnp.where(lane == 2, low, 0.0)))
    tail_rows = tail_rows.astype(jnp.bfloat16)
    sent = jnp.concatenate([pair_sum, copies_of(tail_rows, planes)], axis=1)
    parts = lax.all_to_all(sent, "section", 0, 0, axis_index_groups=same_core, tiled=True)
    sums = jnp.sum(parts.astype(jnp.float32), axis=0)
    factor = 1.0 / math.sqrt(sections * all_rows * replicas)
    norm_count = all_rows * replicas * D
    return (sums[:row_block] * factor, jnp.sum(sums[row_block, :3]) / norm_count)


def solution(mesh):
    placed = (
        P(None, "dp", "tp"),
        P(("section", "dp"), "tp"),
        P("section", None, "tp"),
        P("section", None),
        P("section", "tp"),
    )
    return jax.shard_map(
        local,
        mesh=mesh,
        in_specs=placed,
        out_specs=(P(("section", "dp"), "tp"), P()),
        check_vma=False,
    )
```

```python
import functools
import math

import jax
import jax.numpy as jnp
from jax import lax
from jax.experimental import pallas as pl
from jax.experimental.pallas import tpu as pltpu
from jax.sharding import PartitionSpec as P

D = 4096
GROUP = 128
STAGE = 4

norm_eps = 1e-05
full_turn = 2.0 * math.pi

SIN_TERMS = (3.141592653536291, -5.167712764624543, 2.5501633189471025,
             -0.5992521978250058, 0.08205040181365181, -0.007028386419353805)
COS_TERMS = (0.9999999997799043, -4.934802137078827, 4.058709159556301,
             -1.3352120030506605, 0.23493731381815505, -0.024396324355626643)


def horner(terms, square):
    total = jnp.full_like(square, terms[-1])
    for term in terms[-2::-1]:
        total = total * square + term
    return total


def half_turn(ratio):
    part = ratio - jnp.round(ratio)
    square = part * part
    return part * horner(SIN_TERMS, square), horner(COS_TERMS, square)


def quantize(values, scale):
    ratio = values / scale
    sine, cosine = half_turn(ratio)
    return scale * jnp.clip(ratio - sine * cosine / math.pi, -8.0, 7.0)


def level_and_slope(values, scale):
    ratio = values / scale
    sine, cosine = half_turn(ratio)
    stair = ratio - sine * cosine / math.pi
    inside = (stair > -8.0) & (stair < 7.0)
    level = scale * jnp.clip(stair, -8.0, 7.0)
    return level, jnp.where(inside, 2.0 * sine * sine, 0.0)


def copies_of(value, count):
    return jnp.broadcast_to(value[None], (count,) + value.shape)


def exchange(copies, axis):
    return lax.all_to_all(copies, axis, 0, 0, tiled=True)


def gather(value, axis):
    return exchange(copies_of(value, lax.axis_size(axis)), axis)


def crossed(value, mask):
    return lax.ppermute(value, "section", [(i, i ^ mask) for i in range(lax.axis_size("section"))])


VMEM = pl.BlockSpec(memory_space=pltpu.VMEM)
PARAMS = pltpu.CompilerParams(vmem_limit_bytes=8 * 1024 * 1024)


def pieces_of(layer, place_ref, sources, chunk):
    wanted = place_ref[0] ^ layer
    for mask, pieces in enumerate(sources):
        first = 0
        for piece in pieces:
            for start in range(0, piece.shape[0], chunk):
                yield wanted == mask, (first + start) // chunk, piece.at[pl.ds(start, chunk)]
            first += piece.shape[0]


def start_load(layer, place_ref, refs, into, sems):
    own, by1, by2_head, by2_rest, by3_head, by3_rest = refs
    chunk = into.shape[0] // sems.shape[0]
    sources = ([own], [by1], [by2_head, by2_rest], [by3_head, by3_rest])
    for condition, index, rows in pieces_of(layer, place_ref, sources, chunk):
        @pl.when(condition)
        def _():
            pltpu.make_async_copy(rows, into.at[pl.ds(index * chunk, chunk)], sems.at[index]).start()


def wait_load(refs, into, sems, index):
    chunk = into.shape[0] // sems.shape[0]
    pltpu.make_async_copy(
        refs[0].at[pl.ds(index * chunk, chunk)], into.at[pl.ds(index * chunk, chunk)], sems.at[index]
    ).wait()


def load_kernel(layer, place_ref, *args):
    refs, (out, sems) = args[:6], args[6:]
    start_load(layer, place_ref, refs, out, sems)
    for index in range(sems.shape[0]):
        wait_load(refs, out, sems, index)


def load_weight(layer, place, sources):
    far = pl.BlockSpec(memory_space=pl.ANY)
    own = sources[0]
    return pl.pallas_call(
        functools.partial(load_kernel, layer),
        out_shape=jax.ShapeDtypeStruct(own.shape, own.dtype),
        in_specs=[pl.BlockSpec(memory_space=pltpu.SMEM)] + [far] * 6,
        out_specs=VMEM,
        scratch_shapes=[pltpu.SemaphoreType.DMA((8,))],
        compiler_params=PARAMS,
        name="load_weight",
    )(place, *sources)


def project_from_kernel(layer, place_ref, *args):
    refs, (quant_ref, stream_ref, out_ref, weight_ref, sems) = args[:6], args[6:]
    start_load(layer, place_ref, refs, weight_ref, sems)
    count, tok_rows, part = quant_ref.shape
    total = stream_ref[0].astype(jnp.float32)
    for k in range(count):
        wait_load(refs, weight_ref, sems, k)
        total = total + jnp.dot(
            quant_ref[k], weight_ref[k * part : (k + 1) * part, :], preferred_element_type=jnp.float32
        )
    stream = total.astype(jnp.bfloat16)
    for k in range(count):
        out_ref[k] = stream


def project_from(layer, place, sources, quant_rows, copies):
    far = pl.BlockSpec(memory_space=pl.ANY)
    own = sources[0]
    return pl.pallas_call(
        functools.partial(project_from_kernel, layer),
        out_shape=jax.ShapeDtypeStruct(copies.shape, jnp.bfloat16),
        in_specs=[pl.BlockSpec(memory_space=pltpu.SMEM)] + [far] * 6 + [VMEM] * 2,
        out_specs=VMEM,
        scratch_shapes=[
            pltpu.VMEM(own.shape, own.dtype),
            pltpu.SemaphoreType.DMA((quant_rows.shape[0],)),
        ],
        compiler_params=PARAMS,
        name="project_from",
    )(place, *sources, quant_rows, copies)


def rotate_kernel(rows_ref, gain_ref, rot_ref, scale_ref, normed_ref, rotated_ref, *copies):
    count, _, part = rows_ref.shape
    total = None
    for k in range(count):
        rows = rows_ref[k].astype(jnp.float32)
        square = jnp.sum(rows * rows, axis=-1, keepdims=True)
        total = square if total is None else total + square
    factor = lax.rsqrt(total / (count * part) + norm_eps)
    for k in range(count):
        cols = slice(k * part, (k + 1) * part)
        rows = rows_ref[k].astype(jnp.float32)
        normed_ref[:, cols] = (rows * factor * gain_ref[:, cols]).astype(jnp.bfloat16)
    rotated = jnp.dot(normed_ref[...], rot_ref[...], preferred_element_type=jnp.float32)
    rotated_ref[...] = rotated
    if copies:
        quantized = quantize(rotated, scale_ref[...]).astype(jnp.bfloat16)
        for k in range(count):
            copies[0][k] = quantized


def rotate(rows, gain, rot_cols, scale, last):
    count, tok_rows, part = rows.shape
    shapes = [
        jax.ShapeDtypeStruct((tok_rows, count * part), jnp.bfloat16),
        jax.ShapeDtypeStruct((tok_rows, part), jnp.float32),
        jax.ShapeDtypeStruct(rows.shape, jnp.bfloat16),
    ][: 2 if last else 3]
    return pl.pallas_call(
        rotate_kernel,
        out_shape=shapes,
        in_specs=[VMEM] * 4,
        out_specs=[VMEM] * len(shapes),
        compiler_params=PARAMS,
        name="rotate",
    )(rows, gain, rot_cols, scale)


def project_kernel(quant_ref, weight_ref, stream_ref, out_ref):
    count, tok_rows, part = quant_ref.shape
    total = stream_ref[0].astype(jnp.float32)
    for k in range(count):
        total = total + jnp.dot(
            quant_ref[k], weight_ref[k * part : (k + 1) * part, :], preferred_element_type=jnp.float32
        )
    stream = total.astype(jnp.bfloat16)
    for k in range(count):
        out_ref[k] = stream


def project(quant_rows, weight, copies):
    return pl.pallas_call(
        project_kernel,
        out_shape=jax.ShapeDtypeStruct(copies.shape, jnp.bfloat16),
        in_specs=[VMEM] * 3,
        out_specs=VMEM,
        compiler_params=PARAMS,
        name="project",
    )(quant_rows, weight, copies)


def terms_kernel(part_rows, core_ref, parts_ref, mine_ref, other_ref):
    sources, rows, lanes = parts_ref.shape
    count, _, cols = mine_ref.shape
    features = 2 * count * part_rows
    left = jnp.concatenate([parts_ref[s, :features] for s in range(sources)], axis=1)
    right = jnp.concatenate(
        [
            jnp.concatenate([parts_ref[s, pl.ds(k, lanes)] for k in range(features, rows, lanes)], axis=1)
            for s in range(sources)
        ],
        axis=0,
    )
    terms = jnp.dot(left, right, preferred_element_type=jnp.float32)
    lower = core_ref[0] == 0
    for z in range(count):
        even = terms[2 * z * part_rows : (2 * z + 1) * part_rows]
        odd = terms[(2 * z + 1) * part_rows : (2 * z + 2) * part_rows]
        mine_ref[z] = jnp.where(lower, even, odd)
        other_ref[z] = jnp.where(lower, odd, even).astype(jnp.bfloat16)


def terms_of(core, parts, planes, row_block, part_cols):
    shape = (planes, row_block, part_cols)
    return pl.pallas_call(
        functools.partial(terms_kernel, row_block),
        out_shape=[jax.ShapeDtypeStruct(shape, jnp.float32), jax.ShapeDtypeStruct(shape, jnp.bfloat16)],
        in_specs=[pl.BlockSpec(memory_space=pltpu.SMEM), VMEM],
        out_specs=[VMEM, VMEM],
        compiler_params=pltpu.CompilerParams(vmem_limit_bytes=24 * 1024 * 1024),
        name="terms",
    )(core[None].astype(jnp.int32), parts)


def local(hidden_in, rotation, proj, norm_gain, quant_exp):
    sections = lax.axis_size("section")
    replicas = lax.axis_size("dp")
    tensor = lax.axis_size("tp")
    section_pos = lax.axis_index("section")
    micro_count, tok_rows, part_cols = hidden_in.shape
    stages = sections // STAGE
    planes = sections // 2
    stage_pos = section_pos // STAGE
    place = section_pos % STAGE
    core = section_pos % 2
    same_core = [[2 * z + c for z in range(planes)] for c in range(2)]
    row_block = rotation.shape[0]

    own = proj[0]
    by1 = crossed(own, 1)
    head = D // 4
    by2_head = crossed(own[:head], 2)
    by2_rest = crossed(own[head:], 2)

    along_z = lax.all_to_all(
        copies_of(rotation, planes), "section", 0, 0, axis_index_groups=same_core, tiled=True
    )
    scale_row = jnp.repeat(jnp.exp2(quant_exp.astype(jnp.float32) * 0.25) * 0.125, GROUP, axis=1)
    params = jnp.concatenate([norm_gain, scale_row], axis=1)
    groups = [[STAGE * g + i for i in range(STAGE)] for g in range(stages)]
    params = lax.all_gather(params, "section", axis=0, tiled=True, axis_index_groups=groups)
    along_z, params, by2_head = lax.optimization_barrier((along_z, params, by2_head))
    by3_head = crossed(by2_head, 1)
    gains, scales = params[:, :D], params[:, D:]
    along_x = gather(along_z, "dp")
    other_rows = crossed(along_x, 1)
    even_rows = jnp.where(core == 0, along_x, other_rows)
    odd_rows = jnp.where(core == 0, other_rows, along_x)
    rot_cols = jnp.stack([even_rows, odd_rows]).transpose(2, 0, 1, 3, 4).reshape(D, part_cols)

    copies = copies_of(lax.dynamic_index_in_dim(hidden_in, place, 0, keepdims=False), tensor)
    kept_normed = kept_rotated = None
    weights = []
    where = place[None].astype(jnp.int32)
    for stage in range(stages):
        normed_list, rotated_list = [], []
        for layer in range(STAGE):
            last = stage == stages - 1 and layer == STAGE - 1
            rows = exchange(copies, "tp")
            normed, rotated, *quant = rotate(
                rows, gains[layer : layer + 1], rot_cols, scales[layer : layer + 1], last
            )
            normed_list.append(normed)
            rotated_list.append(rotated)
            if last:
                break
            if stage == 0 and layer == 0:
                by2_rest, _ = lax.optimization_barrier((by2_rest, quant[0]))
                by3_rest = crossed(by2_rest, 1)
                sources = (own, by1, by2_head, by2_rest, by3_head, by3_rest)
            quant_rows = exchange(quant[0], "tp")
            if stage == 0:
                copies = project_from(layer, where, sources, quant_rows, copies)
                later, _ = lax.optimization_barrier((where, copies))
                weights.append(load_weight(layer, later, sources))
            else:
                copies = project(quant_rows, weights[layer], copies)
        normed_now = jnp.concatenate(normed_list, axis=0)
        rotated_now = jnp.concatenate(rotated_list, axis=0)
        if stage == 0:
            kept_normed, kept_rotated = normed_now, rotated_now
        else:
            valid = stage_pos == stage
            kept_normed = jnp.where(valid, normed_now, kept_normed)
            kept_rotated = jnp.where(valid, rotated_now, kept_rotated)
        if stage < stages - 1:
            stream = lax.ppermute(
                copies[0], "section", [(i, i + STAGE) for i in range(sections - STAGE)]
            )
            copies = copies_of(stream, tensor)

    all_rows = STAGE * tok_rows
    lanes = all_rows
    turned = lax.optimization_barrier(kept_normed.T)
    turned = turned.reshape(sections, replicas, row_block, lanes).transpose(1, 0, 2, 3)
    turned = turned.reshape(replicas, sections * row_block, lanes)
    row_scales = jnp.repeat(scales, tok_rows, axis=0)
    level, slope = level_and_slope(kept_rotated, row_scales)
    error_part = level - kept_rotated
    grad_rot = (error_part * (slope - 1.0)).astype(jnp.bfloat16)
    grad_rot = grad_rot.reshape(all_rows, part_cols // lanes, lanes).transpose(1, 0, 2)
    sent = jnp.concatenate([turned, copies_of(grad_rot.reshape(-1, lanes), replicas)], axis=1)
    parts = exchange(sent, "dp")
    mine, other = terms_of(core, parts, planes, row_block, part_cols)
    loss = jnp.full((8, 128), jnp.sum(error_part * error_part), jnp.float32)
    loss, _ = lax.optimization_barrier((loss, parts))
    losses = exchange(copies_of(loss, replicas * tensor), ("dp", "tp"))
    loss = jnp.sum(losses[:, 0], axis=0, keepdims=True)

    pair_sum = (mine + crossed(other, 1).astype(jnp.float32)).astype(jnp.bfloat16)
    loss = (loss + crossed(loss, 1))[0, 0]
    high = lax.reduce_precision(loss, 8, 7)
    middle = lax.reduce_precision(loss - high, 8, 7)
    low = loss - high - middle
    lane = lax.broadcasted_iota(jnp.int32, (16, part_cols), 1)
    tail_rows = jnp.where(lane == 0, high, jnp.where(lane == 1, middle, jnp.where(lane == 2, low, 0.0)))
    tail_rows = tail_rows.astype(jnp.bfloat16)
    sent = jnp.concatenate([pair_sum, copies_of(tail_rows, planes)], axis=1)
    parts = lax.all_to_all(sent, "section", 0, 0, axis_index_groups=same_core, tiled=True)
    sums = jnp.sum(parts.astype(jnp.float32), axis=0)
    factor = 1.0 / math.sqrt(sections * all_rows * replicas)
    norm_count = all_rows * replicas * D
    return (sums[:row_block] * factor, jnp.sum(sums[row_block, :3]) / norm_count)


def solution(mesh):
    placed = (
        P(None, "dp", "tp"),
        P(("section", "dp"), "tp"),
        P("section", None, "tp"),
        P("section", None),
        P("section", "tp"),
    )
    return jax.shard_map(
        local,
        mesh=mesh,
        in_specs=placed,
        out_specs=(P(("section", "dp"), "tp"), P()),
        check_vma=False,
    )
```

```python
import functools
import math

import jax
import jax.numpy as jnp
from jax import lax
from jax.experimental import pallas as pl
from jax.experimental.pallas import tpu as pltpu
from jax.sharding import PartitionSpec as P

D = 4096
GROUP = 128
STAGE = 4

norm_eps = 1e-05
full_turn = 2.0 * math.pi

SIN_TERMS = (3.141592653536291, -5.167712764624543, 2.5501633189471025,
             -0.5992521978250058, 0.08205040181365181, -0.007028386419353805)
COS_TERMS = (0.9999999997799043, -4.934802137078827, 4.058709159556301,
             -1.3352120030506605, 0.23493731381815505, -0.024396324355626643)


def horner(terms, square):
    total = jnp.full_like(square, terms[-1])
    for term in terms[-2::-1]:
        total = total * square + term
    return total


def half_turn(ratio):
    part = ratio - jnp.round(ratio)
    square = part * part
    return part * horner(SIN_TERMS, square), horner(COS_TERMS, square)


def quantize(values, scale):
    ratio = values / scale
    sine, cosine = half_turn(ratio)
    return scale * jnp.clip(ratio - sine * cosine / math.pi, -8.0, 7.0)


def level_and_slope(values, scale):
    ratio = values / scale
    sine, cosine = half_turn(ratio)
    stair = ratio - sine * cosine / math.pi
    inside = (stair > -8.0) & (stair < 7.0)
    level = scale * jnp.clip(stair, -8.0, 7.0)
    return level, jnp.where(inside, 2.0 * sine * sine, 0.0)


def copies_of(value, count):
    return jnp.broadcast_to(value[None], (count,) + value.shape)


def exchange(copies, axis):
    return lax.all_to_all(copies, axis, 0, 0, tiled=True)


def gather(value, axis):
    return exchange(copies_of(value, lax.axis_size(axis)), axis)


def crossed(value, mask):
    return lax.ppermute(value, "section", [(i, i ^ mask) for i in range(lax.axis_size("section"))])


VMEM = pl.BlockSpec(memory_space=pltpu.VMEM)
SMEM = pl.BlockSpec(memory_space=pltpu.SMEM)
FAR = pl.BlockSpec(memory_space=pl.ANY)
PARAMS = pltpu.CompilerParams(vmem_limit_bytes=8 * 1024 * 1024)


def start_load(layer, place_ref, refs, into, sems):
    chunks = sems.shape[0]
    chunk = into.shape[0] // chunks
    plane, core = place_ref[0] // 2, place_ref[0] % 2
    own, by1, even_mine, even_other, odd_mine, odd_other = refs
    mine, other = (odd_mine, odd_other) if layer % 2 else (even_mine, even_other)
    here, same = plane == layer // 2, core == layer % 2
    away, differs = jnp.logical_not(here), jnp.logical_not(same)
    for wanted, source in (
        (here & same, own), (here & differs, by1), (away & same, mine), (away & differs, other)
    ):
        @pl.when(wanted)
        def _():
            for index in range(chunks):
                rows = pl.ds(index * chunk, chunk)
                pltpu.make_async_copy(source.at[rows], into.at[rows], sems.at[index]).start()


def project_kernel(layer, place_ref, *args):
    refs, (quant_ref, stream_ref, copies_ref, out_ref, weight_ref, sems) = args[:6], args[6:]
    start_load(layer, place_ref, refs, weight_ref, sems)
    count, tok_rows, part = quant_ref.shape
    total = stream_ref[...].astype(jnp.float32)
    for k in range(count):
        rows = pl.ds(k * part, part)
        pltpu.make_async_copy(refs[0].at[rows], weight_ref.at[rows], sems.at[k]).wait()
        total = total + jnp.dot(quant_ref[k], weight_ref[rows], preferred_element_type=jnp.float32)
    stream = total.astype(jnp.bfloat16)
    out_ref[...] = stream
    for k in range(count):
        copies_ref[k] = stream


def project(layer, place, sources, quant_rows, stream):
    own = sources[0]
    return pl.pallas_call(
        functools.partial(project_kernel, layer),
        out_shape=[
            jax.ShapeDtypeStruct(quant_rows.shape, jnp.bfloat16),
            jax.ShapeDtypeStruct(stream.shape, jnp.bfloat16),
        ],
        in_specs=[SMEM] + [FAR] * 6 + [VMEM] * 2,
        out_specs=[VMEM] * 2,
        scratch_shapes=[
            pltpu.VMEM(own.shape, own.dtype),
            pltpu.SemaphoreType.DMA((quant_rows.shape[0],)),
        ],
        compiler_params=pltpu.CompilerParams(vmem_limit_bytes=56 * 1024 * 1024),
        name="project",
    )(place, *sources, quant_rows, stream)


def rotate_kernel(layer, last, keep_ref, rows_ref, gain_ref, rot_ref, scale_ref, _, __, *rest):
    (kept_normed, kept_rotated), rest = rest[:2], rest[2:]
    copies, (normed_ref, rotated_ref, sems) = rest[:-3], rest[-3:]
    count, tok_rows, part = rows_ref.shape
    place = pl.ds(layer * tok_rows, tok_rows)
    keep = keep_ref[0] == 1
    keep_normed = pltpu.make_async_copy(normed_ref, kept_normed.at[place], sems.at[0])
    keep_rotated = pltpu.make_async_copy(rotated_ref, kept_rotated.at[place], sems.at[1])
    total = None
    for k in range(count):
        rows = rows_ref[k].astype(jnp.float32)
        square = jnp.sum(rows * rows, axis=-1, keepdims=True)
        total = square if total is None else total + square
    factor = lax.rsqrt(total / (count * part) + norm_eps)
    for k in range(count):
        cols = slice(k * part, (k + 1) * part)
        rows = rows_ref[k].astype(jnp.float32)
        normed_ref[:, cols] = (rows * factor * gain_ref[:, cols]).astype(jnp.bfloat16)
    pl.when(keep)(keep_normed.start)
    rotated = jnp.dot(normed_ref[...], rot_ref[...], preferred_element_type=jnp.float32)
    rotated_ref[...] = rotated
    pl.when(keep)(keep_rotated.start)
    if not last:
        quantized = quantize(rotated, scale_ref[...]).astype(jnp.bfloat16)
        for k in range(count):
            copies[0][k] = quantized

    @pl.when(keep)
    def _():
        keep_normed.wait()
        keep_rotated.wait()


def rotate(layer, last, keep, rows, gain, rot_cols, scale, kept):
    count, tok_rows, part = rows.shape
    shapes = [jax.ShapeDtypeStruct(k.shape, k.dtype) for k in kept]
    if not last:
        shapes.append(jax.ShapeDtypeStruct(rows.shape, jnp.bfloat16))
    return pl.pallas_call(
        functools.partial(rotate_kernel, layer, last),
        out_shape=shapes,
        in_specs=[SMEM] + [VMEM] * 4 + [FAR] * 2,
        out_specs=[FAR] * 2 + [VMEM] * (len(shapes) - 2),
        input_output_aliases={5: 0, 6: 1},
        scratch_shapes=[
            pltpu.VMEM((tok_rows, count * part), jnp.bfloat16),
            pltpu.VMEM((tok_rows, part), jnp.float32),
            pltpu.SemaphoreType.DMA((2,)),
        ],
        compiler_params=PARAMS,
        name="rotate",
    )(keep, rows, gain, rot_cols, scale, *kept)


def terms_kernel(part_rows, core_ref, parts_ref, mine_ref, other_ref):
    sources, rows, lanes = parts_ref.shape
    count, _, cols = mine_ref.shape
    features = 2 * count * part_rows
    left = jnp.concatenate([parts_ref[s, :features] for s in range(sources)], axis=1)
    right = jnp.concatenate(
        [
            jnp.concatenate([parts_ref[s, pl.ds(k, lanes)] for k in range(features, rows, lanes)], axis=1)
            for s in range(sources)
        ],
        axis=0,
    )
    terms = jnp.dot(left, right, preferred_element_type=jnp.float32)
    lower = core_ref[0] == 0
    for z in range(count):
        even = terms[2 * z * part_rows : (2 * z + 1) * part_rows]
        odd = terms[(2 * z + 1) * part_rows : (2 * z + 2) * part_rows]
        mine_ref[z] = jnp.where(lower, even, odd)
        other_ref[z] = jnp.where(lower, odd, even).astype(jnp.bfloat16)


def terms_of(core, parts, planes, row_block, part_cols):
    shape = (planes, row_block, part_cols)
    return pl.pallas_call(
        functools.partial(terms_kernel, row_block),
        out_shape=[jax.ShapeDtypeStruct(shape, jnp.float32), jax.ShapeDtypeStruct(shape, jnp.bfloat16)],
        in_specs=[pl.BlockSpec(memory_space=pltpu.SMEM), VMEM],
        out_specs=[VMEM, VMEM],
        compiler_params=pltpu.CompilerParams(vmem_limit_bytes=24 * 1024 * 1024),
        name="terms",
    )(core[None].astype(jnp.int32), parts)


def local(hidden_in, rotation, proj, norm_gain, quant_exp):
    sections = lax.axis_size("section")
    replicas = lax.axis_size("dp")
    tensor = lax.axis_size("tp")
    section_pos = lax.axis_index("section")
    micro_count, tok_rows, part_cols = hidden_in.shape
    stages = sections // STAGE
    planes = sections // 2
    stage_pos = section_pos // STAGE
    place = section_pos % STAGE
    core = section_pos % 2
    same_core = [[2 * z + c for z in range(planes)] for c in range(2)]
    row_block = rotation.shape[0]

    own = proj[0]
    by1 = crossed(own, 1)
    even_mine = lax.ppermute(own, "section", [(i, i ^ 2) for i in range(0, sections, 2)])

    scale_row = jnp.repeat(jnp.exp2(quant_exp.astype(jnp.float32) * 0.25) * 0.125, GROUP, axis=1)
    params = jnp.concatenate([norm_gain, scale_row], axis=1)
    params_by1 = crossed(params, 1)
    params_by2 = crossed(jnp.concatenate([params, params_by1], axis=0), 2)
    found = jnp.concatenate([params, params_by1, params_by2], axis=0)
    params = jnp.stack([lax.dynamic_index_in_dim(found, place ^ k, 0, False) for k in range(STAGE)])
    gains, scales = params[:, :D], params[:, D:]

    along_z = lax.all_to_all(
        copies_of(rotation, planes), "section", 0, 0, axis_index_groups=same_core, tiled=True
    )
    along_x = gather(along_z, "dp")
    other_rows = crossed(along_x, 1)
    own_later, _ = lax.optimization_barrier((own, other_rows))
    odd_mine = lax.ppermute(own_later, "section", [(i, i ^ 2) for i in range(1, sections, 2)])
    even_rows = jnp.where(core == 0, along_x, other_rows)
    odd_rows = jnp.where(core == 0, other_rows, along_x)
    rot_cols = jnp.stack([even_rows, odd_rows]).transpose(2, 0, 1, 3, 4).reshape(D, part_cols)

    where = place[None].astype(jnp.int32)
    all_rows = STAGE * tok_rows
    stream = lax.dynamic_index_in_dim(hidden_in, place, 0, keepdims=False)
    copies = copies_of(stream, tensor)
    kept = (jnp.zeros((all_rows, D), jnp.bfloat16), jnp.zeros((all_rows, part_cols), jnp.float32))
    for stage in range(stages):
        keep = jnp.full((1,), 1, jnp.int32) if stage == 0 else (stage_pos == stage).astype(jnp.int32)[None]
        for layer in range(STAGE):
            last = stage == stages - 1 and layer == STAGE - 1
            gain, scale = gains[layer : layer + 1], scales[layer : layer + 1]
            results = rotate(layer, last, keep, exchange(copies, "tp"), gain, rot_cols, scale, kept)
            kept = results[:2]
            if last:
                break
            quant = results[2]
            if stage == 0 and layer == 0:
                even_mine, _ = lax.optimization_barrier((even_mine, quant))
                even_other = lax.ppermute(even_mine, "section", [(i, i + 1) for i in range(0, sections, 2)])
                sources = (own, by1, even_mine, even_other, even_mine, even_other)
            if stage == 0 and layer == 1:
                odd_mine, _ = lax.optimization_barrier((odd_mine, quant))
                odd_other = lax.ppermute(odd_mine, "section", [(i + 1, i) for i in range(0, sections, 2)])
                sources = (own, by1, even_mine, even_other, odd_mine, odd_other)
            copies, stream = project(layer, where, sources, exchange(quant, "tp"), stream)
        if stage < stages - 1:
            stream = lax.ppermute(
                stream, "section", [(i, i + STAGE) for i in range(sections - STAGE)]
            )
            copies = copies_of(stream, tensor)
    kept_normed, kept_rotated = kept

    lanes = all_rows
    turned = lax.optimization_barrier(kept_normed.T)
    turned = turned.reshape(sections, replicas, row_block, lanes).transpose(1, 0, 2, 3)
    turned = turned.reshape(replicas, sections * row_block, lanes)
    row_scales = jnp.repeat(scales, tok_rows, axis=0)
    level, slope = level_and_slope(kept_rotated, row_scales)
    error_part = level - kept_rotated
    grad_rot = (error_part * (slope - 1.0)).astype(jnp.bfloat16)
    grad_rot = grad_rot.reshape(all_rows, part_cols // lanes, lanes).transpose(1, 0, 2)
    sent = jnp.concatenate([turned, copies_of(grad_rot.reshape(-1, lanes), replicas)], axis=1)
    parts = exchange(sent, "dp")
    mine, other = terms_of(core, parts, planes, row_block, part_cols)
    loss = jnp.full((8, 128), jnp.sum(error_part * error_part), jnp.float32)
    loss = loss + crossed(loss, 1)
    loss, _ = lax.optimization_barrier((loss, other))
    losses = exchange(copies_of(loss, replicas * tensor), ("dp", "tp"))
    loss = jnp.sum(losses[:, 0, 0])

    pair_sum = (mine + crossed(other, 1).astype(jnp.float32)).astype(jnp.bfloat16)
    high = lax.reduce_precision(loss, 8, 7)
    middle = lax.reduce_precision(loss - high, 8, 7)
    low = loss - high - middle
    lane = lax.broadcasted_iota(jnp.int32, (16, part_cols), 1)
    tail_rows = jnp.where(lane == 0, high, jnp.where(lane == 1, middle, jnp.where(lane == 2, low, 0.0)))
    tail_rows = tail_rows.astype(jnp.bfloat16)
    sent = jnp.concatenate([pair_sum, copies_of(tail_rows, planes)], axis=1)
    parts = lax.all_to_all(sent, "section", 0, 0, axis_index_groups=same_core, tiled=True)
    sums = jnp.sum(parts.astype(jnp.float32), axis=0)
    factor = 1.0 / math.sqrt(sections * all_rows * replicas)
    norm_count = all_rows * replicas * D
    return (sums[:row_block] * factor, jnp.sum(sums[row_block, :3]) / norm_count)


def solution(mesh):
    placed = (
        P(None, "dp", "tp"),
        P(("section", "dp"), "tp"),
        P("section", None, "tp"),
        P("section", None),
        P("section", "tp"),
    )
    return jax.shard_map(
        local,
        mesh=mesh,
        in_specs=placed,
        out_specs=(P(("section", "dp"), "tp"), P()),
        check_vma=False,
    )
```

```python
import functools
import math

import jax
import jax.numpy as jnp
from jax import lax
from jax.experimental import pallas as pl
from jax.experimental.pallas import tpu as pltpu
from jax.sharding import PartitionSpec as P

D = 4096
GROUP = 128
STAGE = 4

norm_eps = 1e-05
full_turn = 2.0 * math.pi

SIN_TERMS = (3.141592653536291, -5.167712764624543, 2.5501633189471025,
             -0.5992521978250058, 0.08205040181365181, -0.007028386419353805)
COS_TERMS = (0.9999999997799043, -4.934802137078827, 4.058709159556301,
             -1.3352120030506605, 0.23493731381815505, -0.024396324355626643)


def horner(terms, square):
    total = jnp.full_like(square, terms[-1])
    for term in terms[-2::-1]:
        total = total * square + term
    return total


def half_turn(ratio):
    part = ratio - jnp.round(ratio)
    square = part * part
    return part * horner(SIN_TERMS, square), horner(COS_TERMS, square)


def quantize(values, scale):
    ratio = values / scale
    sine, cosine = half_turn(ratio)
    return scale * jnp.clip(ratio - sine * cosine / math.pi, -8.0, 7.0)


def level_and_slope(values, scale):
    ratio = values / scale
    sine, cosine = half_turn(ratio)
    stair = ratio - sine * cosine / math.pi
    inside = (stair > -8.0) & (stair < 7.0)
    level = scale * jnp.clip(stair, -8.0, 7.0)
    return level, jnp.where(inside, 2.0 * sine * sine, 0.0)


def copies_of(value, count):
    return jnp.broadcast_to(value[None], (count,) + value.shape)


def exchange(copies, axis):
    return lax.all_to_all(copies, axis, 0, 0, tiled=True)


def gather(value, axis):
    return exchange(copies_of(value, lax.axis_size(axis)), axis)


def crossed(value, mask):
    return lax.ppermute(value, "section", [(i, i ^ mask) for i in range(lax.axis_size("section"))])


VMEM = pl.BlockSpec(memory_space=pltpu.VMEM)
SMEM = pl.BlockSpec(memory_space=pltpu.SMEM)
FAR = pl.BlockSpec(memory_space=pl.ANY)
PARAMS = pltpu.CompilerParams(vmem_limit_bytes=8 * 1024 * 1024)


def start_load(layer, place_ref, refs, into, sems):
    chunks = sems.shape[0]
    chunk = into.shape[0] // chunks
    plane, core = place_ref[0] // 2, place_ref[0] % 2
    own, by1, even_mine, even_other, odd_mine, odd_other = refs
    mine, other = (odd_mine, odd_other) if layer % 2 else (even_mine, even_other)
    here, same = plane == layer // 2, core == layer % 2
    away, differs = jnp.logical_not(here), jnp.logical_not(same)
    for wanted, source in (
        (here & same, own), (here & differs, by1), (away & same, mine), (away & differs, other)
    ):
        @pl.when(wanted)
        def _():
            for index in range(chunks):
                rows = pl.ds(index * chunk, chunk)
                pltpu.make_async_copy(source.at[rows], into.at[rows], sems.at[index]).start()


def project_from_kernel(layer, place_ref, *args):
    refs, (quant_ref, stream_ref, copies_ref, out_ref, weight_ref, sems) = args[:6], args[6:]
    start_load(layer, place_ref, refs, weight_ref, sems)
    count, tok_rows, part = quant_ref.shape
    total = stream_ref[...].astype(jnp.float32)
    for k in range(count):
        rows = pl.ds(k * part, part)
        pltpu.make_async_copy(refs[0].at[rows], weight_ref.at[rows], sems.at[k]).wait()
        total = total + jnp.dot(quant_ref[k], weight_ref[rows], preferred_element_type=jnp.float32)
    stream = total.astype(jnp.bfloat16)
    out_ref[...] = stream
    for k in range(count):
        copies_ref[k] = stream


def project_from(layer, place, sources, quant_rows, stream):
    own = sources[0]
    return pl.pallas_call(
        functools.partial(project_from_kernel, layer),
        out_shape=[
            jax.ShapeDtypeStruct(quant_rows.shape, jnp.bfloat16),
            jax.ShapeDtypeStruct(stream.shape, jnp.bfloat16),
        ],
        in_specs=[SMEM] + [FAR] * 6 + [VMEM] * 2,
        out_specs=[VMEM] * 2,
        scratch_shapes=[
            pltpu.VMEM(own.shape, own.dtype),
            pltpu.SemaphoreType.DMA((quant_rows.shape[0],)),
        ],
        compiler_params=PARAMS,
        name="project_from",
    )(place, *sources, quant_rows, stream)


def project_kernel(quant_ref, weight_ref, stream_ref, copies_ref, out_ref):
    count, tok_rows, part = quant_ref.shape
    total = stream_ref[...].astype(jnp.float32)
    for k in range(count):
        rows = pl.ds(k * part, part)
        total = total + jnp.dot(quant_ref[k], weight_ref[rows], preferred_element_type=jnp.float32)
    stream = total.astype(jnp.bfloat16)
    out_ref[...] = stream
    for k in range(count):
        copies_ref[k] = stream


def project(quant_rows, weight, stream):
    return pl.pallas_call(
        project_kernel,
        out_shape=[
            jax.ShapeDtypeStruct(quant_rows.shape, jnp.bfloat16),
            jax.ShapeDtypeStruct(stream.shape, jnp.bfloat16),
        ],
        in_specs=[VMEM] * 3,
        out_specs=[VMEM] * 2,
        compiler_params=PARAMS,
        name="project",
    )(quant_rows, weight, stream)


def rotate_kernel(layer, last, keep_ref, rows_ref, gain_ref, rot_ref, scale_ref, _, __, *rest):
    (kept_normed, kept_rotated), rest = rest[:2], rest[2:]
    copies, (normed_ref, rotated_ref, sems) = rest[:-3], rest[-3:]
    count, tok_rows, part = rows_ref.shape
    place = pl.ds(layer * tok_rows, tok_rows)
    keep = keep_ref[0] == 1
    keep_normed = pltpu.make_async_copy(normed_ref, kept_normed.at[place], sems.at[0])
    keep_rotated = pltpu.make_async_copy(rotated_ref, kept_rotated.at[place], sems.at[1])
    total = None
    for k in range(count):
        rows = rows_ref[k].astype(jnp.float32)
        square = jnp.sum(rows * rows, axis=-1, keepdims=True)
        total = square if total is None else total + square
    factor = lax.rsqrt(total / (count * part) + norm_eps)
    for k in range(count):
        cols = slice(k * part, (k + 1) * part)
        rows = rows_ref[k].astype(jnp.float32)
        normed_ref[:, cols] = (rows * factor * gain_ref[:, cols]).astype(jnp.bfloat16)
    pl.when(keep)(keep_normed.start)
    rotated = jnp.dot(normed_ref[...], rot_ref[...], preferred_element_type=jnp.float32)
    rotated_ref[...] = rotated
    pl.when(keep)(keep_rotated.start)
    if not last:
        quantized = quantize(rotated, scale_ref[...]).astype(jnp.bfloat16)
        for k in range(count):
            copies[0][k] = quantized

    @pl.when(keep)
    def _():
        keep_normed.wait()
        keep_rotated.wait()


def rotate(layer, last, keep, rows, gain, rot_cols, scale, kept):
    count, tok_rows, part = rows.shape
    shapes = [jax.ShapeDtypeStruct(k.shape, k.dtype) for k in kept]
    if not last:
        shapes.append(jax.ShapeDtypeStruct(rows.shape, jnp.bfloat16))
    return pl.pallas_call(
        functools.partial(rotate_kernel, layer, last),
        out_shape=shapes,
        in_specs=[SMEM] + [VMEM] * 4 + [FAR] * 2,
        out_specs=[FAR] * 2 + [VMEM] * (len(shapes) - 2),
        input_output_aliases={5: 0, 6: 1},
        scratch_shapes=[
            pltpu.VMEM((tok_rows, count * part), jnp.bfloat16),
            pltpu.VMEM((tok_rows, part), jnp.float32),
            pltpu.SemaphoreType.DMA((2,)),
        ],
        compiler_params=PARAMS,
        name="rotate",
    )(keep, rows, gain, rot_cols, scale, *kept)


def terms_kernel(part_rows, core_ref, parts_ref, mine_ref, other_ref):
    sources, rows, lanes = parts_ref.shape
    count, _, cols = mine_ref.shape
    features = 2 * count * part_rows
    left = jnp.concatenate([parts_ref[s, :features] for s in range(sources)], axis=1)
    right = jnp.concatenate(
        [
            jnp.concatenate([parts_ref[s, pl.ds(k, lanes)] for k in range(features, rows, lanes)], axis=1)
            for s in range(sources)
        ],
        axis=0,
    )
    terms = jnp.dot(left, right, preferred_element_type=jnp.float32)
    lower = core_ref[0] == 0
    for z in range(count):
        even = terms[2 * z * part_rows : (2 * z + 1) * part_rows]
        odd = terms[(2 * z + 1) * part_rows : (2 * z + 2) * part_rows]
        mine_ref[z] = jnp.where(lower, even, odd)
        other_ref[z] = jnp.where(lower, odd, even).astype(jnp.bfloat16)


def terms_of(core, parts, planes, row_block, part_cols):
    shape = (planes, row_block, part_cols)
    return pl.pallas_call(
        functools.partial(terms_kernel, row_block),
        out_shape=[jax.ShapeDtypeStruct(shape, jnp.float32), jax.ShapeDtypeStruct(shape, jnp.bfloat16)],
        in_specs=[pl.BlockSpec(memory_space=pltpu.SMEM), VMEM],
        out_specs=[VMEM, VMEM],
        compiler_params=pltpu.CompilerParams(vmem_limit_bytes=24 * 1024 * 1024),
        name="terms",
    )(core[None].astype(jnp.int32), parts)


def local(hidden_in, rotation, proj, norm_gain, quant_exp):
    sections = lax.axis_size("section")
    replicas = lax.axis_size("dp")
    tensor = lax.axis_size("tp")
    section_pos = lax.axis_index("section")
    micro_count, tok_rows, part_cols = hidden_in.shape
    stages = sections // STAGE
    planes = sections // 2
    stage_pos = section_pos // STAGE
    place = section_pos % STAGE
    core = section_pos % 2
    same_core = [[2 * z + c for z in range(planes)] for c in range(2)]
    row_block = rotation.shape[0]

    own = proj[0]
    by1 = crossed(own, 1)
    even_mine = lax.ppermute(own, "section", [(i, i ^ 2) for i in range(0, sections, 2)])

    scale_row = jnp.repeat(jnp.exp2(quant_exp.astype(jnp.float32) * 0.25) * 0.125, GROUP, axis=1)
    params = jnp.concatenate([norm_gain, scale_row], axis=1)
    params_by1 = crossed(params, 1)
    params_by2 = crossed(jnp.concatenate([params, params_by1], axis=0), 2)
    found = jnp.concatenate([params, params_by1, params_by2], axis=0)
    params = jnp.stack([lax.dynamic_index_in_dim(found, place ^ k, 0, False) for k in range(STAGE)])
    gains, scales = params[:, :D], params[:, D:]

    along_z = lax.all_to_all(
        copies_of(rotation, planes), "section", 0, 0, axis_index_groups=same_core, tiled=True
    )
    along_z, gains, scales = lax.optimization_barrier((along_z, gains, scales))
    along_x = gather(along_z, "dp")
    other_rows = crossed(along_x, 1)
    own_later, _ = lax.optimization_barrier((own, other_rows))
    odd_mine = lax.ppermute(own_later, "section", [(i, i ^ 2) for i in range(1, sections, 2)])
    even_rows = jnp.where(core == 0, along_x, other_rows)
    odd_rows = jnp.where(core == 0, other_rows, along_x)
    rot_cols = jnp.stack([even_rows, odd_rows]).transpose(2, 0, 1, 3, 4).reshape(D, part_cols)

    where = place[None].astype(jnp.int32)
    all_rows = STAGE * tok_rows
    stream = lax.dynamic_index_in_dim(hidden_in, place, 0, keepdims=False)
    copies = copies_of(stream, tensor)
    kept = (jnp.zeros((all_rows, D), jnp.bfloat16), jnp.zeros((all_rows, part_cols), jnp.float32))
    weights = []
    for stage in range(stages):
        keep = jnp.full((1,), 1, jnp.int32) if stage == 0 else (stage_pos == stage).astype(jnp.int32)[None]
        for layer in range(STAGE):
            last = stage == stages - 1 and layer == STAGE - 1
            gain, scale = gains[layer : layer + 1], scales[layer : layer + 1]
            rows = exchange(copies, "tp")
            if stage == 0 and layer > 0 or stage == 1 and layer == 0:
                done = (layer - 1) % STAGE
                mine, other = sources[4:] if done % 2 else sources[2:4]
                weight = jnp.where(core == done % 2, mine, other)
                near = jnp.where(core == done % 2, own, by1)
                weight = jnp.where(place // 2 == done // 2, near, weight)
                rows, weight = lax.optimization_barrier((rows, weight))
                weights.append(weight)
            results = rotate(layer, last, keep, rows, gain, rot_cols, scale, kept)
            kept = results[:2]
            if last:
                break
            quant = results[2]
            if stage == 0 and layer == 0:
                even_mine, _ = lax.optimization_barrier((even_mine, quant))
                even_other = lax.ppermute(even_mine, "section", [(i, i + 1) for i in range(0, sections, 2)])
                sources = (own, by1, even_mine, even_other, even_mine, even_other)
            if stage == 0 and layer == 1:
                odd_mine, _ = lax.optimization_barrier((odd_mine, quant))
                odd_other = lax.ppermute(odd_mine, "section", [(i + 1, i) for i in range(0, sections, 2)])
                sources = (own, by1, even_mine, even_other, odd_mine, odd_other)
            quant_rows = exchange(quant, "tp")
            if stage == 0:
                copies, stream = project_from(layer, where, sources, quant_rows, stream)
            else:
                copies, stream = project(quant_rows, weights[layer], stream)
        if stage < stages - 1:
            stream = lax.ppermute(
                stream, "section", [(i, i + STAGE) for i in range(sections - STAGE)]
            )
            copies = copies_of(stream, tensor)
    kept_normed, kept_rotated = kept

    lanes = all_rows
    turned = lax.optimization_barrier(kept_normed.T)
    turned = turned.reshape(sections, replicas, row_block, lanes).transpose(1, 0, 2, 3)
    turned = turned.reshape(replicas, sections * row_block, lanes)
    row_scales = jnp.repeat(scales, tok_rows, axis=0)
    level, slope = level_and_slope(kept_rotated, row_scales)
    error_part = level - kept_rotated
    grad_rot = (error_part * (slope - 1.0)).astype(jnp.bfloat16)
    grad_rot = grad_rot.reshape(all_rows, part_cols // lanes, lanes).transpose(1, 0, 2)
    sent = jnp.concatenate([turned, copies_of(grad_rot.reshape(-1, lanes), replicas)], axis=1)
    dp_pos = lax.axis_index("dp")

    def block(step):
        return lax.dynamic_index_in_dim(sent, lax.rem(dp_pos + step, replicas), 0, keepdims=False)

    parts = jnp.stack(
        [block(0)]
        + [
            lax.ppermute(block(k), "dp", [(i, (i + k) % replicas) for i in range(replicas)])
            for k in range(1, replicas)
        ]
    )
    mine, other = terms_of(core, parts, planes, row_block, part_cols)
    loss = jnp.full((8, 128), jnp.sum(error_part * error_part), jnp.float32)
    loss = loss + crossed(loss, 1)
    losses = exchange(copies_of(loss, replicas * tensor), ("dp", "tp"))
    loss = jnp.sum(losses[:, 0, 0])

    pair_sum = (mine + crossed(other, 1).astype(jnp.float32)).astype(jnp.bfloat16)
    high = lax.reduce_precision(loss, 8, 7)
    middle = lax.reduce_precision(loss - high, 8, 7)
    low = loss - high - middle
    lane = lax.broadcasted_iota(jnp.int32, (16, part_cols), 1)
    tail_rows = jnp.where(lane == 0, high, jnp.where(lane == 1, middle, jnp.where(lane == 2, low, 0.0)))
    tail_rows = tail_rows.astype(jnp.bfloat16)
    sent = jnp.concatenate([pair_sum, copies_of(tail_rows, planes)], axis=1)
    parts = lax.all_to_all(sent, "section", 0, 0, axis_index_groups=same_core, tiled=True)
    sums = jnp.sum(parts.astype(jnp.float32), axis=0)
    factor = 1.0 / math.sqrt(sections * all_rows * replicas)
    norm_count = all_rows * replicas * D
    return (sums[:row_block] * factor, jnp.sum(sums[row_block, :3]) / norm_count)


def solution(mesh):
    placed = (
        P(None, "dp", "tp"),
        P(("section", "dp"), "tp"),
        P("section", None, "tp"),
        P("section", None),
        P("section", "tp"),
    )
    return jax.shard_map(
        local,
        mesh=mesh,
        in_specs=placed,
        out_specs=(P(("section", "dp"), "tp"), P()),
        check_vma=False,
    )
```

```python
import functools
import math

import jax
import jax.numpy as jnp
from jax import lax
from jax.experimental import pallas as pl
from jax.experimental.pallas import tpu as pltpu
from jax.sharding import PartitionSpec as P

D = 4096
GROUP = 128
STAGE = 4

norm_eps = 1e-05
full_turn = 2.0 * math.pi

SIN_TERMS = (3.141592653536291, -5.167712764624543, 2.5501633189471025,
             -0.5992521978250058, 0.08205040181365181, -0.007028386419353805)
COS_TERMS = (0.9999999997799043, -4.934802137078827, 4.058709159556301,
             -1.3352120030506605, 0.23493731381815505, -0.024396324355626643)


def horner(terms, square):
    total = jnp.full_like(square, terms[-1])
    for term in terms[-2::-1]:
        total = total * square + term
    return total


def half_turn(ratio):
    part = ratio - jnp.round(ratio)
    square = part * part
    return part * horner(SIN_TERMS, square), horner(COS_TERMS, square)


def quantize(values, scale):
    ratio = values / scale
    sine, cosine = half_turn(ratio)
    return scale * jnp.clip(ratio - sine * cosine / math.pi, -8.0, 7.0)


def level_and_slope(values, scale):
    ratio = values / scale
    sine, cosine = half_turn(ratio)
    stair = ratio - sine * cosine / math.pi
    inside = (stair > -8.0) & (stair < 7.0)
    level = scale * jnp.clip(stair, -8.0, 7.0)
    return level, jnp.where(inside, 2.0 * sine * sine, 0.0)


def copies_of(value, count):
    return jnp.broadcast_to(value[None], (count,) + value.shape)


def exchange(copies, axis):
    return lax.all_to_all(copies, axis, 0, 0, tiled=True)


def gather(value, axis):
    return exchange(copies_of(value, lax.axis_size(axis)), axis)


def crossed(value, mask):
    return lax.ppermute(value, "section", [(i, i ^ mask) for i in range(lax.axis_size("section"))])


VMEM = pl.BlockSpec(memory_space=pltpu.VMEM)
SMEM = pl.BlockSpec(memory_space=pltpu.SMEM)
FAR = pl.BlockSpec(memory_space=pl.ANY)
PARAMS = pltpu.CompilerParams(vmem_limit_bytes=8 * 1024 * 1024)


def start_load(layer, place_ref, refs, into, sems):
    chunks = sems.shape[0]
    chunk = into.shape[0] // chunks
    plane, core = place_ref[0] // 2, place_ref[0] % 2
    own, by1, even_mine, even_other, odd_mine, odd_other = refs
    mine, other = (odd_mine, odd_other) if layer % 2 else (even_mine, even_other)
    here, same = plane == layer // 2, core == layer % 2
    away, differs = jnp.logical_not(here), jnp.logical_not(same)
    for wanted, source in (
        (here & same, own), (here & differs, by1), (away & same, mine), (away & differs, other)
    ):
        @pl.when(wanted)
        def _():
            for index in range(chunks):
                rows = pl.ds(index * chunk, chunk)
                pltpu.make_async_copy(source.at[rows], into.at[rows], sems.at[index]).start()


def project_from_kernel(layer, place_ref, *args):
    refs, (quant_ref, stream_ref, copies_ref, out_ref, weight_ref, sems) = args[:6], args[6:]
    start_load(layer, place_ref, refs, weight_ref, sems)
    count, tok_rows, part = quant_ref.shape
    total = stream_ref[...].astype(jnp.float32)
    for k in range(count):
        rows = pl.ds(k * part, part)
        pltpu.make_async_copy(refs[0].at[rows], weight_ref.at[rows], sems.at[k]).wait()
        total = total + jnp.dot(quant_ref[k], weight_ref[rows], preferred_element_type=jnp.float32)
    stream = total.astype(jnp.bfloat16)
    out_ref[...] = stream
    for k in range(count):
        copies_ref[k] = stream


def project_from(layer, place, sources, quant_rows, stream):
    own = sources[0]
    return pl.pallas_call(
        functools.partial(project_from_kernel, layer),
        out_shape=[
            jax.ShapeDtypeStruct(quant_rows.shape, jnp.bfloat16),
            jax.ShapeDtypeStruct(stream.shape, jnp.bfloat16),
        ],
        in_specs=[SMEM] + [FAR] * 6 + [VMEM] * 2,
        out_specs=[VMEM] * 2,
        scratch_shapes=[
            pltpu.VMEM(own.shape, own.dtype),
            pltpu.SemaphoreType.DMA((quant_rows.shape[0],)),
        ],
        compiler_params=PARAMS,
        name="project_from",
    )(place, *sources, quant_rows, stream)


def project_kernel(quant_ref, weight_ref, stream_ref, copies_ref, out_ref):
    count, tok_rows, part = quant_ref.shape
    total = stream_ref[...].astype(jnp.float32)
    for k in range(count):
        rows = pl.ds(k * part, part)
        total = total + jnp.dot(quant_ref[k], weight_ref[rows], preferred_element_type=jnp.float32)
    stream = total.astype(jnp.bfloat16)
    out_ref[...] = stream
    for k in range(count):
        copies_ref[k] = stream


def project(quant_rows, weight, stream):
    return pl.pallas_call(
        project_kernel,
        out_shape=[
            jax.ShapeDtypeStruct(quant_rows.shape, jnp.bfloat16),
            jax.ShapeDtypeStruct(stream.shape, jnp.bfloat16),
        ],
        in_specs=[VMEM] * 3,
        out_specs=[VMEM] * 2,
        compiler_params=PARAMS,
        name="project",
    )(quant_rows, weight, stream)


def rotate_kernel(layer, last, keep_ref, rows_ref, gain_ref, rot_ref, scale_ref, _, __, *rest):
    (kept_normed, kept_rotated), rest = rest[:2], rest[2:]
    copies, (normed_ref, rotated_ref, sems) = rest[:-3], rest[-3:]
    count, tok_rows, part = rows_ref.shape
    place = pl.ds(layer * tok_rows, tok_rows)
    keep = keep_ref[0] == 1
    keep_normed = pltpu.make_async_copy(normed_ref, kept_normed.at[place], sems.at[0])
    keep_rotated = pltpu.make_async_copy(rotated_ref, kept_rotated.at[place], sems.at[1])
    total = None
    for k in range(count):
        rows = rows_ref[k].astype(jnp.float32)
        square = jnp.sum(rows * rows, axis=-1, keepdims=True)
        total = square if total is None else total + square
    factor = lax.rsqrt(total / (count * part) + norm_eps)
    for k in range(count):
        cols = slice(k * part, (k + 1) * part)
        rows = rows_ref[k].astype(jnp.float32)
        normed_ref[:, cols] = (rows * factor * gain_ref[:, cols]).astype(jnp.bfloat16)
    pl.when(keep)(keep_normed.start)
    rotated = jnp.dot(normed_ref[...], rot_ref[...], preferred_element_type=jnp.float32)
    rotated_ref[...] = rotated
    pl.when(keep)(keep_rotated.start)
    if not last:
        quantized = quantize(rotated, scale_ref[...]).astype(jnp.bfloat16)
        for k in range(count):
            copies[0][k] = quantized

    @pl.when(keep)
    def _():
        keep_normed.wait()
        keep_rotated.wait()


def rotate(layer, last, keep, rows, gain, rot_cols, scale, kept):
    count, tok_rows, part = rows.shape
    shapes = [jax.ShapeDtypeStruct(k.shape, k.dtype) for k in kept]
    if not last:
        shapes.append(jax.ShapeDtypeStruct(rows.shape, jnp.bfloat16))
    return pl.pallas_call(
        functools.partial(rotate_kernel, layer, last),
        out_shape=shapes,
        in_specs=[SMEM] + [VMEM] * 4 + [FAR] * 2,
        out_specs=[FAR] * 2 + [VMEM] * (len(shapes) - 2),
        input_output_aliases={5: 0, 6: 1},
        scratch_shapes=[
            pltpu.VMEM((tok_rows, count * part), jnp.bfloat16),
            pltpu.VMEM((tok_rows, part), jnp.float32),
            pltpu.SemaphoreType.DMA((2,)),
        ],
        compiler_params=PARAMS,
        name="rotate",
    )(keep, rows, gain, rot_cols, scale, *kept)


def spread_kernel(stream_ref, copies_ref):
    for k in range(copies_ref.shape[0]):
        copies_ref[k] = stream_ref[...]


def spread(stream, count):
    return pl.pallas_call(
        spread_kernel,
        out_shape=jax.ShapeDtypeStruct((count,) + stream.shape, stream.dtype),
        in_specs=[VMEM],
        out_specs=VMEM,
        compiler_params=PARAMS,
        name="spread",
    )(stream)


def terms_kernel(part_rows, core_ref, parts_ref, mine_ref, other_ref):
    sources, rows, lanes = parts_ref.shape
    count, _, cols = mine_ref.shape
    features = 2 * count * part_rows
    left = jnp.concatenate([parts_ref[s, :features] for s in range(sources)], axis=1)
    right = jnp.concatenate(
        [
            jnp.concatenate([parts_ref[s, pl.ds(k, lanes)] for k in range(features, rows, lanes)], axis=1)
            for s in range(sources)
        ],
        axis=0,
    )
    terms = jnp.dot(left, right, preferred_element_type=jnp.float32)
    lower = core_ref[0] == 0
    for z in range(count):
        even = terms[2 * z * part_rows : (2 * z + 1) * part_rows]
        odd = terms[(2 * z + 1) * part_rows : (2 * z + 2) * part_rows]
        mine_ref[z] = jnp.where(lower, even, odd)
        other_ref[z] = jnp.where(lower, odd, even).astype(jnp.bfloat16)


def terms_of(core, parts, planes, row_block, part_cols):
    shape = (planes, row_block, part_cols)
    return pl.pallas_call(
        functools.partial(terms_kernel, row_block),
        out_shape=[jax.ShapeDtypeStruct(shape, jnp.float32), jax.ShapeDtypeStruct(shape, jnp.bfloat16)],
        in_specs=[pl.BlockSpec(memory_space=pltpu.SMEM), VMEM],
        out_specs=[VMEM, VMEM],
        compiler_params=pltpu.CompilerParams(vmem_limit_bytes=24 * 1024 * 1024),
        name="terms",
    )(core, parts)


def local(hidden_in, rotation, proj, norm_gain, quant_exp):
    sections = lax.axis_size("section")
    replicas = lax.axis_size("dp")
    tensor = lax.axis_size("tp")
    section_pos = lax.axis_index("section")
    micro_count, tok_rows, part_cols = hidden_in.shape
    stages = sections // STAGE
    planes = sections // 2
    stage_pos = section_pos // STAGE
    place = section_pos % STAGE
    core = section_pos % 2
    same_core = [[2 * z + c for z in range(planes)] for c in range(2)]
    row_block = rotation.shape[0]

    own = proj[0]
    by1 = crossed(own, 1)

    scale_row = jnp.repeat(jnp.exp2(quant_exp.astype(jnp.float32) * 0.25) * 0.125, GROUP, axis=1)
    params = jnp.concatenate([norm_gain, scale_row], axis=1)
    params_by1 = crossed(params, 1)
    params_by2 = crossed(jnp.concatenate([params, params_by1], axis=0), 2)
    own_now, _ = lax.optimization_barrier((own, params_by2))
    even_mine = lax.ppermute(own_now, "section", [(i, i ^ 2) for i in range(0, sections, 2)])
    found = jnp.concatenate([params, params_by1, params_by2], axis=0)
    params = jnp.stack([lax.dynamic_index_in_dim(found, place ^ k, 0, False) for k in range(STAGE)])
    gains, scales = params[:, :D], params[:, D:]

    along_z = lax.all_to_all(
        copies_of(rotation, planes), "section", 0, 0, axis_index_groups=same_core, tiled=True
    )
    along_z, by1 = lax.optimization_barrier((along_z, by1))
    along_x = gather(along_z, "dp")
    other_rows = crossed(along_x, 1)
    own_later, _ = lax.optimization_barrier((own, other_rows))
    odd_mine = lax.ppermute(own_later, "section", [(i, i ^ 2) for i in range(1, sections, 2)])
    even_rows = jnp.where(core == 0, along_x, other_rows)
    odd_rows = jnp.where(core == 0, other_rows, along_x)
    rot_cols = jnp.stack([even_rows, odd_rows]).transpose(2, 0, 1, 3, 4).reshape(D, part_cols)

    where = place[None].astype(jnp.int32)
    all_rows = STAGE * tok_rows
    stream = lax.dynamic_index_in_dim(hidden_in, place, 0, keepdims=False)
    copies = spread(stream, tensor)
    kept = (jnp.zeros((all_rows, D), jnp.bfloat16), jnp.zeros((all_rows, part_cols), jnp.float32))
    weights = []
    keeps = [jnp.full((1,), 1, jnp.int32)]
    keeps += [(stage_pos == stage).astype(jnp.int32)[None] for stage in range(1, stages)]
    row_scales = jnp.repeat(scales, tok_rows, axis=0)
    partners = [lax.rem(lax.axis_index("dp") + step, replicas) for step in range(replicas)]
    which = core[None].astype(jnp.int32)
    ahead = (keeps, row_scales, partners, which)
    for stage in range(stages):
        keep = keeps[stage]
        for layer in range(STAGE):
            last = stage == stages - 1 and layer == STAGE - 1
            gain, scale = gains[layer : layer + 1], scales[layer : layer + 1]
            rows = exchange(copies, "tp")
            if stage == 0 and layer > 0 or stage == 1 and layer == 0:
                done = (layer - 1) % STAGE
                mine, other = sources[4:] if done % 2 else sources[2:4]
                weight = jnp.where(core == done % 2, mine, other)
                near = jnp.where(core == done % 2, own, by1)
                weight = jnp.where(place // 2 == done // 2, near, weight)
                rows, weight, ahead = lax.optimization_barrier((rows, weight, ahead))
                keeps, row_scales, partners, which = ahead
                weights.append(weight)
            results = rotate(layer, last, keep, rows, gain, rot_cols, scale, kept)
            kept = results[:2]
            if last:
                break
            quant = results[2]
            if stage == 0 and layer == 0:
                even_mine, _ = lax.optimization_barrier((even_mine, quant))
                even_other = lax.ppermute(even_mine, "section", [(i, i + 1) for i in range(0, sections, 2)])
                sources = (own, by1, even_mine, even_other, even_mine, even_other)
            if stage == 0 and layer == 1:
                odd_mine, _ = lax.optimization_barrier((odd_mine, quant))
                odd_other = lax.ppermute(odd_mine, "section", [(i + 1, i) for i in range(0, sections, 2)])
                sources = (own, by1, even_mine, even_other, odd_mine, odd_other)
            quant_rows = exchange(quant, "tp")
            if stage == 0:
                copies, stream = project_from(layer, where, sources, quant_rows, stream)
            else:
                copies, stream = project(quant_rows, weights[layer], stream)
        if stage < stages - 1:
            stream = lax.ppermute(
                stream, "section", [(i, i + STAGE) for i in range(sections - STAGE)]
            )
            copies = spread(stream, tensor)
    kept_normed, kept_rotated = kept

    lanes = all_rows
    turned = lax.optimization_barrier(kept_normed.T)
    turned = turned.reshape(sections, replicas, row_block, lanes).transpose(1, 0, 2, 3)
    turned = turned.reshape(replicas, sections * row_block, lanes)
    level, slope = level_and_slope(kept_rotated, row_scales)
    error_part = level - kept_rotated
    grad_rot = (error_part * (slope - 1.0)).astype(jnp.bfloat16)
    grad_rot = grad_rot.reshape(all_rows, part_cols // lanes, lanes).transpose(1, 0, 2)
    sent = jnp.concatenate([turned, copies_of(grad_rot.reshape(-1, lanes), replicas)], axis=1)

    def block(step):
        return lax.dynamic_index_in_dim(sent, partners[step], 0, keepdims=False)

    parts = jnp.stack(
        [block(0)]
        + [
            lax.ppermute(block(k), "dp", [(i, (i + k) % replicas) for i in range(replicas)])
            for k in range(1, replicas)
        ]
    )
    mine, other = terms_of(which, parts, planes, row_block, part_cols)
    loss = jnp.full((8, 128), jnp.sum(error_part * error_part), jnp.float32)
    loss = jnp.sum(exchange(copies_of(loss, replicas * tensor), ("dp", "tp")), axis=0)
    loss = loss + crossed(loss, 1)
    loss = jnp.concatenate([loss, loss], axis=0)
    high = lax.reduce_precision(loss, 8, 7)
    middle = lax.reduce_precision(loss - high, 8, 7)
    low = loss - high - middle
    lane = lax.broadcasted_iota(jnp.int32, loss.shape, 1)
    tail_rows = jnp.where(lane == 0, high, jnp.where(lane == 1, middle, jnp.where(lane == 2, low, 0.0)))
    tail_rows = jnp.tile(tail_rows.astype(jnp.bfloat16), (1, part_cols // lanes))

    pair_sum = (mine + crossed(other, 1).astype(jnp.float32)).astype(jnp.bfloat16)
    sent = jnp.concatenate([pair_sum, copies_of(tail_rows, planes)], axis=1)
    parts = lax.all_to_all(sent, "section", 0, 0, axis_index_groups=same_core, tiled=True)
    sums = jnp.sum(parts.astype(jnp.float32), axis=0)
    factor = 1.0 / math.sqrt(sections * all_rows * replicas)
    norm_count = all_rows * replicas * D
    return (sums[:row_block] * factor, jnp.sum(sums[row_block, :3]) / norm_count)


def solution(mesh):
    placed = (
        P(None, "dp", "tp"),
        P(("section", "dp"), "tp"),
        P("section", None, "tp"),
        P("section", None),
        P("section", "tp"),
    )
    return jax.shard_map(
        local,
        mesh=mesh,
        in_specs=placed,
        out_specs=(P(("section", "dp"), "tp"), P()),
        check_vma=False,
    )
```

```python
import functools
import math

import jax
import jax.numpy as jnp
from jax import lax
from jax.experimental import pallas as pl
from jax.experimental.pallas import tpu as pltpu
from jax.sharding import PartitionSpec as P

D = 4096
GROUP = 128
STAGE = 4

norm_eps = 1e-05
full_turn = 2.0 * math.pi

SIN_TERMS = (3.141592653536291, -5.167712764624543, 2.5501633189471025,
             -0.5992521978250058, 0.08205040181365181, -0.007028386419353805)
COS_TERMS = (0.9999999997799043, -4.934802137078827, 4.058709159556301,
             -1.3352120030506605, 0.23493731381815505, -0.024396324355626643)


def horner(terms, square):
    total = jnp.full_like(square, terms[-1])
    for term in terms[-2::-1]:
        total = total * square + term
    return total


def half_turn(ratio):
    part = ratio - jnp.round(ratio)
    square = part * part
    return part * horner(SIN_TERMS, square), horner(COS_TERMS, square)


def quantize(values, scale):
    ratio = values / scale
    sine, cosine = half_turn(ratio)
    return scale * jnp.clip(ratio - sine * cosine / math.pi, -8.0, 7.0)


def level_and_slope(values, scale):
    ratio = values / scale
    sine, cosine = half_turn(ratio)
    stair = ratio - sine * cosine / math.pi
    inside = (stair > -8.0) & (stair < 7.0)
    level = scale * jnp.clip(stair, -8.0, 7.0)
    return level, jnp.where(inside, 2.0 * sine * sine, 0.0)


def copies_of(value, count):
    return jnp.broadcast_to(value[None], (count,) + value.shape)


def exchange(copies, axis):
    return lax.all_to_all(copies, axis, 0, 0, tiled=True)


def gather(value, axis):
    return exchange(copies_of(value, lax.axis_size(axis)), axis)


def crossed(value, mask):
    return lax.ppermute(value, "section", [(i, i ^ mask) for i in range(lax.axis_size("section"))])


VMEM = pl.BlockSpec(memory_space=pltpu.VMEM)
SMEM = pl.BlockSpec(memory_space=pltpu.SMEM)
FAR = pl.BlockSpec(memory_space=pl.ANY)
PARAMS = pltpu.CompilerParams(vmem_limit_bytes=8 * 1024 * 1024)


def start_load(layer, place_ref, refs, into, sems):
    chunks = sems.shape[0]
    chunk = into.shape[0] // chunks
    plane, core = place_ref[0] // 2, place_ref[0] % 2
    own, by1, even_mine, even_other, odd_mine, odd_other = refs
    mine, other = (odd_mine, odd_other) if layer % 2 else (even_mine, even_other)
    here, same = plane == layer // 2, core == layer % 2
    away, differs = jnp.logical_not(here), jnp.logical_not(same)
    for wanted, source in (
        (here & same, own), (here & differs, by1), (away & same, mine), (away & differs, other)
    ):
        @pl.when(wanted)
        def _():
            for index in range(chunks):
                rows = pl.ds(index * chunk, chunk)
                pltpu.make_async_copy(source.at[rows], into.at[rows], sems.at[index]).start()


def project_from_kernel(layer, place_ref, *args):
    refs, (quant_ref, stream_ref, copies_ref, out_ref, weight_ref, sems) = args[:6], args[6:]
    start_load(layer, place_ref, refs, weight_ref, sems)
    count, tok_rows, part = quant_ref.shape
    total = stream_ref[...].astype(jnp.float32)
    for k in range(count):
        rows = pl.ds(k * part, part)
        pltpu.make_async_copy(refs[0].at[rows], weight_ref.at[rows], sems.at[k]).wait()
        total = total + jnp.dot(quant_ref[k], weight_ref[rows], preferred_element_type=jnp.float32)
    stream = total.astype(jnp.bfloat16)
    out_ref[...] = stream
    for k in range(count):
        copies_ref[k] = stream


def project_from(layer, place, sources, quant_rows, stream):
    own = sources[0]
    return pl.pallas_call(
        functools.partial(project_from_kernel, layer),
        out_shape=[
            jax.ShapeDtypeStruct(quant_rows.shape, jnp.bfloat16),
            jax.ShapeDtypeStruct(stream.shape, jnp.bfloat16),
        ],
        in_specs=[SMEM] + [FAR] * 6 + [VMEM] * 2,
        out_specs=[VMEM] * 2,
        scratch_shapes=[
            pltpu.VMEM(own.shape, own.dtype),
            pltpu.SemaphoreType.DMA((quant_rows.shape[0],)),
        ],
        compiler_params=PARAMS,
        name="project_from",
    )(place, *sources, quant_rows, stream)


def project_kernel(quant_ref, weight_ref, stream_ref, copies_ref, out_ref):
    count, tok_rows, part = quant_ref.shape
    total = stream_ref[...].astype(jnp.float32)
    for k in range(count):
        rows = pl.ds(k * part, part)
        total = total + jnp.dot(quant_ref[k], weight_ref[rows], preferred_element_type=jnp.float32)
    stream = total.astype(jnp.bfloat16)
    out_ref[...] = stream
    for k in range(count):
        copies_ref[k] = stream


def project(quant_rows, weight, stream):
    return pl.pallas_call(
        project_kernel,
        out_shape=[
            jax.ShapeDtypeStruct(quant_rows.shape, jnp.bfloat16),
            jax.ShapeDtypeStruct(stream.shape, jnp.bfloat16),
        ],
        in_specs=[VMEM] * 3,
        out_specs=[VMEM] * 2,
        compiler_params=PARAMS,
        name="project",
    )(quant_rows, weight, stream)


def rotate_kernel(layer, last, keep_ref, rows_ref, gain_ref, rot_ref, scale_ref, _, __, *rest):
    (kept_normed, kept_rotated), rest = rest[:2], rest[2:]
    copies, (normed_ref, rotated_ref, sems) = rest[:-3], rest[-3:]
    count, tok_rows, part = rows_ref.shape
    place = pl.ds(layer * tok_rows, tok_rows)
    keep = keep_ref[0] == 1
    keep_normed = pltpu.make_async_copy(normed_ref, kept_normed.at[place], sems.at[0])
    keep_rotated = pltpu.make_async_copy(rotated_ref, kept_rotated.at[place], sems.at[1])
    total = None
    for k in range(count):
        rows = rows_ref[k].astype(jnp.float32)
        square = jnp.sum(rows * rows, axis=-1, keepdims=True)
        total = square if total is None else total + square
    factor = lax.rsqrt(total / (count * part) + norm_eps)
    for k in range(count):
        cols = slice(k * part, (k + 1) * part)
        rows = rows_ref[k].astype(jnp.float32)
        normed_ref[:, cols] = (rows * factor * gain_ref[:, cols]).astype(jnp.bfloat16)
    pl.when(keep)(keep_normed.start)
    rotated = jnp.dot(normed_ref[...], rot_ref[...], preferred_element_type=jnp.float32)
    rotated_ref[...] = rotated
    pl.when(keep)(keep_rotated.start)
    if not last:
        quantized = quantize(rotated, scale_ref[...]).astype(jnp.bfloat16)
        for k in range(count):
            copies[0][k] = quantized

    @pl.when(keep)
    def _():
        keep_normed.wait()
        keep_rotated.wait()


def rotate(layer, last, keep, rows, gain, rot_cols, scale, kept):
    count, tok_rows, part = rows.shape
    shapes = [jax.ShapeDtypeStruct(k.shape, k.dtype) for k in kept]
    if not last:
        shapes.append(jax.ShapeDtypeStruct(rows.shape, jnp.bfloat16))
    return pl.pallas_call(
        functools.partial(rotate_kernel, layer, last),
        out_shape=shapes,
        in_specs=[SMEM] + [VMEM] * 4 + [FAR] * 2,
        out_specs=[FAR] * 2 + [VMEM] * (len(shapes) - 2),
        input_output_aliases={5: 0, 6: 1},
        scratch_shapes=[
            pltpu.VMEM((tok_rows, count * part), jnp.bfloat16),
            pltpu.VMEM((tok_rows, part), jnp.float32),
            pltpu.SemaphoreType.DMA((2,)),
        ],
        compiler_params=PARAMS,
        name="rotate",
    )(keep, rows, gain, rot_cols, scale, *kept)


def spread_kernel(stream_ref, copies_ref):
    for k in range(copies_ref.shape[0]):
        copies_ref[k] = stream_ref[...]


def spread(stream, count):
    return pl.pallas_call(
        spread_kernel,
        out_shape=jax.ShapeDtypeStruct((count,) + stream.shape, stream.dtype),
        in_specs=[VMEM],
        out_specs=VMEM,
        compiler_params=PARAMS,
        name="spread",
    )(stream)


def terms_kernel(part_rows, core_ref, parts_ref, mine_ref, other_ref):
    sources, rows, lanes = parts_ref.shape
    count, _, cols = mine_ref.shape
    features = 2 * count * part_rows
    left = jnp.concatenate([parts_ref[s, :features] for s in range(sources)], axis=1)
    right = jnp.concatenate(
        [
            jnp.concatenate([parts_ref[s, pl.ds(k, lanes)] for k in range(features, rows, lanes)], axis=1)
            for s in range(sources)
        ],
        axis=0,
    )
    terms = jnp.dot(left, right, preferred_element_type=jnp.float32)
    lower = core_ref[0] == 0
    for z in range(count):
        even = terms[2 * z * part_rows : (2 * z + 1) * part_rows]
        odd = terms[(2 * z + 1) * part_rows : (2 * z + 2) * part_rows]
        mine_ref[z] = jnp.where(lower, even, odd)
        other_ref[z] = jnp.where(lower, odd, even).astype(jnp.bfloat16)


def terms_of(core, parts, planes, row_block, part_cols):
    shape = (planes, row_block, part_cols)
    return pl.pallas_call(
        functools.partial(terms_kernel, row_block),
        out_shape=[jax.ShapeDtypeStruct(shape, jnp.float32), jax.ShapeDtypeStruct(shape, jnp.bfloat16)],
        in_specs=[pl.BlockSpec(memory_space=pltpu.SMEM), VMEM],
        out_specs=[VMEM, VMEM],
        compiler_params=pltpu.CompilerParams(vmem_limit_bytes=24 * 1024 * 1024),
        name="terms",
    )(core, parts)


def local(hidden_in, rotation, proj, norm_gain, quant_exp):
    sections = lax.axis_size("section")
    replicas = lax.axis_size("dp")
    tensor = lax.axis_size("tp")
    section_pos = lax.axis_index("section")
    micro_count, tok_rows, part_cols = hidden_in.shape
    stages = sections // STAGE
    planes = sections // 2
    stage_pos = section_pos // STAGE
    place = section_pos % STAGE
    core = section_pos % 2
    same_core = [[2 * z + c for z in range(planes)] for c in range(2)]
    row_block = rotation.shape[0]

    own = proj[0]
    by1 = crossed(own, 1)

    scale_row = jnp.repeat(jnp.exp2(quant_exp.astype(jnp.float32) * 0.25) * 0.125, GROUP, axis=1)
    params = jnp.concatenate([norm_gain, scale_row], axis=1)
    params_by1 = crossed(params, 1)
    params_by2 = crossed(params, 2)
    along_z = lax.all_to_all(
        copies_of(rotation, planes), "section", 0, 0, axis_index_groups=same_core, tiled=True
    )
    along_z, by1, params_by2 = lax.optimization_barrier((along_z, by1, params_by2))
    params_by3 = crossed(params_by2, 1)
    own_now, _ = lax.optimization_barrier((own, params_by2))
    even_mine = lax.ppermute(own_now, "section", [(i, i ^ 2) for i in range(0, sections, 2)])
    found = jnp.concatenate([params, params_by1, params_by2, params_by3], axis=0)
    params = jnp.stack([lax.dynamic_index_in_dim(found, place ^ k, 0, False) for k in range(STAGE)])
    gains, scales = params[:, :D], params[:, D:]

    along_x = gather(along_z, "dp")
    other_rows = crossed(along_x, 1)
    own_later, _ = lax.optimization_barrier((own, other_rows))
    odd_mine = lax.ppermute(own_later, "section", [(i, i ^ 2) for i in range(1, sections, 2)])
    even_rows = jnp.where(core == 0, along_x, other_rows)
    odd_rows = jnp.where(core == 0, other_rows, along_x)
    rot_cols = jnp.stack([even_rows, odd_rows]).transpose(2, 0, 1, 3, 4).reshape(D, part_cols)

    where = place[None].astype(jnp.int32)
    all_rows = STAGE * tok_rows
    stream = lax.dynamic_index_in_dim(hidden_in, place, 0, keepdims=False)
    copies = spread(stream, tensor)
    kept = (jnp.zeros((all_rows, D), jnp.bfloat16), jnp.zeros((all_rows, part_cols), jnp.float32))
    weights = []
    keeps = [jnp.full((1,), 1, jnp.int32)]
    keeps += [(stage_pos == stage).astype(jnp.int32)[None] for stage in range(1, stages)]
    row_scales = jnp.repeat(scales, tok_rows, axis=0)
    dp_pos = lax.axis_index("dp").astype(jnp.uint32)
    partners = [lax.rem(dp_pos + jnp.uint32(step), jnp.uint32(replicas)) for step in range(replicas)]
    which = core[None].astype(jnp.int32)
    ahead = (keeps, row_scales, partners, which)
    for stage in range(stages):
        keep = keeps[stage]
        for layer in range(STAGE):
            last = stage == stages - 1 and layer == STAGE - 1
            gain, scale = gains[layer : layer + 1], scales[layer : layer + 1]
            rows = exchange(copies, "tp")
            if stage == 0 and layer in (1, 2):
                odd = layer - 1
                mine, other = sources[4:] if odd else sources[2:4]
                far = jnp.where(core == odd, mine, other)
                near = jnp.where(core == odd, own, by1)
                pair = jnp.where(place // 2 == 0, near, far), jnp.where(place // 2 == 0, far, near)
                rows, pair, ahead = lax.optimization_barrier((rows, pair, ahead))
                weights.append(pair)
                keeps, row_scales, partners, which = ahead
            results = rotate(layer, last, keep, rows, gain, rot_cols, scale, kept)
            kept = results[:2]
            if last:
                break
            quant = results[2]
            if stage == 0 and layer == 0:
                even_mine, _ = lax.optimization_barrier((even_mine, quant))
                even_other = lax.ppermute(even_mine, "section", [(i, i + 1) for i in range(0, sections, 2)])
                sources = (own, by1, even_mine, even_other, even_mine, even_other)
            if stage == 0 and layer == 1:
                odd_mine, _ = lax.optimization_barrier((odd_mine, quant))
                odd_other = lax.ppermute(odd_mine, "section", [(i + 1, i) for i in range(0, sections, 2)])
                sources = (own, by1, even_mine, even_other, odd_mine, odd_other)
            quant_rows = exchange(quant, "tp")
            if stage == 0 and layer < 2:
                copies, stream = project_from(layer, where, sources, quant_rows, stream)
            else:
                copies, stream = project(quant_rows, weights[layer % 2][layer // 2], stream)
        if stage < stages - 1:
            stream = lax.ppermute(
                stream, "section", [(i, i + STAGE) for i in range(sections - STAGE)]
            )
            copies = spread(stream, tensor)
    kept_normed, kept_rotated = kept

    lanes = all_rows
    turned = lax.optimization_barrier(kept_normed.T)
    turned = turned.reshape(sections, replicas, row_block, lanes).transpose(1, 0, 2, 3)
    turned = turned.reshape(replicas, sections * row_block, lanes)
    level, slope = level_and_slope(kept_rotated, row_scales)
    error_part = level - kept_rotated
    grad_rot = (error_part * (slope - 1.0)).astype(jnp.bfloat16)
    grad_rot = grad_rot.reshape(all_rows, part_cols // lanes, lanes).transpose(1, 0, 2)
    sent = jnp.concatenate([turned, copies_of(grad_rot.reshape(-1, lanes), replicas)], axis=1)

    def block(step):
        return lax.dynamic_index_in_dim(sent, partners[step], 0, keepdims=False)

    parts = jnp.stack(
        [block(0)]
        + [
            lax.ppermute(block(k), "dp", [(i, (i + k) % replicas) for i in range(replicas)])
            for k in range(1, replicas)
        ]
    )
    mine, other = terms_of(which, parts, planes, row_block, part_cols)
    loss = jnp.full((8, 128), jnp.sum(error_part * error_part), jnp.float32)
    loss = jnp.sum(exchange(copies_of(loss, replicas * tensor), ("dp", "tp")), axis=0)
    loss = loss + crossed(loss, 1)
    loss = jnp.concatenate([loss, loss], axis=0)
    high = lax.reduce_precision(loss, 8, 7)
    middle = lax.reduce_precision(loss - high, 8, 7)
    low = loss - high - middle
    lane = lax.broadcasted_iota(jnp.int32, loss.shape, 1)
    tail_rows = jnp.where(lane == 0, high, jnp.where(lane == 1, middle, jnp.where(lane == 2, low, 0.0)))
    tail_rows = jnp.tile(tail_rows.astype(jnp.bfloat16), (1, part_cols // lanes))

    pair_sum = (mine + crossed(other, 1).astype(jnp.float32)).astype(jnp.bfloat16)
    sent = jnp.concatenate([pair_sum, copies_of(tail_rows, planes)], axis=1)
    parts = lax.all_to_all(sent, "section", 0, 0, axis_index_groups=same_core, tiled=True)
    sums = jnp.sum(parts.astype(jnp.float32), axis=0)
    factor = 1.0 / math.sqrt(sections * all_rows * replicas)
    norm_count = all_rows * replicas * D
    return (sums[:row_block] * factor, jnp.sum(sums[row_block, :3]) / norm_count)


def solution(mesh):
    placed = (
        P(None, "dp", "tp"),
        P(("section", "dp"), "tp"),
        P("section", None, "tp"),
        P("section", None),
        P("section", "tp"),
    )
    return jax.shard_map(
        local,
        mesh=mesh,
        in_specs=placed,
        out_specs=(P(("section", "dp"), "tp"), P()),
        check_vma=False,
    )
```

```python
import functools
import math

import jax
import jax.numpy as jnp
from jax import lax
from jax.experimental import pallas as pl
from jax.experimental.pallas import tpu as pltpu
from jax.sharding import PartitionSpec as P

D = 4096
GROUP = 128
STAGE = 4

norm_eps = 1e-05
full_turn = 2.0 * math.pi

SIN_TERMS = (3.141592653536291, -5.167712764624543, 2.5501633189471025,
             -0.5992521978250058, 0.08205040181365181, -0.007028386419353805)
COS_TERMS = (0.9999999997799043, -4.934802137078827, 4.058709159556301,
             -1.3352120030506605, 0.23493731381815505, -0.024396324355626643)


def horner(terms, square):
    total = jnp.full_like(square, terms[-1])
    for term in terms[-2::-1]:
        total = total * square + term
    return total


def half_turn(ratio):
    part = ratio - jnp.round(ratio)
    square = part * part
    return part * horner(SIN_TERMS, square), horner(COS_TERMS, square)


def quantize(values, scale):
    ratio = values / scale
    sine, cosine = half_turn(ratio)
    return scale * jnp.clip(ratio - sine * cosine / math.pi, -8.0, 7.0)


def level_and_slope(values, scale):
    ratio = values / scale
    sine, cosine = half_turn(ratio)
    stair = ratio - sine * cosine / math.pi
    inside = (stair > -8.0) & (stair < 7.0)
    level = scale * jnp.clip(stair, -8.0, 7.0)
    return level, jnp.where(inside, 2.0 * sine * sine, 0.0)


def copies_of(value, count):
    return jnp.broadcast_to(value[None], (count,) + value.shape)


def exchange(copies, axis):
    return lax.all_to_all(copies, axis, 0, 0, tiled=True)


def gather(value, axis):
    return exchange(copies_of(value, lax.axis_size(axis)), axis)


def crossed(value, mask):
    return lax.ppermute(value, "section", [(i, i ^ mask) for i in range(lax.axis_size("section"))])


VMEM = pl.BlockSpec(memory_space=pltpu.VMEM)
SMEM = pl.BlockSpec(memory_space=pltpu.SMEM)
FAR = pl.BlockSpec(memory_space=pl.ANY)
PARAMS = pltpu.CompilerParams(vmem_limit_bytes=8 * 1024 * 1024)


def start_load(layer, place_ref, refs, into, sems):
    chunks = sems.shape[0]
    chunk = into.shape[0] // chunks
    plane, core = place_ref[0] // 2, place_ref[0] % 2
    own, by1, even_mine, even_other, odd_mine, odd_other = refs
    mine, other = (odd_mine, odd_other) if layer % 2 else (even_mine, even_other)
    here, same = plane == layer // 2, core == layer % 2
    away, differs = jnp.logical_not(here), jnp.logical_not(same)
    for wanted, source in (
        (here & same, own), (here & differs, by1), (away & same, mine), (away & differs, other)
    ):
        @pl.when(wanted)
        def _():
            for index in range(chunks):
                rows = pl.ds(index * chunk, chunk)
                pltpu.make_async_copy(source.at[rows], into.at[rows], sems.at[index]).start()


def project_from_kernel(layer, place_ref, *args):
    refs, (quant_ref, stream_ref, copies_ref, out_ref, weight_ref, sems) = args[:6], args[6:]
    start_load(layer, place_ref, refs, weight_ref, sems)
    count, tok_rows, part = quant_ref.shape
    total = stream_ref[...].astype(jnp.float32)
    for k in range(count):
        rows = pl.ds(k * part, part)
        pltpu.make_async_copy(refs[0].at[rows], weight_ref.at[rows], sems.at[k]).wait()
        total = total + jnp.dot(quant_ref[k], weight_ref[rows], preferred_element_type=jnp.float32)
    stream = total.astype(jnp.bfloat16)
    out_ref[...] = stream
    for k in range(count):
        copies_ref[k] = stream


def project_from(layer, place, sources, quant_rows, stream):
    own = sources[0]
    return pl.pallas_call(
        functools.partial(project_from_kernel, layer),
        out_shape=[
            jax.ShapeDtypeStruct(quant_rows.shape, jnp.bfloat16),
            jax.ShapeDtypeStruct(stream.shape, jnp.bfloat16),
        ],
        in_specs=[SMEM] + [FAR] * 6 + [VMEM] * 2,
        out_specs=[VMEM] * 2,
        scratch_shapes=[
            pltpu.VMEM(own.shape, own.dtype),
            pltpu.SemaphoreType.DMA((quant_rows.shape[0],)),
        ],
        compiler_params=PARAMS,
        name="project_from",
    )(place, *sources, quant_rows, stream)


def project_kernel(quant_ref, weight_ref, stream_ref, copies_ref, out_ref):
    count, tok_rows, part = quant_ref.shape
    total = stream_ref[...].astype(jnp.float32)
    for k in range(count):
        rows = pl.ds(k * part, part)
        total = total + jnp.dot(quant_ref[k], weight_ref[rows], preferred_element_type=jnp.float32)
    stream = total.astype(jnp.bfloat16)
    out_ref[...] = stream
    for k in range(count):
        copies_ref[k] = stream


def project(quant_rows, weight, stream):
    return pl.pallas_call(
        project_kernel,
        out_shape=[
            jax.ShapeDtypeStruct(quant_rows.shape, jnp.bfloat16),
            jax.ShapeDtypeStruct(stream.shape, jnp.bfloat16),
        ],
        in_specs=[VMEM] * 3,
        out_specs=[VMEM] * 2,
        compiler_params=PARAMS,
        name="project",
    )(quant_rows, weight, stream)


def rotate_kernel(layer, last, keep_ref, rows_ref, gain_ref, rot_ref, scale_ref, _, __, *rest):
    (kept_normed, kept_rotated), rest = rest[:2], rest[2:]
    copies, (normed_ref, rotated_ref, sems) = rest[:-3], rest[-3:]
    count, tok_rows, part = rows_ref.shape
    place = pl.ds(layer * tok_rows, tok_rows)
    keep = keep_ref[0] == 1
    keep_normed = pltpu.make_async_copy(normed_ref, kept_normed.at[place], sems.at[0])
    keep_rotated = pltpu.make_async_copy(rotated_ref, kept_rotated.at[place], sems.at[1])
    total = None
    for k in range(count):
        rows = rows_ref[k].astype(jnp.float32)
        square = jnp.sum(rows * rows, axis=-1, keepdims=True)
        total = square if total is None else total + square
    factor = lax.rsqrt(total / (count * part) + norm_eps)
    for k in range(count):
        cols = slice(k * part, (k + 1) * part)
        rows = rows_ref[k].astype(jnp.float32)
        normed_ref[:, cols] = (rows * factor * gain_ref[:, cols]).astype(jnp.bfloat16)
    pl.when(keep)(keep_normed.start)
    rotated = jnp.dot(normed_ref[...], rot_ref[...], preferred_element_type=jnp.float32)
    rotated_ref[...] = rotated
    pl.when(keep)(keep_rotated.start)
    if not last:
        quantized = quantize(rotated, scale_ref[...]).astype(jnp.bfloat16)
        for k in range(count):
            copies[0][k] = quantized

    @pl.when(keep)
    def _():
        keep_normed.wait()
        keep_rotated.wait()


def rotate(layer, last, keep, rows, gain, rot_cols, scale, kept):
    count, tok_rows, part = rows.shape
    shapes = [jax.ShapeDtypeStruct(k.shape, k.dtype) for k in kept]
    if not last:
        shapes.append(jax.ShapeDtypeStruct(rows.shape, jnp.bfloat16))
    return pl.pallas_call(
        functools.partial(rotate_kernel, layer, last),
        out_shape=shapes,
        in_specs=[SMEM] + [VMEM] * 4 + [FAR] * 2,
        out_specs=[FAR] * 2 + [VMEM] * (len(shapes) - 2),
        input_output_aliases={5: 0, 6: 1},
        scratch_shapes=[
            pltpu.VMEM((tok_rows, count * part), jnp.bfloat16),
            pltpu.VMEM((tok_rows, part), jnp.float32),
            pltpu.SemaphoreType.DMA((2,)),
        ],
        compiler_params=PARAMS,
        name="rotate",
    )(keep, rows, gain, rot_cols, scale, *kept)


def spread_kernel(stream_ref, copies_ref):
    for k in range(copies_ref.shape[0]):
        copies_ref[k] = stream_ref[...]


def spread(stream, count):
    return pl.pallas_call(
        spread_kernel,
        out_shape=jax.ShapeDtypeStruct((count,) + stream.shape, stream.dtype),
        in_specs=[VMEM],
        out_specs=VMEM,
        compiler_params=PARAMS,
        name="spread",
    )(stream)


def terms_kernel(part_rows, core_ref, parts_ref, mine_ref, other_ref):
    sources, rows, lanes = parts_ref.shape
    count, _, cols = mine_ref.shape
    features = 2 * count * part_rows
    left = jnp.concatenate([parts_ref[s, :features] for s in range(sources)], axis=1)
    right = jnp.concatenate(
        [
            jnp.concatenate([parts_ref[s, pl.ds(k, lanes)] for k in range(features, rows, lanes)], axis=1)
            for s in range(sources)
        ],
        axis=0,
    )
    terms = jnp.dot(left, right, preferred_element_type=jnp.float32)
    lower = core_ref[0] == 0
    for z in range(count):
        even = terms[2 * z * part_rows : (2 * z + 1) * part_rows]
        odd = terms[(2 * z + 1) * part_rows : (2 * z + 2) * part_rows]
        mine_ref[z] = jnp.where(lower, even, odd)
        other_ref[z] = jnp.where(lower, odd, even).astype(jnp.bfloat16)


def terms_of(core, parts, planes, row_block, part_cols):
    shape = (planes, row_block, part_cols)
    return pl.pallas_call(
        functools.partial(terms_kernel, row_block),
        out_shape=[jax.ShapeDtypeStruct(shape, jnp.float32), jax.ShapeDtypeStruct(shape, jnp.bfloat16)],
        in_specs=[pl.BlockSpec(memory_space=pltpu.SMEM), VMEM],
        out_specs=[VMEM, VMEM],
        compiler_params=pltpu.CompilerParams(vmem_limit_bytes=24 * 1024 * 1024),
        name="terms",
    )(core, parts)


def local(hidden_in, rotation, proj, norm_gain, quant_exp):
    sections = lax.axis_size("section")
    replicas = lax.axis_size("dp")
    tensor = lax.axis_size("tp")
    section_pos = lax.axis_index("section")
    micro_count, tok_rows, part_cols = hidden_in.shape
    stages = sections // STAGE
    planes = sections // 2
    stage_pos = section_pos // STAGE
    place = section_pos % STAGE
    core = section_pos % 2
    same_core = [[2 * z + c for z in range(planes)] for c in range(2)]
    row_block = rotation.shape[0]

    own = proj[0]
    by1 = crossed(own, 1)

    scale_row = jnp.repeat(jnp.exp2(quant_exp.astype(jnp.float32) * 0.25) * 0.125, GROUP, axis=1)
    params = jnp.concatenate([norm_gain, scale_row], axis=1)
    params_by1 = crossed(params, 1)
    params_by2 = crossed(params, 2)
    along_z = lax.all_to_all(
        copies_of(rotation, planes), "section", 0, 0, axis_index_groups=same_core, tiled=True
    )
    along_z, by1, params_by2 = lax.optimization_barrier((along_z, by1, params_by2))
    params_by3 = crossed(params_by2, 1)
    own_now, _ = lax.optimization_barrier((own, params_by2))
    even_mine = lax.ppermute(own_now, "section", [(i, i ^ 2) for i in range(0, sections, 2)])
    found = jnp.concatenate([params, params_by1, params_by2, params_by3], axis=0)
    params = jnp.stack([lax.dynamic_index_in_dim(found, place ^ k, 0, False) for k in range(STAGE)])
    gains, scales = params[:, :D], params[:, D:]

    along_x = gather(along_z, "dp")
    stream = lax.dynamic_index_in_dim(hidden_in, place, 0, keepdims=False)
    copies = spread(stream, tensor)
    along_x, gains, scales, stream, copies = lax.optimization_barrier((along_x, gains, scales, stream, copies))
    other_rows = crossed(along_x, 1)
    own_later, _ = lax.optimization_barrier((own, other_rows))
    odd_mine = lax.ppermute(own_later, "section", [(i, i ^ 2) for i in range(1, sections, 2)])
    even_rows = jnp.where(core == 0, along_x, other_rows)
    odd_rows = jnp.where(core == 0, other_rows, along_x)
    rot_cols = jnp.stack([even_rows, odd_rows]).transpose(2, 0, 1, 3, 4).reshape(D, part_cols)

    where = place[None].astype(jnp.int32)
    all_rows = STAGE * tok_rows
    kept = (jnp.zeros((all_rows, D), jnp.bfloat16), jnp.zeros((all_rows, part_cols), jnp.float32))
    weights = []
    keeps = [jnp.full((1,), 1, jnp.int32)]
    keeps += [(stage_pos == stage).astype(jnp.int32)[None] for stage in range(1, stages)]
    row_scales = jnp.repeat(scales, tok_rows, axis=0)
    dp_pos = lax.axis_index("dp").astype(jnp.uint32)
    partners = [lax.rem(dp_pos + jnp.uint32(step), jnp.uint32(replicas)) for step in range(replicas)]
    which = core[None].astype(jnp.int32)
    ahead = (keeps, row_scales, partners, which)
    for stage in range(stages):
        keep = keeps[stage]
        for layer in range(STAGE):
            last = stage == stages - 1 and layer == STAGE - 1
            gain, scale = gains[layer : layer + 1], scales[layer : layer + 1]
            rows = exchange(copies, "tp")
            if stage == 0 and layer in (1, 2):
                odd = layer - 1
                mine, other = sources[4:] if odd else sources[2:4]
                far = jnp.where(core == odd, mine, other)
                near = jnp.where(core == odd, own, by1)
                pair = jnp.where(place // 2 == 0, near, far), jnp.where(place // 2 == 0, far, near)
                rows, pair, ahead = lax.optimization_barrier((rows, pair, ahead))
                weights.append(pair)
                keeps, row_scales, partners, which = ahead
            results = rotate(layer, last, keep, rows, gain, rot_cols, scale, kept)
            kept = results[:2]
            if last:
                break
            quant = results[2]
            if stage == 0 and layer == 0:
                even_mine, _ = lax.optimization_barrier((even_mine, quant))
                even_other = lax.ppermute(even_mine, "section", [(i, i + 1) for i in range(0, sections, 2)])
                sources = (own, by1, even_mine, even_other, even_mine, even_other)
            if stage == 0 and layer == 1:
                odd_mine, _ = lax.optimization_barrier((odd_mine, quant))
                odd_other = lax.ppermute(odd_mine, "section", [(i + 1, i) for i in range(0, sections, 2)])
                sources = (own, by1, even_mine, even_other, odd_mine, odd_other)
            quant_rows = exchange(quant, "tp")
            if stage == 0 and layer < 2:
                copies, stream = project_from(layer, where, sources, quant_rows, stream)
            else:
                copies, stream = project(quant_rows, weights[layer % 2][layer // 2], stream)
        if stage < stages - 1:
            stream = lax.ppermute(
                stream, "section", [(i, i + STAGE) for i in range(sections - STAGE)]
            )
            copies = spread(stream, tensor)
    kept_normed, kept_rotated = kept

    lanes = all_rows
    turned = lax.optimization_barrier(kept_normed.T)
    turned = turned.reshape(sections, replicas, row_block, lanes).transpose(1, 0, 2, 3)
    turned = turned.reshape(replicas, sections * row_block, lanes)
    level, slope = level_and_slope(kept_rotated, row_scales)
    error_part = level - kept_rotated
    grad_rot = (error_part * (slope - 1.0)).astype(jnp.bfloat16)
    grad_rot = grad_rot.reshape(all_rows, part_cols // lanes, lanes).transpose(1, 0, 2)
    sent = jnp.concatenate([turned, copies_of(grad_rot.reshape(-1, lanes), replicas)], axis=1)

    def block(step):
        return lax.dynamic_index_in_dim(sent, partners[step], 0, keepdims=False)

    parts = jnp.stack(
        [block(0)]
        + [
            lax.ppermute(block(k), "dp", [(i, (i + k) % replicas) for i in range(replicas)])
            for k in range(1, replicas)
        ]
    )
    mine, other = terms_of(which, parts, planes, row_block, part_cols)
    loss = jnp.full((8, 128), jnp.sum(error_part * error_part), jnp.float32)
    losses = exchange(copies_of(loss, replicas * tensor), ("dp", "tp"))
    losses, _ = lax.optimization_barrier((losses, other))
    loss = jnp.sum(losses, axis=0)
    loss = loss + crossed(loss, 1)
    high = lax.reduce_precision(loss, 8, 7)
    middle = lax.reduce_precision(loss - high, 8, 7)
    low = loss - high - middle
    lane = lax.broadcasted_iota(jnp.int32, loss.shape, 1)
    tail_rows = jnp.where(lane == 0, high, jnp.where(lane == 1, middle, jnp.where(lane == 2, low, 0.0)))
    tail_rows = jnp.tile(tail_rows.astype(jnp.bfloat16), (1, part_cols // lanes))

    pair_sum = (mine + crossed(other, 1).astype(jnp.float32)).astype(jnp.bfloat16)
    sent = jnp.concatenate([pair_sum, copies_of(tail_rows, planes)], axis=1)
    parts = lax.all_to_all(sent, "section", 0, 0, axis_index_groups=same_core, tiled=True)
    sums = jnp.sum(parts.astype(jnp.float32), axis=0)
    factor = 1.0 / math.sqrt(sections * all_rows * replicas)
    norm_count = all_rows * replicas * D
    return (sums[:row_block] * factor, jnp.sum(sums[row_block, :3]) / norm_count)


def solution(mesh):
    placed = (
        P(None, "dp", "tp"),
        P(("section", "dp"), "tp"),
        P("section", None, "tp"),
        P("section", None),
        P("section", "tp"),
    )
    return jax.shard_map(
        local,
        mesh=mesh,
        in_specs=placed,
        out_specs=(P(("section", "dp"), "tp"), P()),
        check_vma=False,
    )
```

```python
import functools
import math

import jax
import jax.numpy as jnp
from jax import lax
from jax.experimental import pallas as pl
from jax.experimental.pallas import tpu as pltpu
from jax.sharding import PartitionSpec as P

D = 4096
GROUP = 128
STAGE = 4

norm_eps = 1e-05
full_turn = 2.0 * math.pi

SIN_TERMS = (3.141592653536291, -5.167712764624543, 2.5501633189471025,
             -0.5992521978250058, 0.08205040181365181, -0.007028386419353805)
COS_TERMS = (0.9999999997799043, -4.934802137078827, 4.058709159556301,
             -1.3352120030506605, 0.23493731381815505, -0.024396324355626643)


def horner(terms, square):
    total = jnp.full_like(square, terms[-1])
    for term in terms[-2::-1]:
        total = total * square + term
    return total


def half_turn(ratio):
    part = ratio - jnp.round(ratio)
    square = part * part
    return part * horner(SIN_TERMS, square), horner(COS_TERMS, square)


def quantize(values, scale):
    ratio = values / scale
    sine, cosine = half_turn(ratio)
    return scale * jnp.clip(ratio - sine * cosine / math.pi, -8.0, 7.0)


def level_and_slope(values, scale):
    ratio = values / scale
    sine, cosine = half_turn(ratio)
    stair = ratio - sine * cosine / math.pi
    inside = (stair > -8.0) & (stair < 7.0)
    level = scale * jnp.clip(stair, -8.0, 7.0)
    return level, jnp.where(inside, 2.0 * sine * sine, 0.0)


def copies_of(value, count):
    return jnp.broadcast_to(value[None], (count,) + value.shape)


def exchange(copies, axis):
    return lax.all_to_all(copies, axis, 0, 0, tiled=True)


def gather(value, axis):
    return exchange(copies_of(value, lax.axis_size(axis)), axis)


def crossed(value, mask):
    return lax.ppermute(value, "section", [(i, i ^ mask) for i in range(lax.axis_size("section"))])


def doubled(value):
    count, position = lax.axis_size("tp"), lax.axis_index("tp")
    value, mask = value[None], 1
    while mask < count:
        other = lax.ppermute(value, "tp", [(i, i ^ mask) for i in range(count)])
        upper = position & mask != 0
        value = jnp.concatenate([jnp.where(upper, other, value), jnp.where(upper, value, other)], axis=0)
        mask *= 2
    return value


VMEM = pl.BlockSpec(memory_space=pltpu.VMEM)
SMEM = pl.BlockSpec(memory_space=pltpu.SMEM)
FAR = pl.BlockSpec(memory_space=pl.ANY)
PARAMS = pltpu.CompilerParams(vmem_limit_bytes=8 * 1024 * 1024)


def start_load(layer, place_ref, refs, into, sems):
    chunks = sems.shape[0]
    chunk = into.shape[0] // chunks
    plane, core = place_ref[0] // 2, place_ref[0] % 2
    own, by1, even_mine, even_other, odd_mine, odd_other = refs
    mine, other = (odd_mine, odd_other) if layer % 2 else (even_mine, even_other)
    here, same = plane == layer // 2, core == layer % 2
    away, differs = jnp.logical_not(here), jnp.logical_not(same)
    for wanted, source in (
        (here & same, own), (here & differs, by1), (away & same, mine), (away & differs, other)
    ):
        @pl.when(wanted)
        def _():
            for index in range(chunks):
                rows = pl.ds(index * chunk, chunk)
                pltpu.make_async_copy(source.at[rows], into.at[rows], sems.at[index]).start()


def project_from_kernel(layer, place_ref, *args):
    refs, (quant_ref, stream_ref, copies_ref, out_ref, weight_ref, sems) = args[:6], args[6:]
    start_load(layer, place_ref, refs, weight_ref, sems)
    count, tok_rows, part = quant_ref.shape
    total = stream_ref[...].astype(jnp.float32)
    for k in range(count):
        rows = pl.ds(k * part, part)
        pltpu.make_async_copy(refs[0].at[rows], weight_ref.at[rows], sems.at[k]).wait()
        total = total + jnp.dot(quant_ref[k], weight_ref[rows], preferred_element_type=jnp.float32)
    stream = total.astype(jnp.bfloat16)
    out_ref[...] = stream
    for k in range(count):
        copies_ref[k] = stream


def project_from(layer, place, sources, quant_rows, stream):
    own = sources[0]
    return pl.pallas_call(
        functools.partial(project_from_kernel, layer),
        out_shape=[
            jax.ShapeDtypeStruct(quant_rows.shape, jnp.bfloat16),
            jax.ShapeDtypeStruct(stream.shape, jnp.bfloat16),
        ],
        in_specs=[SMEM] + [FAR] * 6 + [VMEM] * 2,
        out_specs=[VMEM] * 2,
        scratch_shapes=[
            pltpu.VMEM(own.shape, own.dtype),
            pltpu.SemaphoreType.DMA((quant_rows.shape[0],)),
        ],
        compiler_params=PARAMS,
        name="project_from",
    )(place, *sources, quant_rows, stream)


def project_kernel(quant_ref, weight_ref, stream_ref, copies_ref, out_ref):
    count, tok_rows, part = quant_ref.shape
    total = stream_ref[...].astype(jnp.float32)
    for k in range(count):
        rows = pl.ds(k * part, part)
        total = total + jnp.dot(quant_ref[k], weight_ref[rows], preferred_element_type=jnp.float32)
    stream = total.astype(jnp.bfloat16)
    out_ref[...] = stream
    for k in range(count):
        copies_ref[k] = stream


def project(quant_rows, weight, stream):
    return pl.pallas_call(
        project_kernel,
        out_shape=[
            jax.ShapeDtypeStruct(quant_rows.shape, jnp.bfloat16),
            jax.ShapeDtypeStruct(stream.shape, jnp.bfloat16),
        ],
        in_specs=[VMEM] * 3,
        out_specs=[VMEM] * 2,
        compiler_params=PARAMS,
        name="project",
    )(quant_rows, weight, stream)


def rotate_kernel(layer, last, keep_ref, rows_ref, gain_ref, rot_ref, scale_ref, _, __, *rest):
    (kept_normed, kept_rotated), rest = rest[:2], rest[2:]
    copies, (normed_ref, rotated_ref, sems) = rest[:-3], rest[-3:]
    count, tok_rows, part = rows_ref.shape
    place = pl.ds(layer * tok_rows, tok_rows)
    keep = keep_ref[0] == 1
    keep_normed = pltpu.make_async_copy(normed_ref, kept_normed.at[place], sems.at[0])
    keep_rotated = pltpu.make_async_copy(rotated_ref, kept_rotated.at[place], sems.at[1])
    total = None
    for k in range(count):
        rows = rows_ref[k].astype(jnp.float32)
        square = jnp.sum(rows * rows, axis=-1, keepdims=True)
        total = square if total is None else total + square
    factor = lax.rsqrt(total / (count * part) + norm_eps)
    for k in range(count):
        cols = slice(k * part, (k + 1) * part)
        rows = rows_ref[k].astype(jnp.float32)
        normed_ref[:, cols] = (rows * factor * gain_ref[:, cols]).astype(jnp.bfloat16)
    pl.when(keep)(keep_normed.start)
    rotated = jnp.dot(normed_ref[...], rot_ref[...], preferred_element_type=jnp.float32)
    rotated_ref[...] = rotated
    pl.when(keep)(keep_rotated.start)
    if not last:
        quantized = quantize(rotated, scale_ref[...]).astype(jnp.bfloat16)
        for k in range(count):
            copies[0][k] = quantized

    @pl.when(keep)
    def _():
        keep_normed.wait()
        keep_rotated.wait()


def rotate(layer, last, keep, rows, gain, rot_cols, scale, kept):
    count, tok_rows, part = rows.shape
    shapes = [jax.ShapeDtypeStruct(k.shape, k.dtype) for k in kept]
    if not last:
        shapes.append(jax.ShapeDtypeStruct(rows.shape, jnp.bfloat16))
    return pl.pallas_call(
        functools.partial(rotate_kernel, layer, last),
        out_shape=shapes,
        in_specs=[SMEM] + [VMEM] * 4 + [FAR] * 2,
        out_specs=[FAR] * 2 + [VMEM] * (len(shapes) - 2),
        input_output_aliases={5: 0, 6: 1},
        scratch_shapes=[
            pltpu.VMEM((tok_rows, count * part), jnp.bfloat16),
            pltpu.VMEM((tok_rows, part), jnp.float32),
            pltpu.SemaphoreType.DMA((2,)),
        ],
        compiler_params=PARAMS,
        name="rotate",
    )(keep, rows, gain, rot_cols, scale, *kept)


def spread_kernel(stream_ref, copies_ref):
    for k in range(copies_ref.shape[0]):
        copies_ref[k] = stream_ref[...]


def spread(stream, count):
    return pl.pallas_call(
        spread_kernel,
        out_shape=jax.ShapeDtypeStruct((count,) + stream.shape, stream.dtype),
        in_specs=[VMEM],
        out_specs=VMEM,
        compiler_params=PARAMS,
        name="spread",
    )(stream)


def terms_kernel(part_rows, core_ref, parts_ref, mine_ref, other_ref):
    sources, rows, lanes = parts_ref.shape
    count, _, cols = mine_ref.shape
    features = 2 * count * part_rows
    left = jnp.concatenate([parts_ref[s, :features] for s in range(sources)], axis=1)
    right = jnp.concatenate(
        [
            jnp.concatenate([parts_ref[s, pl.ds(k, lanes)] for k in range(features, rows, lanes)], axis=1)
            for s in range(sources)
        ],
        axis=0,
    )
    terms = jnp.dot(left, right, preferred_element_type=jnp.float32)
    lower = core_ref[0] == 0
    for z in range(count):
        even = terms[2 * z * part_rows : (2 * z + 1) * part_rows]
        odd = terms[(2 * z + 1) * part_rows : (2 * z + 2) * part_rows]
        mine_ref[z] = jnp.where(lower, even, odd)
        other_ref[z] = jnp.where(lower, odd, even).astype(jnp.bfloat16)


def terms_of(core, parts, planes, row_block, part_cols):
    shape = (planes, row_block, part_cols)
    return pl.pallas_call(
        functools.partial(terms_kernel, row_block),
        out_shape=[jax.ShapeDtypeStruct(shape, jnp.float32), jax.ShapeDtypeStruct(shape, jnp.bfloat16)],
        in_specs=[pl.BlockSpec(memory_space=pltpu.SMEM), VMEM],
        out_specs=[VMEM, VMEM],
        compiler_params=pltpu.CompilerParams(vmem_limit_bytes=24 * 1024 * 1024),
        name="terms",
    )(core, parts)


def local(hidden_in, rotation, proj, norm_gain, quant_exp):
    sections = lax.axis_size("section")
    replicas = lax.axis_size("dp")
    tensor = lax.axis_size("tp")
    section_pos = lax.axis_index("section")
    micro_count, tok_rows, part_cols = hidden_in.shape
    stages = sections // STAGE
    planes = sections // 2
    stage_pos = section_pos // STAGE
    place = section_pos % STAGE
    core = section_pos % 2
    same_core = [[2 * z + c for z in range(planes)] for c in range(2)]
    row_block = rotation.shape[0]

    own = proj[0]
    by1 = crossed(own, 1)

    scale_row = jnp.repeat(jnp.exp2(quant_exp.astype(jnp.float32) * 0.25) * 0.125, GROUP, axis=1)
    params = jnp.concatenate([norm_gain, scale_row], axis=1)
    params_by1 = crossed(params, 1)
    params_by2 = crossed(params, 2)
    along_z = lax.all_to_all(
        copies_of(rotation, planes), "section", 0, 0, axis_index_groups=same_core, tiled=True
    )
    params_by3 = crossed(params_by2, 1)
    along_z, by1, params_by2, params_by3 = lax.optimization_barrier((along_z, by1, params_by2, params_by3))
    own_now, _ = lax.optimization_barrier((own, params_by2))
    even_mine = lax.ppermute(own_now, "section", [(i, i ^ 2) for i in range(0, sections, 2)])
    found = jnp.concatenate([params, params_by1, params_by2, params_by3], axis=0)
    params = jnp.stack([lax.dynamic_index_in_dim(found, place ^ k, 0, False) for k in range(STAGE)])
    gains, scales = params[:, :D], params[:, D:]

    along_x = gather(along_z, "dp")
    stream = lax.dynamic_index_in_dim(hidden_in, place, 0, keepdims=False)
    stream, _ = lax.optimization_barrier((stream, along_z))
    first_rows = doubled(stream)
    along_x, gains, scales, stream, first_rows = lax.optimization_barrier(
        (along_x, gains, scales, stream, first_rows)
    )
    other_rows = crossed(along_x, 1)
    own_later, _ = lax.optimization_barrier((own, other_rows))
    odd_mine = lax.ppermute(own_later, "section", [(i, i ^ 2) for i in range(1, sections, 2)])
    even_rows = jnp.where(core == 0, along_x, other_rows)
    odd_rows = jnp.where(core == 0, other_rows, along_x)
    rot_cols = jnp.stack([even_rows, odd_rows]).transpose(2, 0, 1, 3, 4).reshape(D, part_cols)

    where = place[None].astype(jnp.int32)
    all_rows = STAGE * tok_rows
    kept = (jnp.zeros((all_rows, D), jnp.bfloat16), jnp.zeros((all_rows, part_cols), jnp.float32))
    weights = []
    keeps = [jnp.full((1,), 1, jnp.int32)]
    keeps += [(stage_pos == stage).astype(jnp.int32)[None] for stage in range(1, stages)]
    row_scales = jnp.repeat(scales, tok_rows, axis=0)
    dp_pos = lax.axis_index("dp").astype(jnp.uint32)
    partners = [lax.rem(dp_pos + jnp.uint32(step), jnp.uint32(replicas)) for step in range(replicas)]
    which = core[None].astype(jnp.int32)
    ahead = (keeps, row_scales, partners, which)
    for stage in range(stages):
        keep = keeps[stage]
        for layer in range(STAGE):
            last = stage == stages - 1 and layer == STAGE - 1
            gain, scale = gains[layer : layer + 1], scales[layer : layer + 1]
            rows = exchange(copies, "tp") if stage or layer else first_rows
            if stage == 0 and layer in (1, 2):
                odd = layer - 1
                mine, other = sources[4:] if odd else sources[2:4]
                far = jnp.where(core == odd, mine, other)
                near = jnp.where(core == odd, own, by1)
                pair = jnp.where(place // 2 == 0, near, far), jnp.where(place // 2 == 0, far, near)
                rows, pair, ahead = lax.optimization_barrier((rows, pair, ahead))
                weights.append(pair)
                keeps, row_scales, partners, which = ahead
            results = rotate(layer, last, keep, rows, gain, rot_cols, scale, kept)
            kept = results[:2]
            if last:
                break
            quant = results[2]
            if stage == 0 and layer == 0:
                even_mine, _ = lax.optimization_barrier((even_mine, quant))
                even_other = lax.ppermute(even_mine, "section", [(i, i + 1) for i in range(0, sections, 2)])
                sources = (own, by1, even_mine, even_other, even_mine, even_other)
            if stage == 0 and layer == 1:
                odd_mine, _ = lax.optimization_barrier((odd_mine, quant))
                odd_other = lax.ppermute(odd_mine, "section", [(i + 1, i) for i in range(0, sections, 2)])
                sources = (own, by1, even_mine, even_other, odd_mine, odd_other)
            quant_rows = exchange(quant, "tp")
            if stage == 0 and layer < 2:
                copies, stream = project_from(layer, where, sources, quant_rows, stream)
            else:
                copies, stream = project(quant_rows, weights[layer % 2][layer // 2], stream)
        if stage < stages - 1:
            stream = lax.ppermute(
                stream, "section", [(i, i + STAGE) for i in range(sections - STAGE)]
            )
            copies = spread(stream, tensor)
    kept_normed, kept_rotated = kept

    lanes = all_rows
    turned = lax.optimization_barrier(kept_normed.T)
    turned = turned.reshape(sections, replicas, row_block, lanes).transpose(1, 0, 2, 3)
    turned = turned.reshape(replicas, sections * row_block, lanes)
    level, slope = level_and_slope(kept_rotated, row_scales)
    error_part = level - kept_rotated
    grad_rot = (error_part * (slope - 1.0)).astype(jnp.bfloat16)
    grad_rot = grad_rot.reshape(all_rows, part_cols // lanes, lanes).transpose(1, 0, 2)
    sent = jnp.concatenate([turned, copies_of(grad_rot.reshape(-1, lanes), replicas)], axis=1)

    def block(step):
        return lax.dynamic_index_in_dim(sent, partners[step], 0, keepdims=False)

    parts = jnp.stack(
        [block(0)]
        + [
            lax.ppermute(block(k), "dp", [(i, (i + k) % replicas) for i in range(replicas)])
            for k in range(1, replicas)
        ]
    )
    mine, other = terms_of(which, parts, planes, row_block, part_cols)
    loss = jnp.full((8, 128), jnp.sum(error_part * error_part), jnp.float32)
    losses = exchange(copies_of(loss, replicas * tensor), ("dp", "tp"))
    losses, _ = lax.optimization_barrier((losses, other))
    loss = jnp.sum(losses, axis=0)
    loss = loss + crossed(loss, 1)
    high = lax.reduce_precision(loss, 8, 7)
    middle = lax.reduce_precision(loss - high, 8, 7)
    low = loss - high - middle
    lane = lax.broadcasted_iota(jnp.int32, loss.shape, 1)
    tail_rows = jnp.where(lane == 0, high, jnp.where(lane == 1, middle, jnp.where(lane == 2, low, 0.0)))
    tail_rows = jnp.tile(tail_rows.astype(jnp.bfloat16), (1, part_cols // lanes))

    pair_sum = (mine + crossed(other, 1).astype(jnp.float32)).astype(jnp.bfloat16)
    sent = jnp.concatenate([pair_sum, copies_of(tail_rows, planes)], axis=1)
    parts = lax.all_to_all(sent, "section", 0, 0, axis_index_groups=same_core, tiled=True)
    sums = jnp.sum(parts.astype(jnp.float32), axis=0)
    factor = 1.0 / math.sqrt(sections * all_rows * replicas)
    norm_count = all_rows * replicas * D
    return (sums[:row_block] * factor, jnp.sum(sums[row_block, :3]) / norm_count)


def solution(mesh):
    placed = (
        P(None, "dp", "tp"),
        P(("section", "dp"), "tp"),
        P("section", None, "tp"),
        P("section", None),
        P("section", "tp"),
    )
    return jax.shard_map(
        local,
        mesh=mesh,
        in_specs=placed,
        out_specs=(P(("section", "dp"), "tp"), P()),
        check_vma=False,
    )
```

```python
import functools
import math

import jax
import jax.numpy as jnp
from jax import lax
from jax.experimental import pallas as pl
from jax.experimental.pallas import tpu as pltpu
from jax.sharding import PartitionSpec as P

D = 4096
GROUP = 128
STAGE = 4

norm_eps = 1e-05
full_turn = 2.0 * math.pi

SIN_TERMS = (3.141592653536291, -5.167712764624543, 2.5501633189471025,
             -0.5992521978250058, 0.08205040181365181, -0.007028386419353805)
COS_TERMS = (0.9999999997799043, -4.934802137078827, 4.058709159556301,
             -1.3352120030506605, 0.23493731381815505, -0.024396324355626643)


def horner(terms, square):
    total = jnp.full_like(square, terms[-1])
    for term in terms[-2::-1]:
        total = total * square + term
    return total


def half_turn(ratio):
    part = ratio - jnp.round(ratio)
    square = part * part
    return part * horner(SIN_TERMS, square), horner(COS_TERMS, square)


def quantize(values, scale):
    ratio = values / scale
    sine, cosine = half_turn(ratio)
    return scale * jnp.clip(ratio - sine * cosine / math.pi, -8.0, 7.0)


def level_and_slope(values, scale):
    ratio = values / scale
    sine, cosine = half_turn(ratio)
    stair = ratio - sine * cosine / math.pi
    inside = (stair > -8.0) & (stair < 7.0)
    level = scale * jnp.clip(stair, -8.0, 7.0)
    return level, jnp.where(inside, 2.0 * sine * sine, 0.0)


def copies_of(value, count):
    return jnp.broadcast_to(value[None], (count,) + value.shape)


def exchange(copies, axis):
    return lax.all_to_all(copies, axis, 0, 0, tiled=True)


def gather(value, axis):
    return exchange(copies_of(value, lax.axis_size(axis)), axis)


def crossed(value, mask):
    return lax.ppermute(value, "section", [(i, i ^ mask) for i in range(lax.axis_size("section"))])


def doubled(value):
    count, position = lax.axis_size("tp"), lax.axis_index("tp")
    value, mask = value[None], 1
    while mask < count:
        other = lax.ppermute(value, "tp", [(i, i ^ mask) for i in range(count)])
        upper = position & mask != 0
        value = jnp.concatenate([jnp.where(upper, other, value), jnp.where(upper, value, other)], axis=0)
        mask *= 2
    return value


VMEM = pl.BlockSpec(memory_space=pltpu.VMEM)
SMEM = pl.BlockSpec(memory_space=pltpu.SMEM)
FAR = pl.BlockSpec(memory_space=pl.ANY)
PARAMS = pltpu.CompilerParams(vmem_limit_bytes=8 * 1024 * 1024)


def start_load(layer, place_ref, refs, into, sems):
    chunks = sems.shape[0]
    chunk = into.shape[0] // chunks
    plane, core = place_ref[0] // 2, place_ref[0] % 2
    own, by1, even_mine, even_other, odd_mine, odd_other = refs
    mine, other = (odd_mine, odd_other) if layer % 2 else (even_mine, even_other)
    here, same = plane == layer // 2, core == layer % 2
    away, differs = jnp.logical_not(here), jnp.logical_not(same)
    for wanted, source in (
        (here & same, own), (here & differs, by1), (away & same, mine), (away & differs, other)
    ):
        @pl.when(wanted)
        def _():
            for index in range(chunks):
                rows = pl.ds(index * chunk, chunk)
                pltpu.make_async_copy(source.at[rows], into.at[rows], sems.at[index]).start()


def project_from_kernel(layer, place_ref, *args):
    refs, (quant_ref, stream_ref, copies_ref, out_ref, weight_ref, sems) = args[:6], args[6:]
    start_load(layer, place_ref, refs, weight_ref, sems)
    count, tok_rows, part = quant_ref.shape
    total = stream_ref[...].astype(jnp.float32)
    for k in range(count):
        rows = pl.ds(k * part, part)
        pltpu.make_async_copy(refs[0].at[rows], weight_ref.at[rows], sems.at[k]).wait()
        total = total + jnp.dot(quant_ref[k], weight_ref[rows], preferred_element_type=jnp.float32)
    stream = total.astype(jnp.bfloat16)
    out_ref[...] = stream
    for k in range(count):
        copies_ref[k] = stream


def project_from(layer, place, sources, quant_rows, stream):
    own = sources[0]
    return pl.pallas_call(
        functools.partial(project_from_kernel, layer),
        out_shape=[
            jax.ShapeDtypeStruct(quant_rows.shape, jnp.bfloat16),
            jax.ShapeDtypeStruct(stream.shape, jnp.bfloat16),
        ],
        in_specs=[SMEM] + [FAR] * 6 + [VMEM] * 2,
        out_specs=[VMEM] * 2,
        scratch_shapes=[
            pltpu.VMEM(own.shape, own.dtype),
            pltpu.SemaphoreType.DMA((quant_rows.shape[0],)),
        ],
        compiler_params=PARAMS,
        name="project_from",
    )(place, *sources, quant_rows, stream)


def project_kernel(quant_ref, weight_ref, stream_ref, copies_ref, out_ref):
    count, tok_rows, part = quant_ref.shape
    total = stream_ref[...].astype(jnp.float32)
    for k in range(count):
        rows = pl.ds(k * part, part)
        total = total + jnp.dot(quant_ref[k], weight_ref[rows], preferred_element_type=jnp.float32)
    stream = total.astype(jnp.bfloat16)
    out_ref[...] = stream
    for k in range(count):
        copies_ref[k] = stream


def project(quant_rows, weight, stream):
    return pl.pallas_call(
        project_kernel,
        out_shape=[
            jax.ShapeDtypeStruct(quant_rows.shape, jnp.bfloat16),
            jax.ShapeDtypeStruct(stream.shape, jnp.bfloat16),
        ],
        in_specs=[VMEM] * 3,
        out_specs=[VMEM] * 2,
        compiler_params=PARAMS,
        name="project",
    )(quant_rows, weight, stream)


def rotate_kernel(layer, last, keep_ref, rows_ref, gain_ref, rot_ref, scale_ref, _, __, *rest):
    (kept_normed, kept_rotated), rest = rest[:2], rest[2:]
    copies, (normed_ref, rotated_ref, sems) = rest[:-3], rest[-3:]
    count, tok_rows, part = rows_ref.shape
    place = pl.ds(layer * tok_rows, tok_rows)
    keep = keep_ref[0] == 1
    keep_normed = pltpu.make_async_copy(normed_ref, kept_normed.at[place], sems.at[0])
    keep_rotated = pltpu.make_async_copy(rotated_ref, kept_rotated.at[place], sems.at[1])
    total = None
    for k in range(count):
        rows = rows_ref[k].astype(jnp.float32)
        square = jnp.sum(rows * rows, axis=-1, keepdims=True)
        total = square if total is None else total + square
    factor = lax.rsqrt(total / (count * part) + norm_eps)
    for k in range(count):
        cols = slice(k * part, (k + 1) * part)
        rows = rows_ref[k].astype(jnp.float32)
        normed_ref[:, cols] = (rows * factor * gain_ref[:, cols]).astype(jnp.bfloat16)
    pl.when(keep)(keep_normed.start)
    rotated = jnp.dot(normed_ref[...], rot_ref[...], preferred_element_type=jnp.float32)
    rotated_ref[...] = rotated
    pl.when(keep)(keep_rotated.start)
    if not last:
        quantized = quantize(rotated, scale_ref[...]).astype(jnp.bfloat16)
        for k in range(count):
            copies[0][k] = quantized

    @pl.when(keep)
    def _():
        keep_normed.wait()
        keep_rotated.wait()


def rotate(layer, last, keep, rows, gain, rot_cols, scale, kept):
    count, tok_rows, part = rows.shape
    shapes = [jax.ShapeDtypeStruct(k.shape, k.dtype) for k in kept]
    if not last:
        shapes.append(jax.ShapeDtypeStruct(rows.shape, jnp.bfloat16))
    return pl.pallas_call(
        functools.partial(rotate_kernel, layer, last),
        out_shape=shapes,
        in_specs=[SMEM] + [VMEM] * 4 + [FAR] * 2,
        out_specs=[FAR] * 2 + [VMEM] * (len(shapes) - 2),
        input_output_aliases={5: 0, 6: 1},
        scratch_shapes=[
            pltpu.VMEM((tok_rows, count * part), jnp.bfloat16),
            pltpu.VMEM((tok_rows, part), jnp.float32),
            pltpu.SemaphoreType.DMA((2,)),
        ],
        compiler_params=PARAMS,
        name="rotate",
    )(keep, rows, gain, rot_cols, scale, *kept)


def spread_kernel(stream_ref, copies_ref):
    for k in range(copies_ref.shape[0]):
        copies_ref[k] = stream_ref[...]


def spread(stream, count):
    return pl.pallas_call(
        spread_kernel,
        out_shape=jax.ShapeDtypeStruct((count,) + stream.shape, stream.dtype),
        in_specs=[VMEM],
        out_specs=VMEM,
        compiler_params=PARAMS,
        name="spread",
    )(stream)


def terms_kernel(part_rows, core_ref, parts_ref, mine_ref, other_ref):
    sources, rows, lanes = parts_ref.shape
    count, _, cols = mine_ref.shape
    features = 2 * count * part_rows
    left = jnp.concatenate([parts_ref[s, :features] for s in range(sources)], axis=1)
    right = jnp.concatenate(
        [
            jnp.concatenate([parts_ref[s, pl.ds(k, lanes)] for k in range(features, rows, lanes)], axis=1)
            for s in range(sources)
        ],
        axis=0,
    )
    terms = jnp.dot(left, right, preferred_element_type=jnp.float32)
    lower = core_ref[0] == 0
    for z in range(count):
        even = terms[2 * z * part_rows : (2 * z + 1) * part_rows]
        odd = terms[(2 * z + 1) * part_rows : (2 * z + 2) * part_rows]
        mine_ref[z] = jnp.where(lower, even, odd)
        other_ref[z] = jnp.where(lower, odd, even).astype(jnp.bfloat16)


def terms_of(core, parts, planes, row_block, part_cols):
    shape = (planes, row_block, part_cols)
    return pl.pallas_call(
        functools.partial(terms_kernel, row_block),
        out_shape=[jax.ShapeDtypeStruct(shape, jnp.float32), jax.ShapeDtypeStruct(shape, jnp.bfloat16)],
        in_specs=[pl.BlockSpec(memory_space=pltpu.SMEM), VMEM],
        out_specs=[VMEM, VMEM],
        compiler_params=pltpu.CompilerParams(vmem_limit_bytes=24 * 1024 * 1024),
        name="terms",
    )(core, parts)


def local(hidden_in, rotation, proj, norm_gain, quant_exp):
    sections = lax.axis_size("section")
    replicas = lax.axis_size("dp")
    tensor = lax.axis_size("tp")
    section_pos = lax.axis_index("section")
    micro_count, tok_rows, part_cols = hidden_in.shape
    stages = sections // STAGE
    planes = sections // 2
    stage_pos = section_pos // STAGE
    place = section_pos % STAGE
    core = section_pos % 2
    same_core = [[2 * z + c for z in range(planes)] for c in range(2)]
    row_block = rotation.shape[0]

    own = proj[0]
    by1 = crossed(own, 1)

    scale_row = jnp.repeat(jnp.exp2(quant_exp.astype(jnp.float32) * 0.25) * 0.125, GROUP, axis=1)
    params = jnp.concatenate([norm_gain, scale_row], axis=1)
    params_by1 = crossed(params, 1)
    params_by2 = crossed(params, 2)
    along_z = lax.all_to_all(
        copies_of(rotation, planes), "section", 0, 0, axis_index_groups=same_core, tiled=True
    )
    along_z, by1, params_by2 = lax.optimization_barrier((along_z, by1, params_by2))
    own_now, _ = lax.optimization_barrier((own, params_by2))
    even_mine = lax.ppermute(own_now, "section", [(i, i ^ 2) for i in range(0, sections, 2)])
    along_x = gather(along_z, "dp")
    stream = lax.dynamic_index_in_dim(hidden_in, place, 0, keepdims=False)
    stream, _ = lax.optimization_barrier((stream, along_z))
    first_rows = doubled(stream)
    keeps = [jnp.full((1,), 1, jnp.int32)]
    keeps += [(stage_pos == stage).astype(jnp.int32)[None] for stage in range(1, stages)]
    dp_pos = lax.axis_index("dp").astype(jnp.uint32)
    partners = [lax.rem(dp_pos + jnp.uint32(step), jnp.uint32(replicas)) for step in range(replicas)]
    which, where = core[None].astype(jnp.int32), place[None].astype(jnp.int32)
    on_core, low_plane = [core == 0, core == 1], place // 2 == 0
    ahead = (keeps, partners, which, where, on_core, low_plane)
    along_x, stream, first_rows, ahead = lax.optimization_barrier((along_x, stream, first_rows, ahead))
    keeps, partners, which, where, on_core, low_plane = ahead
    params_by2, _ = lax.optimization_barrier((params_by2, along_x))
    params_by3 = crossed(params_by2, 1)
    found = jnp.concatenate([params, params_by1, params_by2, params_by3], axis=0)
    params = jnp.stack([lax.dynamic_index_in_dim(found, place ^ k, 0, False) for k in range(STAGE)])
    gains, scales = params[:, :D], params[:, D:]
    row_scales = jnp.repeat(scales, tok_rows, axis=0)
    other_rows = crossed(along_x, 1)
    own_later, _ = lax.optimization_barrier((own, other_rows))
    odd_mine = lax.ppermute(own_later, "section", [(i, i ^ 2) for i in range(1, sections, 2)])
    even_rows = jnp.where(core == 0, along_x, other_rows)
    odd_rows = jnp.where(core == 0, other_rows, along_x)
    rot_cols = jnp.stack([even_rows, odd_rows]).transpose(2, 0, 1, 3, 4).reshape(D, part_cols)
    rot_cols, row_scales = lax.optimization_barrier((rot_cols, row_scales))

    all_rows = STAGE * tok_rows
    kept = (jnp.zeros((all_rows, D), jnp.bfloat16), jnp.zeros((all_rows, part_cols), jnp.float32))
    weights = []

    def ordered(odd):
        mine, other = sources[4:] if odd else sources[2:4]
        far = jnp.where(on_core[odd], mine, other)
        near = jnp.where(on_core[odd], own, by1)
        return jnp.where(low_plane, near, far), jnp.where(low_plane, far, near)

    for stage in range(stages):
        keep = keeps[stage]
        for layer in range(STAGE):
            last = stage == stages - 1 and layer == STAGE - 1
            gain, scale = gains[layer : layer + 1], scales[layer : layer + 1]
            rows = exchange(copies, "tp") if stage or layer else first_rows
            if stage == 0 and layer in (1, 2):
                rows, pair = lax.optimization_barrier((rows, ordered(layer - 1)))
                weights.append(pair)
            results = rotate(layer, last, keep, rows, gain, rot_cols, scale, kept)
            kept = results[:2]
            if last:
                break
            quant = results[2]
            if stage == 0 and layer == 0:
                even_mine, _ = lax.optimization_barrier((even_mine, quant))
                even_other = lax.ppermute(even_mine, "section", [(i, i + 1) for i in range(0, sections, 2)])
                sources = (own, by1, even_mine, even_other, even_mine, even_other)
            if stage == 0 and layer == 1:
                odd_mine, _ = lax.optimization_barrier((odd_mine, quant))
                odd_other = lax.ppermute(odd_mine, "section", [(i + 1, i) for i in range(0, sections, 2)])
                sources = (own, by1, even_mine, even_other, odd_mine, odd_other)
            quant_rows = exchange(quant, "tp")
            if stage == 0 and layer < 2:
                copies, stream = project_from(layer, where, sources, quant_rows, stream)
            else:
                copies, stream = project(quant_rows, weights[layer % 2][layer // 2], stream)
        if stage < stages - 1:
            stream = lax.ppermute(
                stream, "section", [(i, i + STAGE) for i in range(sections - STAGE)]
            )
            copies = spread(stream, tensor)
    kept_normed, kept_rotated = kept

    lanes = all_rows
    turned = lax.optimization_barrier(kept_normed.T)
    turned = turned.reshape(sections, replicas, row_block, lanes).transpose(1, 0, 2, 3)
    turned = turned.reshape(replicas, sections * row_block, lanes)
    level, slope = level_and_slope(kept_rotated, row_scales)
    error_part = level - kept_rotated
    grad_rot = (error_part * (slope - 1.0)).astype(jnp.bfloat16)
    grad_rot = grad_rot.reshape(all_rows, part_cols // lanes, lanes).transpose(1, 0, 2)
    sent = jnp.concatenate([turned, copies_of(grad_rot.reshape(-1, lanes), replicas)], axis=1)

    def block(step):
        return lax.dynamic_index_in_dim(sent, partners[step], 0, keepdims=False)

    parts = jnp.stack(
        [block(0)]
        + [
            lax.ppermute(block(k), "dp", [(i, (i + k) % replicas) for i in range(replicas)])
            for k in range(1, replicas)
        ]
    )
    mine, other = terms_of(which, parts, planes, row_block, part_cols)
    loss = jnp.full((8, 128), jnp.sum(error_part * error_part), jnp.float32)
    losses = exchange(copies_of(loss, replicas * tensor), ("dp", "tp"))
    losses, _ = lax.optimization_barrier((losses, other))
    loss = jnp.sum(losses, axis=0)
    loss = loss + crossed(loss, 1)
    high = lax.reduce_precision(loss, 8, 7)
    middle = lax.reduce_precision(loss - high, 8, 7)
    low = loss - high - middle
    lane = lax.broadcasted_iota(jnp.int32, loss.shape, 1)
    tail_rows = jnp.where(lane == 0, high, jnp.where(lane == 1, middle, jnp.where(lane == 2, low, 0.0)))
    tail_rows = jnp.tile(tail_rows.astype(jnp.bfloat16), (1, part_cols // lanes))

    pair_sum = (mine + crossed(other, 1).astype(jnp.float32)).astype(jnp.bfloat16)
    sent = jnp.concatenate([pair_sum, copies_of(tail_rows, planes)], axis=1)
    parts = lax.all_to_all(sent, "section", 0, 0, axis_index_groups=same_core, tiled=True)
    sums = jnp.sum(parts.astype(jnp.float32), axis=0)
    factor = 1.0 / math.sqrt(sections * all_rows * replicas)
    norm_count = all_rows * replicas * D
    return (sums[:row_block] * factor, jnp.sum(sums[row_block, :3]) / norm_count)


def solution(mesh):
    placed = (
        P(None, "dp", "tp"),
        P(("section", "dp"), "tp"),
        P("section", None, "tp"),
        P("section", None),
        P("section", "tp"),
    )
    return jax.shard_map(
        local,
        mesh=mesh,
        in_specs=placed,
        out_specs=(P(("section", "dp"), "tp"), P()),
        check_vma=False,
    )
```

```python
import functools
import math

import jax
import jax.numpy as jnp
from jax import lax
from jax.experimental import pallas as pl
from jax.experimental.pallas import tpu as pltpu
from jax.sharding import PartitionSpec as P

D = 4096
GROUP = 128
STAGE = 4

norm_eps = 1e-05
full_turn = 2.0 * math.pi

SIN_TERMS = (3.141592653536291, -5.167712764624543, 2.5501633189471025,
             -0.5992521978250058, 0.08205040181365181, -0.007028386419353805)
COS_TERMS = (0.9999999997799043, -4.934802137078827, 4.058709159556301,
             -1.3352120030506605, 0.23493731381815505, -0.024396324355626643)


def horner(terms, square):
    total = jnp.full_like(square, terms[-1])
    for term in terms[-2::-1]:
        total = total * square + term
    return total


def half_turn(ratio):
    part = ratio - jnp.round(ratio)
    square = part * part
    return part * horner(SIN_TERMS, square), horner(COS_TERMS, square)


def quantize(values, scale):
    ratio = values / scale
    sine, cosine = half_turn(ratio)
    return scale * jnp.clip(ratio - sine * cosine / math.pi, -8.0, 7.0)


def level_and_slope(values, scale):
    ratio = values / scale
    sine, cosine = half_turn(ratio)
    stair = ratio - sine * cosine / math.pi
    inside = (stair > -8.0) & (stair < 7.0)
    level = scale * jnp.clip(stair, -8.0, 7.0)
    return level, jnp.where(inside, 2.0 * sine * sine, 0.0)


def copies_of(value, count):
    return jnp.broadcast_to(value[None], (count,) + value.shape)


def exchange(copies, axis):
    return lax.all_to_all(copies, axis, 0, 0, tiled=True)


def gather(value, axis):
    return exchange(copies_of(value, lax.axis_size(axis)), axis)


def crossed(value, mask):
    return lax.ppermute(value, "section", [(i, i ^ mask) for i in range(lax.axis_size("section"))])


def doubled(value):
    count, position = lax.axis_size("tp"), lax.axis_index("tp")
    value, mask = value[None], 1
    while mask < count:
        other = lax.ppermute(value, "tp", [(i, i ^ mask) for i in range(count)])
        upper = position & mask != 0
        value = jnp.concatenate([jnp.where(upper, other, value), jnp.where(upper, value, other)], axis=0)
        mask *= 2
    return value


VMEM = pl.BlockSpec(memory_space=pltpu.VMEM)
SMEM = pl.BlockSpec(memory_space=pltpu.SMEM)
FAR = pl.BlockSpec(memory_space=pl.ANY)
PARAMS = pltpu.CompilerParams(vmem_limit_bytes=8 * 1024 * 1024)


def start_load(layer, place_ref, refs, into, sems):
    chunks = sems.shape[0]
    chunk = into.shape[0] // chunks
    plane, core = place_ref[0] // 2, place_ref[0] % 2
    own, by1, even_mine, even_other, odd_mine, odd_other = refs
    mine, other = (odd_mine, odd_other) if layer % 2 else (even_mine, even_other)
    here, same = plane == layer // 2, core == layer % 2
    away, differs = jnp.logical_not(here), jnp.logical_not(same)
    for wanted, source in (
        (here & same, own), (here & differs, by1), (away & same, mine), (away & differs, other)
    ):
        @pl.when(wanted)
        def _():
            for index in range(chunks):
                rows = pl.ds(index * chunk, chunk)
                pltpu.make_async_copy(source.at[rows], into.at[rows], sems.at[index]).start()


def project_from_kernel(layer, place_ref, *args):
    refs, (quant_ref, stream_ref, copies_ref, out_ref, weight_ref, sems) = args[:6], args[6:]
    start_load(layer, place_ref, refs, weight_ref, sems)
    count, tok_rows, part = quant_ref.shape
    total = stream_ref[...].astype(jnp.float32)
    for k in range(count):
        rows = pl.ds(k * part, part)
        pltpu.make_async_copy(refs[0].at[rows], weight_ref.at[rows], sems.at[k]).wait()
        total = total + jnp.dot(quant_ref[k], weight_ref[rows], preferred_element_type=jnp.float32)
    stream = total.astype(jnp.bfloat16)
    out_ref[...] = stream
    for k in range(count):
        copies_ref[k] = stream


def project_from(layer, place, sources, quant_rows, stream):
    own = sources[0]
    return pl.pallas_call(
        functools.partial(project_from_kernel, layer),
        out_shape=[
            jax.ShapeDtypeStruct(quant_rows.shape, jnp.bfloat16),
            jax.ShapeDtypeStruct(stream.shape, jnp.bfloat16),
        ],
        in_specs=[SMEM] + [FAR] * 6 + [VMEM] * 2,
        out_specs=[VMEM] * 2,
        scratch_shapes=[
            pltpu.VMEM(own.shape, own.dtype),
            pltpu.SemaphoreType.DMA((quant_rows.shape[0],)),
        ],
        compiler_params=PARAMS,
        name="project_from",
    )(place, *sources, quant_rows, stream)


def project_kernel(quant_ref, weight_ref, stream_ref, copies_ref, out_ref):
    count, tok_rows, part = quant_ref.shape
    total = stream_ref[...].astype(jnp.float32)
    for k in range(count):
        rows = pl.ds(k * part, part)
        total = total + jnp.dot(quant_ref[k], weight_ref[rows], preferred_element_type=jnp.float32)
    stream = total.astype(jnp.bfloat16)
    out_ref[...] = stream
    for k in range(count):
        copies_ref[k] = stream


def project(quant_rows, weight, stream):
    return pl.pallas_call(
        project_kernel,
        out_shape=[
            jax.ShapeDtypeStruct(quant_rows.shape, jnp.bfloat16),
            jax.ShapeDtypeStruct(stream.shape, jnp.bfloat16),
        ],
        in_specs=[VMEM] * 3,
        out_specs=[VMEM] * 2,
        compiler_params=PARAMS,
        name="project",
    )(quant_rows, weight, stream)


def rotate_kernel(layer, last, keep_ref, rows_ref, gain_ref, rot_ref, scale_ref, _, __, *rest):
    (kept_normed, kept_rotated), rest = rest[:2], rest[2:]
    copies, (normed_ref, rotated_ref, sems) = rest[:-3], rest[-3:]
    count, tok_rows, part = rows_ref.shape
    place = pl.ds(layer * tok_rows, tok_rows)
    keep = keep_ref[0] == 1
    keep_normed = pltpu.make_async_copy(normed_ref, kept_normed.at[place], sems.at[0])
    keep_rotated = pltpu.make_async_copy(rotated_ref, kept_rotated.at[place], sems.at[1])
    total = None
    for k in range(count):
        rows = rows_ref[k].astype(jnp.float32)
        square = jnp.sum(rows * rows, axis=-1, keepdims=True)
        total = square if total is None else total + square
    factor = lax.rsqrt(total / (count * part) + norm_eps)
    for k in range(count):
        cols = slice(k * part, (k + 1) * part)
        rows = rows_ref[k].astype(jnp.float32)
        normed_ref[:, cols] = (rows * factor * gain_ref[:, cols]).astype(jnp.bfloat16)
    pl.when(keep)(keep_normed.start)
    rotated = jnp.dot(normed_ref[...], rot_ref[...], preferred_element_type=jnp.float32)
    rotated_ref[...] = rotated
    pl.when(keep)(keep_rotated.start)
    if not last:
        quantized = quantize(rotated, scale_ref[...]).astype(jnp.bfloat16)
        for k in range(count):
            copies[0][k] = quantized

    @pl.when(keep)
    def _():
        keep_normed.wait()
        keep_rotated.wait()


def rotate(layer, last, keep, rows, gain, rot_cols, scale, kept):
    count, tok_rows, part = rows.shape
    shapes = [jax.ShapeDtypeStruct(k.shape, k.dtype) for k in kept]
    if not last:
        shapes.append(jax.ShapeDtypeStruct(rows.shape, jnp.bfloat16))
    return pl.pallas_call(
        functools.partial(rotate_kernel, layer, last),
        out_shape=shapes,
        in_specs=[SMEM] + [VMEM] * 4 + [FAR] * 2,
        out_specs=[FAR] * 2 + [VMEM] * (len(shapes) - 2),
        input_output_aliases={5: 0, 6: 1},
        scratch_shapes=[
            pltpu.VMEM((tok_rows, count * part), jnp.bfloat16),
            pltpu.VMEM((tok_rows, part), jnp.float32),
            pltpu.SemaphoreType.DMA((2,)),
        ],
        compiler_params=PARAMS,
        name="rotate",
    )(keep, rows, gain, rot_cols, scale, *kept)


def spread_kernel(stream_ref, copies_ref):
    for k in range(copies_ref.shape[0]):
        copies_ref[k] = stream_ref[...]


def spread(stream, count):
    return pl.pallas_call(
        spread_kernel,
        out_shape=jax.ShapeDtypeStruct((count,) + stream.shape, stream.dtype),
        in_specs=[VMEM],
        out_specs=VMEM,
        compiler_params=PARAMS,
        name="spread",
    )(stream)


def terms_kernel(part_rows, core_ref, parts_ref, mine_ref, other_ref):
    sources, rows, lanes = parts_ref.shape
    count, _, cols = mine_ref.shape
    features = 2 * count * part_rows
    left = jnp.concatenate([parts_ref[s, :features] for s in range(sources)], axis=1)
    right = jnp.concatenate(
        [
            jnp.concatenate([parts_ref[s, pl.ds(k, lanes)] for k in range(features, rows, lanes)], axis=1)
            for s in range(sources)
        ],
        axis=0,
    )
    terms = jnp.dot(left, right, preferred_element_type=jnp.float32)
    lower = core_ref[0] == 0
    for z in range(count):
        even = terms[2 * z * part_rows : (2 * z + 1) * part_rows]
        odd = terms[(2 * z + 1) * part_rows : (2 * z + 2) * part_rows]
        mine_ref[z] = jnp.where(lower, even, odd)
        other_ref[z] = jnp.where(lower, odd, even).astype(jnp.bfloat16)


def terms_of(core, parts, planes, row_block, part_cols):
    shape = (planes, row_block, part_cols)
    return pl.pallas_call(
        functools.partial(terms_kernel, row_block),
        out_shape=[jax.ShapeDtypeStruct(shape, jnp.float32), jax.ShapeDtypeStruct(shape, jnp.bfloat16)],
        in_specs=[pl.BlockSpec(memory_space=pltpu.SMEM), VMEM],
        out_specs=[VMEM, VMEM],
        compiler_params=pltpu.CompilerParams(vmem_limit_bytes=24 * 1024 * 1024),
        name="terms",
    )(core, parts)


def local(hidden_in, rotation, proj, norm_gain, quant_exp):
    sections = lax.axis_size("section")
    replicas = lax.axis_size("dp")
    tensor = lax.axis_size("tp")
    section_pos = lax.axis_index("section")
    micro_count, tok_rows, part_cols = hidden_in.shape
    stages = sections // STAGE
    planes = sections // 2
    stage_pos = section_pos // STAGE
    place = section_pos % STAGE
    core = section_pos % 2
    same_core = [[2 * z + c for z in range(planes)] for c in range(2)]
    row_block = rotation.shape[0]

    own = proj[0]
    by1 = crossed(own, 1)

    scale_row = jnp.repeat(jnp.exp2(quant_exp.astype(jnp.float32) * 0.25) * 0.125, GROUP, axis=1)
    params = jnp.concatenate([norm_gain, scale_row], axis=1)
    params_by1 = crossed(params, 1)
    params_by2 = crossed(params, 2)
    along_z = lax.all_to_all(
        copies_of(rotation, planes), "section", 0, 0, axis_index_groups=same_core, tiled=True
    )
    params_by3 = crossed(params_by2, 1)
    along_z, by1, params_by2, params_by3 = lax.optimization_barrier((along_z, by1, params_by2, params_by3))
    own_now, _ = lax.optimization_barrier((own, params_by1))
    even_mine = lax.ppermute(own_now, "section", [(i, i ^ 2) for i in range(0, sections, 2)])
    found = jnp.concatenate([params, params_by1, params_by2, params_by3], axis=0)
    params = jnp.stack([lax.dynamic_index_in_dim(found, place ^ k, 0, False) for k in range(STAGE)])
    gains, scales = params[:, :D], params[:, D:]

    along_x = gather(along_z, "dp")
    stream = lax.dynamic_index_in_dim(hidden_in, place, 0, keepdims=False)
    stream, _ = lax.optimization_barrier((stream, along_z))
    first_rows = doubled(stream)
    along_x, gains, scales, stream, first_rows = lax.optimization_barrier(
        (along_x, gains, scales, stream, first_rows)
    )
    other_rows = crossed(along_x, 1)
    own_later, _ = lax.optimization_barrier((own, other_rows))
    odd_mine = lax.ppermute(own_later, "section", [(i, i ^ 2) for i in range(1, sections, 2)])
    even_rows = jnp.where(core == 0, along_x, other_rows)
    odd_rows = jnp.where(core == 0, other_rows, along_x)
    rot_cols = jnp.stack([even_rows, odd_rows]).transpose(2, 0, 1, 3, 4).reshape(D, part_cols)

    where = place[None].astype(jnp.int32)
    all_rows = STAGE * tok_rows
    kept = (jnp.zeros((all_rows, D), jnp.bfloat16), jnp.zeros((all_rows, part_cols), jnp.float32))
    weights = []
    keeps = [jnp.full((1,), 1, jnp.int32)]
    keeps += [(stage_pos == stage).astype(jnp.int32)[None] for stage in range(1, stages)]
    row_scales = jnp.repeat(scales, tok_rows, axis=0)
    dp_pos = lax.axis_index("dp").astype(jnp.uint32)
    partners = [lax.rem(dp_pos + jnp.uint32(step), jnp.uint32(replicas)) for step in range(replicas)]
    which = core[None].astype(jnp.int32)
    ahead = (keeps, row_scales, partners, which)
    for stage in range(stages):
        keep = keeps[stage]
        for layer in range(STAGE):
            last = stage == stages - 1 and layer == STAGE - 1
            gain, scale = gains[layer : layer + 1], scales[layer : layer + 1]
            rows = exchange(copies, "tp") if stage or layer else first_rows
            if stage == 0 and layer in (1, 2):
                odd = layer - 1
                mine, other = sources[4:] if odd else sources[2:4]
                far = jnp.where(core == odd, mine, other)
                near = jnp.where(core == odd, own, by1)
                pair = jnp.where(place // 2 == 0, near, far), jnp.where(place // 2 == 0, far, near)
                rows, pair, ahead = lax.optimization_barrier((rows, pair, ahead))
                weights.append(pair)
                keeps, row_scales, partners, which = ahead
            results = rotate(layer, last, keep, rows, gain, rot_cols, scale, kept)
            kept = results[:2]
            if last:
                break
            quant = results[2]
            if stage == 0 and layer == 0:
                even_mine, _ = lax.optimization_barrier((even_mine, quant))
                even_other = lax.ppermute(even_mine, "section", [(i, i + 1) for i in range(0, sections, 2)])
                sources = (own, by1, even_mine, even_other, even_mine, even_other)
            if stage == 0 and layer == 1:
                odd_mine, _ = lax.optimization_barrier((odd_mine, quant))
                odd_other = lax.ppermute(odd_mine, "section", [(i + 1, i) for i in range(0, sections, 2)])
                sources = (own, by1, even_mine, even_other, odd_mine, odd_other)
            quant_rows = exchange(quant, "tp")
            if stage == 0 and layer < 2:
                copies, stream = project_from(layer, where, sources, quant_rows, stream)
            else:
                copies, stream = project(quant_rows, weights[layer % 2][layer // 2], stream)
        if stage < stages - 1:
            stream = lax.ppermute(
                stream, "section", [(i, i + STAGE) for i in range(sections - STAGE)]
            )
            copies = spread(stream, tensor)
    kept_normed, kept_rotated = kept

    lanes = all_rows
    turned = lax.optimization_barrier(kept_normed.T)
    turned = turned.reshape(sections, replicas, row_block, lanes).transpose(1, 0, 2, 3)
    turned = turned.reshape(replicas, sections * row_block, lanes)
    level, slope = level_and_slope(kept_rotated, row_scales)
    error_part = level - kept_rotated
    grad_rot = (error_part * (slope - 1.0)).astype(jnp.bfloat16)
    grad_rot = grad_rot.reshape(all_rows, part_cols // lanes, lanes).transpose(1, 0, 2)
    sent = jnp.concatenate([turned, copies_of(grad_rot.reshape(-1, lanes), replicas)], axis=1)

    def block(step):
        return lax.dynamic_index_in_dim(sent, partners[step], 0, keepdims=False)

    parts = jnp.stack(
        [block(0)]
        + [
            lax.ppermute(block(k), "dp", [(i, (i + k) % replicas) for i in range(replicas)])
            for k in range(1, replicas)
        ]
    )
    mine, other = terms_of(which, parts, planes, row_block, part_cols)
    loss = jnp.full((8, 128), jnp.sum(error_part * error_part), jnp.float32)
    losses = exchange(copies_of(loss, replicas * tensor), ("dp", "tp"))
    losses, _ = lax.optimization_barrier((losses, other))
    loss = jnp.sum(losses, axis=0)
    loss = loss + crossed(loss, 1)
    high = lax.reduce_precision(loss, 8, 7)
    middle = lax.reduce_precision(loss - high, 8, 7)
    low = loss - high - middle
    lane = lax.broadcasted_iota(jnp.int32, loss.shape, 1)
    tail_rows = jnp.where(lane == 0, high, jnp.where(lane == 1, middle, jnp.where(lane == 2, low, 0.0)))
    tail_rows = jnp.tile(tail_rows.astype(jnp.bfloat16), (1, part_cols // lanes))

    pair_sum = (mine + crossed(other, 1).astype(jnp.float32)).astype(jnp.bfloat16)
    sent = jnp.concatenate([pair_sum, copies_of(tail_rows, planes)], axis=1)
    parts = lax.all_to_all(sent, "section", 0, 0, axis_index_groups=same_core, tiled=True)
    sums = jnp.sum(parts.astype(jnp.float32), axis=0)
    factor = 1.0 / math.sqrt(sections * all_rows * replicas)
    norm_count = all_rows * replicas * D
    return (sums[:row_block] * factor, jnp.sum(sums[row_block, :3]) / norm_count)


def solution(mesh):
    placed = (
        P(None, "dp", "tp"),
        P(("section", "dp"), "tp"),
        P("section", None, "tp"),
        P("section", None),
        P("section", "tp"),
    )
    return jax.shard_map(
        local,
        mesh=mesh,
        in_specs=placed,
        out_specs=(P(("section", "dp"), "tp"), P()),
        check_vma=False,
    )
```

```python
import functools
import math

import jax
import jax.numpy as jnp
from jax import lax
from jax.experimental import pallas as pl
from jax.experimental.pallas import tpu as pltpu
from jax.sharding import PartitionSpec as P

D = 4096
GROUP = 128
STAGE = 4

norm_eps = 1e-05
full_turn = 2.0 * math.pi

SIN_TERMS = (3.141592653536291, -5.167712764624543, 2.5501633189471025,
             -0.5992521978250058, 0.08205040181365181, -0.007028386419353805)
COS_TERMS = (0.9999999997799043, -4.934802137078827, 4.058709159556301,
             -1.3352120030506605, 0.23493731381815505, -0.024396324355626643)


def horner(terms, square):
    total = jnp.full_like(square, terms[-1])
    for term in terms[-2::-1]:
        total = total * square + term
    return total


def half_turn(ratio):
    part = ratio - jnp.round(ratio)
    square = part * part
    return part * horner(SIN_TERMS, square), horner(COS_TERMS, square)


def quantize(values, scale):
    ratio = values / scale
    sine, cosine = half_turn(ratio)
    return scale * jnp.clip(ratio - sine * cosine / math.pi, -8.0, 7.0)


def level_and_slope(values, scale):
    ratio = values / scale
    sine, cosine = half_turn(ratio)
    stair = ratio - sine * cosine / math.pi
    inside = (stair > -8.0) & (stair < 7.0)
    level = scale * jnp.clip(stair, -8.0, 7.0)
    return level, jnp.where(inside, 2.0 * sine * sine, 0.0)


def copies_of(value, count):
    return jnp.broadcast_to(value[None], (count,) + value.shape)


def exchange(copies, axis):
    return lax.all_to_all(copies, axis, 0, 0, tiled=True)


def gather(value, axis):
    return exchange(copies_of(value, lax.axis_size(axis)), axis)


def crossed(value, mask):
    return lax.ppermute(value, "section", [(i, i ^ mask) for i in range(lax.axis_size("section"))])


def doubled(value, after):
    count, position = lax.axis_size("tp"), lax.axis_index("tp")
    value, mask = value[None], 1
    while mask < count:
        other = lax.ppermute(value, "tp", [(i, i ^ mask) for i in range(count)])
        upper = position & mask != 0
        value = jnp.concatenate([jnp.where(upper, other, value), jnp.where(upper, value, other)], axis=0)
        if mask == 1:
            value, _ = lax.optimization_barrier((value, after))
        mask *= 2
    return value


VMEM = pl.BlockSpec(memory_space=pltpu.VMEM)
SMEM = pl.BlockSpec(memory_space=pltpu.SMEM)
FAR = pl.BlockSpec(memory_space=pl.ANY)
PARAMS = pltpu.CompilerParams(vmem_limit_bytes=8 * 1024 * 1024)


def start_load(layer, place_ref, refs, into, sems):
    chunks = sems.shape[0]
    chunk = into.shape[0] // chunks
    plane, core = place_ref[0] // 2, place_ref[0] % 2
    own, by1, even_mine, even_other, odd_mine, odd_other = refs
    mine, other = (odd_mine, odd_other) if layer % 2 else (even_mine, even_other)
    here, same = plane == layer // 2, core == layer % 2
    away, differs = jnp.logical_not(here), jnp.logical_not(same)
    for wanted, source in (
        (here & same, own), (here & differs, by1), (away & same, mine), (away & differs, other)
    ):
        @pl.when(wanted)
        def _():
            for index in range(chunks):
                rows = pl.ds(index * chunk, chunk)
                pltpu.make_async_copy(source.at[rows], into.at[rows], sems.at[index]).start()


def project_from_kernel(layer, place_ref, *args):
    refs, (quant_ref, stream_ref, copies_ref, out_ref, weight_ref, sems) = args[:6], args[6:]
    start_load(layer, place_ref, refs, weight_ref, sems)
    count, tok_rows, part = quant_ref.shape
    total = stream_ref[...].astype(jnp.float32)
    for k in range(count):
        rows = pl.ds(k * part, part)
        pltpu.make_async_copy(refs[0].at[rows], weight_ref.at[rows], sems.at[k]).wait()
        total = total + jnp.dot(quant_ref[k], weight_ref[rows], preferred_element_type=jnp.float32)
    stream = total.astype(jnp.bfloat16)
    out_ref[...] = stream
    for k in range(count):
        copies_ref[k] = stream


def project_from(layer, place, sources, quant_rows, stream):
    own = sources[0]
    return pl.pallas_call(
        functools.partial(project_from_kernel, layer),
        out_shape=[
            jax.ShapeDtypeStruct(quant_rows.shape, jnp.bfloat16),
            jax.ShapeDtypeStruct(stream.shape, jnp.bfloat16),
        ],
        in_specs=[SMEM] + [FAR] * 6 + [VMEM] * 2,
        out_specs=[VMEM] * 2,
        scratch_shapes=[
            pltpu.VMEM(own.shape, own.dtype),
            pltpu.SemaphoreType.DMA((quant_rows.shape[0],)),
        ],
        compiler_params=PARAMS,
        name="project_from",
    )(place, *sources, quant_rows, stream)


def project_kernel(quant_ref, weight_ref, stream_ref, copies_ref, out_ref):
    count, tok_rows, part = quant_ref.shape
    total = stream_ref[...].astype(jnp.float32)
    for k in range(count):
        rows = pl.ds(k * part, part)
        total = total + jnp.dot(quant_ref[k], weight_ref[rows], preferred_element_type=jnp.float32)
    stream = total.astype(jnp.bfloat16)
    out_ref[...] = stream
    for k in range(count):
        copies_ref[k] = stream


def project(quant_rows, weight, stream):
    return pl.pallas_call(
        project_kernel,
        out_shape=[
            jax.ShapeDtypeStruct(quant_rows.shape, jnp.bfloat16),
            jax.ShapeDtypeStruct(stream.shape, jnp.bfloat16),
        ],
        in_specs=[VMEM] * 3,
        out_specs=[VMEM] * 2,
        compiler_params=PARAMS,
        name="project",
    )(quant_rows, weight, stream)


def rotate_kernel(layer, last, keep_ref, rows_ref, gain_ref, rot_ref, scale_ref, _, __, *rest):
    (kept_normed, kept_rotated), rest = rest[:2], rest[2:]
    copies, (normed_ref, rotated_ref, sems) = rest[:-3], rest[-3:]
    count, tok_rows, part = rows_ref.shape
    place = pl.ds(layer * tok_rows, tok_rows)
    keep = keep_ref[0] == 1
    keep_normed = pltpu.make_async_copy(normed_ref, kept_normed.at[place], sems.at[0])
    keep_rotated = pltpu.make_async_copy(rotated_ref, kept_rotated.at[place], sems.at[1])
    total = None
    for k in range(count):
        rows = rows_ref[k].astype(jnp.float32)
        square = jnp.sum(rows * rows, axis=-1, keepdims=True)
        total = square if total is None else total + square
    factor = lax.rsqrt(total / (count * part) + norm_eps)
    for k in range(count):
        cols = slice(k * part, (k + 1) * part)
        rows = rows_ref[k].astype(jnp.float32)
        normed_ref[:, cols] = (rows * factor * gain_ref[:, cols]).astype(jnp.bfloat16)
    pl.when(keep)(keep_normed.start)
    rotated = jnp.dot(normed_ref[...], rot_ref[...], preferred_element_type=jnp.float32)
    rotated_ref[...] = rotated
    pl.when(keep)(keep_rotated.start)
    if not last:
        quantized = quantize(rotated, scale_ref[...]).astype(jnp.bfloat16)
        for k in range(count):
            copies[0][k] = quantized

    @pl.when(keep)
    def _():
        keep_normed.wait()
        keep_rotated.wait()


def rotate(layer, last, keep, rows, gain, rot_cols, scale, kept):
    count, tok_rows, part = rows.shape
    shapes = [jax.ShapeDtypeStruct(k.shape, k.dtype) for k in kept]
    if not last:
        shapes.append(jax.ShapeDtypeStruct(rows.shape, jnp.bfloat16))
    return pl.pallas_call(
        functools.partial(rotate_kernel, layer, last),
        out_shape=shapes,
        in_specs=[SMEM] + [VMEM] * 4 + [FAR] * 2,
        out_specs=[FAR] * 2 + [VMEM] * (len(shapes) - 2),
        input_output_aliases={5: 0, 6: 1},
        scratch_shapes=[
            pltpu.VMEM((tok_rows, count * part), jnp.bfloat16),
            pltpu.VMEM((tok_rows, part), jnp.float32),
            pltpu.SemaphoreType.DMA((2,)),
        ],
        compiler_params=PARAMS,
        name="rotate",
    )(keep, rows, gain, rot_cols, scale, *kept)


def spread_kernel(stream_ref, copies_ref):
    for k in range(copies_ref.shape[0]):
        copies_ref[k] = stream_ref[...]


def spread(stream, count):
    return pl.pallas_call(
        spread_kernel,
        out_shape=jax.ShapeDtypeStruct((count,) + stream.shape, stream.dtype),
        in_specs=[VMEM],
        out_specs=VMEM,
        compiler_params=PARAMS,
        name="spread",
    )(stream)


def terms_kernel(part_rows, core_ref, parts_ref, mine_ref, other_ref):
    sources, rows, lanes = parts_ref.shape
    count, _, cols = mine_ref.shape
    features = 2 * count * part_rows
    left = jnp.concatenate([parts_ref[s, :features] for s in range(sources)], axis=1)
    right = jnp.concatenate(
        [
            jnp.concatenate([parts_ref[s, pl.ds(k, lanes)] for k in range(features, rows, lanes)], axis=1)
            for s in range(sources)
        ],
        axis=0,
    )
    terms = jnp.dot(left, right, preferred_element_type=jnp.float32)
    lower = core_ref[0] == 0
    for z in range(count):
        even = terms[2 * z * part_rows : (2 * z + 1) * part_rows]
        odd = terms[(2 * z + 1) * part_rows : (2 * z + 2) * part_rows]
        mine_ref[z] = jnp.where(lower, even, odd)
        other_ref[z] = jnp.where(lower, odd, even).astype(jnp.bfloat16)


def terms_of(core, parts, planes, row_block, part_cols):
    shape = (planes, row_block, part_cols)
    return pl.pallas_call(
        functools.partial(terms_kernel, row_block),
        out_shape=[jax.ShapeDtypeStruct(shape, jnp.float32), jax.ShapeDtypeStruct(shape, jnp.bfloat16)],
        in_specs=[pl.BlockSpec(memory_space=pltpu.SMEM), VMEM],
        out_specs=[VMEM, VMEM],
        compiler_params=pltpu.CompilerParams(vmem_limit_bytes=24 * 1024 * 1024),
        name="terms",
    )(core, parts)


def local(hidden_in, rotation, proj, norm_gain, quant_exp):
    sections = lax.axis_size("section")
    replicas = lax.axis_size("dp")
    tensor = lax.axis_size("tp")
    section_pos = lax.axis_index("section")
    micro_count, tok_rows, part_cols = hidden_in.shape
    stages = sections // STAGE
    planes = sections // 2
    stage_pos = section_pos // STAGE
    place = section_pos % STAGE
    core = section_pos % 2
    same_core = [[2 * z + c for z in range(planes)] for c in range(2)]
    row_block = rotation.shape[0]

    own = proj[0]
    by1 = crossed(own, 1)

    scale_row = jnp.repeat(jnp.exp2(quant_exp.astype(jnp.float32) * 0.25) * 0.125, GROUP, axis=1)
    params = jnp.concatenate([norm_gain, scale_row], axis=1)
    params_by1 = crossed(params, 1)
    params_by2 = crossed(params, 2)
    along_z = lax.all_to_all(
        copies_of(rotation, planes), "section", 0, 0, axis_index_groups=same_core, tiled=True
    )
    params_by3 = crossed(params_by2, 1)
    along_z, by1, params_by2, params_by3 = lax.optimization_barrier((along_z, by1, params_by2, params_by3))
    own_now, _ = lax.optimization_barrier((own, params_by1))
    even_mine = lax.ppermute(own_now, "section", [(i, i ^ 2) for i in range(0, sections, 2)])
    found = jnp.concatenate([params, params_by1, params_by2, params_by3], axis=0)
    params = jnp.stack([lax.dynamic_index_in_dim(found, place ^ k, 0, False) for k in range(STAGE)])
    gains, scales = params[:, :D], params[:, D:]

    along_x = gather(along_z, "dp")
    stream = lax.dynamic_index_in_dim(hidden_in, place, 0, keepdims=False)
    stream, _ = lax.optimization_barrier((stream, params_by1))
    first_rows = doubled(stream, along_z)
    along_x, gains, scales, stream, first_rows = lax.optimization_barrier(
        (along_x, gains, scales, stream, first_rows)
    )
    other_rows = crossed(along_x, 1)
    own_later, _ = lax.optimization_barrier((own, other_rows))
    odd_mine = lax.ppermute(own_later, "section", [(i, i ^ 2) for i in range(1, sections, 2)])
    even_rows = jnp.where(core == 0, along_x, other_rows)
    odd_rows = jnp.where(core == 0, other_rows, along_x)
    rot_cols = jnp.stack([even_rows, odd_rows]).transpose(2, 0, 1, 3, 4).reshape(D, part_cols)

    where = place[None].astype(jnp.int32)
    all_rows = STAGE * tok_rows
    kept = (jnp.zeros((all_rows, D), jnp.bfloat16), jnp.zeros((all_rows, part_cols), jnp.float32))
    weights = []
    keeps = [jnp.full((1,), 1, jnp.int32)]
    keeps += [(stage_pos == stage).astype(jnp.int32)[None] for stage in range(1, stages)]
    row_scales = jnp.repeat(scales, tok_rows, axis=0)
    dp_pos = lax.axis_index("dp").astype(jnp.uint32)
    partners = [lax.rem(dp_pos + jnp.uint32(step), jnp.uint32(replicas)) for step in range(replicas)]
    which = core[None].astype(jnp.int32)
    ahead = (keeps, row_scales, partners, which)
    for stage in range(stages):
        keep = keeps[stage]
        for layer in range(STAGE):
            last = stage == stages - 1 and layer == STAGE - 1
            gain, scale = gains[layer : layer + 1], scales[layer : layer + 1]
            rows = exchange(copies, "tp") if stage or layer else first_rows
            if stage == 0 and layer in (1, 2):
                odd = layer - 1
                mine, other = sources[4:] if odd else sources[2:4]
                far = jnp.where(core == odd, mine, other)
                near = jnp.where(core == odd, own, by1)
                pair = jnp.where(place // 2 == 0, near, far), jnp.where(place // 2 == 0, far, near)
                rows, pair, ahead = lax.optimization_barrier((rows, pair, ahead))
                weights.append(pair)
                keeps, row_scales, partners, which = ahead
            results = rotate(layer, last, keep, rows, gain, rot_cols, scale, kept)
            kept = results[:2]
            if last:
                break
            quant = results[2]
            if stage == 0 and layer == 0:
                even_mine, _ = lax.optimization_barrier((even_mine, quant))
                even_other = lax.ppermute(even_mine, "section", [(i, i + 1) for i in range(0, sections, 2)])
                sources = (own, by1, even_mine, even_other, even_mine, even_other)
            if stage == 0 and layer == 1:
                odd_mine, _ = lax.optimization_barrier((odd_mine, quant))
                odd_other = lax.ppermute(odd_mine, "section", [(i + 1, i) for i in range(0, sections, 2)])
                sources = (own, by1, even_mine, even_other, odd_mine, odd_other)
            quant_rows = exchange(quant, "tp")
            if stage == 0 and layer < 2:
                copies, stream = project_from(layer, where, sources, quant_rows, stream)
            else:
                copies, stream = project(quant_rows, weights[layer % 2][layer // 2], stream)
        if stage < stages - 1:
            stream = lax.ppermute(
                stream, "section", [(i, i + STAGE) for i in range(sections - STAGE)]
            )
            copies = spread(stream, tensor)
    kept_normed, kept_rotated = kept

    lanes = all_rows
    turned = lax.optimization_barrier(kept_normed.T)
    turned = turned.reshape(sections, replicas, row_block, lanes).transpose(1, 0, 2, 3)
    turned = turned.reshape(replicas, sections * row_block, lanes)
    level, slope = level_and_slope(kept_rotated, row_scales)
    error_part = level - kept_rotated
    grad_rot = (error_part * (slope - 1.0)).astype(jnp.bfloat16)
    grad_rot = grad_rot.reshape(all_rows, part_cols // lanes, lanes).transpose(1, 0, 2)
    sent = jnp.concatenate([turned, copies_of(grad_rot.reshape(-1, lanes), replicas)], axis=1)

    def block(step):
        return lax.dynamic_index_in_dim(sent, partners[step], 0, keepdims=False)

    parts = jnp.stack(
        [block(0)]
        + [
            lax.ppermute(block(k), "dp", [(i, (i + k) % replicas) for i in range(replicas)])
            for k in range(1, replicas)
        ]
    )
    mine, other = terms_of(which, parts, planes, row_block, part_cols)
    loss = jnp.full((8, 128), jnp.sum(error_part * error_part), jnp.float32)
    losses = exchange(copies_of(loss, replicas * tensor), ("dp", "tp"))
    losses, _ = lax.optimization_barrier((losses, other))
    loss = jnp.sum(losses, axis=0)
    loss = loss + crossed(loss, 1)
    high = lax.reduce_precision(loss, 8, 7)
    middle = lax.reduce_precision(loss - high, 8, 7)
    low = loss - high - middle
    lane = lax.broadcasted_iota(jnp.int32, loss.shape, 1)
    tail_rows = jnp.where(lane == 0, high, jnp.where(lane == 1, middle, jnp.where(lane == 2, low, 0.0)))
    tail_rows = jnp.tile(tail_rows.astype(jnp.bfloat16), (1, part_cols // lanes))

    pair_sum = (mine + crossed(other, 1).astype(jnp.float32)).astype(jnp.bfloat16)
    sent = jnp.concatenate([pair_sum, copies_of(tail_rows, planes)], axis=1)
    parts = lax.all_to_all(sent, "section", 0, 0, axis_index_groups=same_core, tiled=True)
    sums = jnp.sum(parts.astype(jnp.float32), axis=0)
    factor = 1.0 / math.sqrt(sections * all_rows * replicas)
    norm_count = all_rows * replicas * D
    return (sums[:row_block] * factor, jnp.sum(sums[row_block, :3]) / norm_count)


def solution(mesh):
    placed = (
        P(None, "dp", "tp"),
        P(("section", "dp"), "tp"),
        P("section", None, "tp"),
        P("section", None),
        P("section", "tp"),
    )
    return jax.shard_map(
        local,
        mesh=mesh,
        in_specs=placed,
        out_specs=(P(("section", "dp"), "tp"), P()),
        check_vma=False,
    )
```
